512 devices in a mesh: dp: 8 (over y), expert: 64 (over x, z, core).
Axes of the slice: x: 4, y: 8, z: 8, core: 2. Of those that a mesh axis runs over, the one named last changes fastest.
Arguments:
- tokens: bfloat16 [8192, 2048], P(('dp', 'expert')), may hold values from -6 to 6
- cotangent: bfloat16 [8192, 2048], P(('dp', 'expert')), may hold values from -6 to 6
- gate_probs: float32 [8192, 8], P(('dp', 'expert')), may hold values from 0.15 to 0.35
- expert_ids: int32 [8192, 8], P(('dp', 'expert')), may hold values from 0 to 63, as said below
- up_weight: bfloat16 [64, 768, 2048], P('expert', 'dp'), may hold values from -0.125 to 0.125
- down_weight: bfloat16 [64, 768, 2048], P('expert', 'dp'), may hold values from -0.21875 to 0.21875
Outputs:
- mixture: bfloat16 [8192, 2048], P(('dp', 'expert'))
- input_grad: bfloat16 [8192, 2048], P(('dp', 'expert'))
- gate_grad: float32 [8192, 8], P(('dp', 'expert'))
The draws below stay inside these ranges and needn't reach their ends.
Inputs may be any that keep to these rules, and one draw needn't show every extreme that they name: `expert_ids`: the 8 experts of a row differ. The 16 rows of every device name one and the same expert exactly 9 times; they name every other expert at most 2 times, and one other expert exactly 2 times on every device.
All inputs are finite; a program needn't handle non-finite values.
Results may differ from the reference program's by a relative error of at most 0.0058.
Values may be sent and summed in bfloat16 or wider, within the bound.
No kernel may reach another device: no remote copies, remote signals or barrier semaphores. Data moves between devices by JAX's collectives and lax.ppermute only.
A program may use at most 64 MiB of HBM per device.

```python
import jax
import jax.numpy as jnp
from jax import lax

D = 2048
H = 768
TOP = 8
TOK_DEV = 16
EXPERTS = 64
TOKENS = 8192
HOTL = 9
CAP = 2
DEVICES = 512


def draw_expert_ids(key, part):
    key = jax.random.fold_in(key, 5)
    cold_total = EXPERTS - 1
    hottest = jax.random.randint(jax.random.fold_in(key, 1), (), 0, EXPERTS)
    filled = jax.random.randint(jax.random.fold_in(key, 2), (), 0, cold_total)
    blocks = TOKENS // TOK_DEV

    def one_block(block_index):
        block_key = jax.random.fold_in(key, block_index + 100)
        row_order = jax.random.permutation(jax.random.fold_in(block_key, 1), TOK_DEV)
        marked = jnp.zeros((TOK_DEV,), jnp.int32).at[row_order[:HOTL]].set(1)
        cold_count = TOP - marked
        offset = jnp.cumsum(cold_count) - cold_count
        column = jnp.arange(TOP, dtype=jnp.int32)
        position = offset[:, None] + column[None, :]
        mixing = jax.random.permutation(jax.random.fold_in(block_key, 2), cold_total)
        leading = mixing[0]
        mixing = jnp.where(mixing == filled, leading, mixing).at[0].set(filled)
        cold_index = mixing[position % cold_total]
        chosen = cold_index + (cold_index >= hottest).astype(jnp.int32)
        picked = jnp.where(column[None, :] < cold_count[:, None], chosen, hottest)
        rotation = jax.random.randint(jax.random.fold_in(block_key, 3), (TOK_DEV,), 0, TOP)
        return jnp.take_along_axis(picked, (column[None, :] + rotation[:, None]) % TOP, axis=1)
    return jax.vmap(one_block)(jnp.arange(blocks)).reshape(TOKENS, TOP).astype(jnp.int32)


def block_scale(rng, dims, split, smallest, high):
    level = 1.0
    for dim, shards_of in split:
        steps = jax.random.uniform(jax.random.fold_in(jax.random.fold_in(rng, 6), dim), (shards_of,), jnp.float32, smallest / len(split), high / len(split))
        level = level * jnp.repeat(jnp.exp(steps), dims[dim] // shards_of).reshape((-1,) + (1,) * (len(dims) - 1 - dim))
    return level


def gaussian(key, dims, deviation, reach, pieces=(), kind=jnp.bfloat16):
    level = block_scale(key, dims, pieces, -0.22, 0.18) if pieces else 1.0
    values = jax.random.normal(key, dims, jnp.float32) * deviation * level
    return jnp.minimum(jnp.maximum(values, -reach), reach).astype(kind)


def setup_inputs(seed: int = 0) -> dict:
    arg_keys = jax.random.split(jax.random.key(seed), 7)
    return {
        "tokens": gaussian(arg_keys[0], (TOKENS, D), 1.0, 6.0, ((0, 512),)),
        "cotangent": gaussian(arg_keys[1], (TOKENS, D), 1.0, 6.0, ((0, 512),)),
        "gate_probs": jnp.clip(0.15 + 0.19999999 * jax.random.uniform(arg_keys[2], (TOKENS, TOP), jnp.float32) ** block_scale(arg_keys[2], (TOKENS, TOP), ((0, 512),), -0.2, 0.2), 0.15, 0.35),
        "expert_ids": draw_expert_ids(jax.random.fold_in(arg_keys[6], 71), 0),
        "up_weight": gaussian(arg_keys[4], (EXPERTS, H, D), D ** -0.5, 0.125, ((0, 64), (1, 8))),
        "down_weight": gaussian(arg_keys[5], (EXPERTS, H, D), H ** -0.5, 0.21875, ((0, 64), (1, 8))),
    }


def expert_terms(features, row_grads, up_part, down_part):
    pre_act = jnp.dot(features, up_part.T, preferred_element_type=jnp.float32)
    gating = jax.nn.sigmoid(pre_act)
    hidden = (pre_act * gating).astype(jnp.bfloat16)
    output_rows = jnp.dot(hidden, down_part, preferred_element_type=jnp.float32)
    hidden_grad = jnp.dot(row_grads, down_part.T, preferred_element_type=jnp.float32)
    act_grad = (hidden_grad * gating * (1.0 + pre_act * (1.0 - gating))).astype(jnp.bfloat16)
    input_rows = jnp.dot(act_grad, up_part, preferred_element_type=jnp.float32)
    return output_rows.astype(jnp.bfloat16), input_rows.astype(jnp.bfloat16)


def reference(tokens, cotangent, gate_probs, expert_ids, up_weight, down_weight):
    flat_ids = expert_ids.reshape(-1).astype(jnp.int32)
    slots_all = flat_ids.shape[0]
    one_hot = (flat_ids[:, None] == jnp.arange(EXPERTS, dtype=jnp.int32)[None, :]).astype(jnp.int32)
    hottest = jnp.argmax(jnp.sum(one_hot, 0)).astype(jnp.int32)
    zero_row = jnp.zeros((1, D), tokens.dtype)
    padded_tokens = jnp.concatenate([tokens, zero_row], 0)
    padded_grads = jnp.concatenate([cotangent, zero_row], 0)
    padded_gates = jnp.concatenate([gate_probs.reshape(-1), jnp.zeros((1,), gate_probs.dtype)], 0)

    def visit(running, expert, row_limit, selected):
        slot_ids = jnp.nonzero(selected, size=row_limit, fill_value=slots_all)[0].astype(jnp.int32)
        row_ids = slot_ids // TOP
        features = padded_tokens[row_ids]
        row_grads = padded_grads[row_ids]
        output_rows, input_rows = expert_terms(features, row_grads, up_weight[expert], down_weight[expert])
        scale = padded_gates[slot_ids][:, None]
        mix_total, grad_total, gate_total = running
        mix_total = mix_total.at[row_ids].add(scale * output_rows.astype(jnp.float32), mode="drop")
        grad_total = grad_total.at[row_ids].add(scale * input_rows.astype(jnp.float32), mode="drop")
        products = jnp.sum(row_grads.astype(jnp.float32) * output_rows.astype(jnp.float32), 1)
        gate_total = gate_total.at[slot_ids].set(products, mode="drop")
        return (mix_total, grad_total, gate_total)

    def cold_step(running, expert):
        selected = jnp.logical_and(flat_ids == expert, expert != hottest)
        return visit(running, expert, CAP * DEVICES, selected), None

    initial = (jnp.zeros((TOKENS, D), jnp.float32), jnp.zeros((TOKENS, D), jnp.float32), jnp.zeros((slots_all,), jnp.float32))
    running, unused = lax.scan(cold_step, initial, jnp.arange(EXPERTS, dtype=jnp.int32))
    running = visit(running, hottest, HOTL * DEVICES, flat_ids == hottest)
    mix_total, grad_total, gate_total = running
    return mix_total.astype(jnp.bfloat16), grad_total.astype(jnp.bfloat16), gate_total.reshape(TOKENS, TOP)
```

```python
import functools

import jax
import jax.numpy as jnp
from jax import lax
from jax.experimental import pallas as pl
from jax.experimental.pallas import tpu as pltpu
from jax.sharding import PartitionSpec as P

BF16, F32, I32 = jnp.bfloat16, jnp.float32, jnp.int32
HOT_PAD = 16
VMEM_LIMIT = 40 * 1024 * 1024


def matmul(a, b):
    return lax.dot_general(a, b, (((1,), (0,)), ((), ())), preferred_element_type=F32)


def matmul_nt(a, b):
    return lax.dot_general(a, b, (((1,), (1,)), ((), ())), preferred_element_type=F32)


def matmul_tn(a, b):
    return lax.dot_general(a, b, (((0,), (0,)), ((), ())), preferred_element_type=F32)


def slot_maps(ids, slots, capacity):
    tok_rows, top_count = ids.shape
    slot = lax.broadcasted_iota(I32, (tok_rows, slots), 1)
    expert = slot // capacity
    named = jnp.zeros((tok_rows, slots), F32)
    for k in range(top_count):
        named = named + (ids[:, k : k + 1] == expert).astype(F32)
    counts = jnp.sum(named, 0, keepdims=True)
    is_hot = (counts == jnp.max(counts)).astype(F32)
    earlier = (
        lax.broadcasted_iota(I32, (tok_rows, tok_rows), 0)
        > lax.broadcasted_iota(I32, (tok_rows, tok_rows), 1)
    ).astype(BF16)
    rank = matmul(earlier, named.astype(BF16))
    cold = named * (1.0 - is_hot) * (rank == (slot % capacity).astype(F32)).astype(F32)
    first = (slot % capacity == 0).astype(F32)
    hot_token = jnp.sum(named * is_hot * first, 1, keepdims=True)
    hot_rank = jnp.sum(rank * is_hot * first, 1, keepdims=True)
    hot_row = lax.broadcasted_iota(I32, (tok_rows, HOT_PAD), 1).astype(F32)
    hot = hot_token * (hot_rank == hot_row).astype(F32)
    hottest = jnp.sum(is_hot * first[:1] * expert[:1].astype(F32), 1, keepdims=True)
    return cold, hot, expert, is_hot, hottest


def route_kernel(capacity, ids_ref, tok_ref, cot_ref, out_ref, hot_tok_ref, hot_cot_ref, hottest_ref):
    slots = out_ref.shape[0]
    width = tok_ref.shape[1]
    cold, hot, _, _, hottest = slot_maps(ids_ref[...], slots, capacity)
    cold, hot = cold.astype(BF16), hot.astype(BF16)
    tok, cot = tok_ref[...], cot_ref[...]
    out_ref[:, :width] = matmul_tn(cold, tok).astype(BF16)
    out_ref[:, width:] = matmul_tn(cold, cot).astype(BF16)
    hot_tok_ref[...] = matmul_tn(hot, tok).astype(BF16)
    hot_cot_ref[...] = matmul_tn(hot, cot).astype(BF16)
    hottest_ref[...] = jnp.broadcast_to(hottest, hottest_ref.shape).astype(I32)


def route(ids, tokens, cotangent, slots, capacity):
    width = tokens.shape[1]
    return pl.pallas_call(
        functools.partial(route_kernel, capacity),
        out_shape=(
            jax.ShapeDtypeStruct((slots, 2 * width), BF16),
            jax.ShapeDtypeStruct((HOT_PAD, width), BF16),
            jax.ShapeDtypeStruct((HOT_PAD, width), BF16),
            jax.ShapeDtypeStruct((8, 128), I32),
        ),
        compiler_params=pltpu.CompilerParams(vmem_limit_bytes=VMEM_LIMIT),
        name="route",
    )(ids, tokens, cotangent)


def activations(pre_act, hidden_grad):
    gating = jax.nn.sigmoid(pre_act)
    hidden = (pre_act * gating).astype(BF16)
    act_grad = (hidden_grad * gating * (1.0 + pre_act * (1.0 - gating))).astype(BF16)
    return hidden, act_grad


def gathered_kernel(units, rows_ref, *refs):
    pieces, acc_ref, up, down, sems = refs[:-4], refs[-4], refs[-3], refs[-2], refs[-1]
    width = up.shape[1]
    half = pieces[0].shape[0] // 2
    copies = []
    for i, piece in enumerate(pieces):
        for j, whole in enumerate((up, down)):
            copy = pltpu.make_async_copy(
                piece.at[pl.ds(j * half, units)], whole.at[pl.ds(i * units, units)], sems.at[i, j]
            )
            copy.start()
            copies.append(copy)
    for copy in copies:
        copy.wait()
    tok, cot = rows_ref[:, :width], rows_ref[:, width:]
    hidden, act_grad = activations(matmul_nt(tok, up[...]), matmul_nt(cot, down[...]))
    acc_ref[:, :width] = matmul(hidden, down[...])
    acc_ref[:, width:] = matmul(act_grad, up[...])


def gathered(rows, pieces, units):
    width = rows.shape[1] // 2
    count = len(pieces)
    return pl.pallas_call(
        functools.partial(gathered_kernel, units),
        out_shape=jax.ShapeDtypeStruct(rows.shape, F32),
        in_specs=[pl.BlockSpec(memory_space=pltpu.VMEM)] + [pl.BlockSpec(memory_space=pl.ANY)] * count,
        out_specs=pl.BlockSpec(memory_space=pltpu.VMEM),
        scratch_shapes=[
            pltpu.VMEM((count * units, width), BF16),
            pltpu.VMEM((count * units, width), BF16),
            pltpu.SemaphoreType.DMA((count, 2)),
        ],
        compiler_params=pltpu.CompilerParams(vmem_limit_bytes=VMEM_LIMIT),
        cost_estimate=pl.CostEstimate(
            flops=8 * rows.shape[0] * count * units * width,
            bytes_accessed=4 * count * units * width,
            transcendentals=0,
        ),
        name="gathered",
    )(rows, *pieces)


def last_kernel(units, rows_ref, acc_ref, up_ref, down_ref, out_ref):
    width = up_ref.shape[1]
    up, down = up_ref[:units, :], down_ref[:units, :]
    tok, cot = rows_ref[:, :width], rows_ref[:, width:]
    hidden, act_grad = activations(matmul_nt(tok, up), matmul_nt(cot, down))
    out_ref[:, :width] = (acc_ref[:, :width] + matmul(hidden, down)).astype(BF16)
    out_ref[:, width:] = (acc_ref[:, width:] + matmul(act_grad, up)).astype(BF16)


def last(rows, acc, up_half, down_half, units):
    return pl.pallas_call(
        functools.partial(last_kernel, units),
        out_shape=jax.ShapeDtypeStruct(rows.shape, BF16),
        compiler_params=pltpu.CompilerParams(vmem_limit_bytes=VMEM_LIMIT),
        name="last",
    )(rows, acc, up_half, down_half)


def hot_kernel(units, hot_rows, where_ref, weight_ref, *refs):
    blocks, out_ref, tok, cot, sems = refs[:-4], refs[-4], refs[-3], refs[-2], refs[-1]
    ring = len(blocks) // 2
    width = tok.shape[1]
    here = where_ref[0]
    copies = []
    for i in range(ring):
        place = pl.multiple_of(lax.rem(here + i, ring) * HOT_PAD, HOT_PAD)
        for j, whole in enumerate((tok, cot)):
            copy = pltpu.make_async_copy(
                blocks[2 * i + j], whole.at[pl.ds(place, HOT_PAD)], sems.at[i, j]
            )
            copy.start()
            copies.append(copy)
    for copy in copies:
        copy.wait()
    up, down = weight_ref[:units, :], weight_ref[units:, :]
    hidden, act_grad = activations(matmul_nt(tok[...], up), matmul_nt(cot[...], down))
    mixed = matmul(hidden, down).astype(BF16)
    grads = matmul(act_grad, up).astype(BF16)
    for i in range(ring):
        out_ref[i, :, :width] = mixed[i * HOT_PAD : i * HOT_PAD + hot_rows]
        out_ref[i, :, width:] = grads[i * HOT_PAD : i * HOT_PAD + hot_rows]


def hot_partials(here, weights, blocks, units, hot_rows):
    width = weights.shape[1]
    ring = len(blocks) // 2
    return pl.pallas_call(
        functools.partial(hot_kernel, units, hot_rows),
        out_shape=jax.ShapeDtypeStruct((ring, hot_rows, 2 * width), BF16),
        in_specs=[
            pl.BlockSpec(memory_space=pltpu.SMEM),
            pl.BlockSpec(memory_space=pltpu.VMEM),
        ]
        + [pl.BlockSpec(memory_space=pl.ANY)] * len(blocks),
        out_specs=pl.BlockSpec(memory_space=pltpu.VMEM),
        scratch_shapes=[
            pltpu.VMEM((ring * HOT_PAD, width), BF16),
            pltpu.VMEM((ring * HOT_PAD, width), BF16),
            pltpu.SemaphoreType.DMA((ring, 2)),
        ],
        compiler_params=pltpu.CompilerParams(vmem_limit_bytes=VMEM_LIMIT),
        name="hot",
    )(here, weights, *blocks)


def thirds(x):
    first = x.astype(BF16)
    rest = x - first.astype(F32)
    second = rest.astype(BF16)
    third = (rest - second.astype(F32)).astype(BF16)
    return jnp.concatenate([first, second, third], 0)


def combine_kernel(capacity, ids_ref, gate_ref, cot_ref, cold_ref, part_ref, mix_ref, grad_ref, gate_grad_ref):
    ids, gates, cot = ids_ref[...], gate_ref[...], cot_ref[...]
    tok_rows, top_count = ids.shape
    slots = cold_ref.shape[0]
    width = cot.shape[1]
    ring, hot_rows = part_ref.shape[0], part_ref.shape[1]
    cold, hot, expert, is_hot, _ = slot_maps(ids, slots, capacity)
    per_slot = jnp.zeros((tok_rows, slots), F32)
    for k in range(top_count):
        per_slot = per_slot + jnp.where(ids[:, k : k + 1] == expert, gates[:, k : k + 1], 0.0)
    hot_gate = jnp.max(per_slot * is_hot, 1, keepdims=True)
    cold_scale = thirds(jnp.where(cold > 0, per_slot, 0.0))
    hot_scale = thirds(jnp.where(hot > 0, hot_gate, 0.0))[:, :hot_rows]
    total = part_ref[0].astype(F32)
    for i in range(1, ring):
        total = total + part_ref[i].astype(F32)
    hot_result = total.astype(BF16)

    def weighted(lo):
        sums = matmul(cold_scale, cold_ref[:, lo : lo + width])
        sums = sums + matmul(hot_scale, hot_result[:, lo : lo + width])
        return sums[:tok_rows] + sums[tok_rows : 2 * tok_rows] + sums[2 * tok_rows :]

    mix_ref[...] = weighted(0).astype(BF16)
    grad_ref[...] = weighted(width).astype(BF16)
    cold_dots = jnp.where(cold > 0, matmul_nt(cot, cold_ref[:, :width]), 0.0)
    hot_dots = matmul_nt(cot, hot_result[:, :width])
    hot_dot = jnp.sum(jnp.where(hot[:, :hot_rows] > 0, hot_dots, 0.0), 1, keepdims=True)
    for k in range(top_count):
        mine = ids[:, k : k + 1] == expert
        cold_part = jnp.sum(jnp.where(mine, cold_dots, 0.0), 1, keepdims=True)
        named_hot = jnp.max(jnp.where(mine, is_hot, 0.0), 1, keepdims=True)
        gate_grad_ref[:, k : k + 1] = cold_part + named_hot * hot_dot


def combine(ids, gates, cotangent, cold_results, hot_parts, capacity):
    return pl.pallas_call(
        functools.partial(combine_kernel, capacity),
        out_shape=(
            jax.ShapeDtypeStruct(cotangent.shape, BF16),
            jax.ShapeDtypeStruct(cotangent.shape, BF16),
            jax.ShapeDtypeStruct(gates.shape, F32),
        ),
        compiler_params=pltpu.CompilerParams(vmem_limit_bytes=VMEM_LIMIT),
        name="combine",
    )(ids, gates, cotangent, cold_results, hot_parts)


def shift(x, by):
    ring = lax.axis_size("dp")
    return lax.ppermute(x, "dp", [(i, (i + by) % ring) for i in range(ring)])


def plane(experts):
    xs, zs, cores = 4, experts // 8, 2
    return xs, zs, cores


def spread_hot(weights, hottest):
    experts = lax.axis_size("expert")
    xs, zs, cores = plane(experts)
    me = lax.axis_index("expert")
    line = [[(x * zs + z) * cores + c for x in range(xs) for c in range(cores)] for z in range(zs)]
    parts = xs * cores
    rows, width = weights.shape
    chunks = lax.all_to_all(
        weights.reshape(parts, rows // parts, width), "expert", 0, 0, axis_index_groups=line, tiled=True
    )
    hot_x, hot_z, hot_c = hottest // (zs * cores), (hottest // cores) % zs, hottest % cores
    z = (me // cores) % zs
    chunk = lax.dynamic_index_in_dim(chunks, hot_x * cores + hot_c, 0, keepdims=False)
    chunk = jnp.where(z == hot_z, chunk, jnp.zeros_like(chunk))
    step = 1
    while step < zs:
        pairs = [(e, (e // (zs * cores)) * zs * cores + ((((e // cores) % zs) ^ step) * cores) + e % cores) for e in range(experts)]
        chunk = chunk + lax.ppermute(chunk, "expert", pairs)
        step *= 2
    return lax.all_gather(chunk, "expert", axis=0, axis_index_groups=line, tiled=True)


def shards(tokens, cotangent, gate_probs, expert_ids, up_weight, down_weight):
    tok_rows, width = tokens.shape
    top_count = expert_ids.shape[1]
    experts = lax.axis_size("expert")
    hot_rows = 9 * tok_rows // 16
    capacity = (tok_rows * top_count - hot_rows + experts - 2) // (experts - 1)
    slots = experts * capacity
    up, down = up_weight[0], down_weight[0]
    units = up.shape[0]

    outgoing, hot_tok, hot_cot, hottest = route(expert_ids, tokens, cotangent, slots, capacity)
    own = jnp.concatenate([up, hot_tok, down, hot_cot], 0)
    half = own.shape[0] // 2
    right, left = [own], [own]
    for _ in range(3):
        right.append(shift(right[-1], 1))
        left.append(shift(left[-1], -1))
    far_up, far_down = shift(right[-1][:half], 1), shift(left[-1][half:], -1)

    arrived = lax.all_to_all(
        outgoing.reshape(experts, capacity, 2 * width), "expert", 0, 0, tiled=True
    ).reshape(slots, 2 * width)
    hot_weights = spread_hot(jnp.concatenate([up, down], 0), hottest[0, 0])

    acc = gathered(arrived, [own] + right[1:] + left[1:], units)
    results = last(arrived, acc, far_up, far_down, units)
    came_back = lax.all_to_all(
        results.reshape(experts, capacity, 2 * width), "expert", 0, 0, tiled=True
    ).reshape(slots, 2 * width)

    def hot_of(block):
        return [block[units:half], block[half + units :]]

    blocks = [hot_tok, hot_cot]
    for block in left[1:]:
        blocks += hot_of(block)
    blocks += [far_up[units:], far_down[units:]]
    for block in right[:0:-1]:
        blocks += hot_of(block)
    here = lax.axis_index("dp").astype(I32).reshape(1)
    partials = hot_partials(here, hot_weights, blocks, units, hot_rows)
    hot_parts = lax.all_to_all(partials, "dp", 0, 0, tiled=True)
    return combine(expert_ids, gate_probs, cotangent, came_back, hot_parts, capacity)


def solution(mesh):
    rows = P(("dp", "expert"), None)
    weights = P("expert", "dp", None)
    return jax.shard_map(
        shards,
        mesh=mesh,
        in_specs=(rows, rows, rows, rows, weights, weights),
        out_specs=(rows, rows, rows),
        check_vma=False,
    )
```

```python
import functools

import jax
import jax.numpy as jnp
from jax import lax
from jax.experimental import pallas as pl
from jax.experimental.pallas import tpu as pltpu
from jax.sharding import PartitionSpec as P

BF16, F32, I32 = jnp.bfloat16, jnp.float32, jnp.int32
HOT_PAD = 16
VMEM_LIMIT = 16 * 1024 * 1024


def outside(x):
    return pltpu.with_memory_space_constraint(x, pltpu.HBM)


def matmul(a, b):
    return lax.dot_general(a, b, (((1,), (0,)), ((), ())), preferred_element_type=F32)


def matmul_nt(a, b):
    return lax.dot_general(a, b, (((1,), (1,)), ((), ())), preferred_element_type=F32)


def matmul_tn(a, b):
    return lax.dot_general(a, b, (((0,), (0,)), ((), ())), preferred_element_type=F32)


def slot_maps(ids, slots, capacity):
    top_count, tok_rows = ids.shape
    slot = lax.broadcasted_iota(I32, (slots, tok_rows), 0)
    expert = slot // capacity
    named = jnp.zeros((slots, tok_rows), F32)
    for k in range(top_count):
        named = named + (ids[k : k + 1, :] == expert).astype(F32)
    counts = jnp.sum(named, 1, keepdims=True)
    is_hot = (counts == jnp.max(counts)).astype(F32)
    earlier = (
        lax.broadcasted_iota(I32, (tok_rows, tok_rows), 0)
        < lax.broadcasted_iota(I32, (tok_rows, tok_rows), 1)
    ).astype(BF16)
    rank = matmul(named.astype(BF16), earlier)
    cold = named * (1.0 - is_hot) * (rank == (slot % capacity).astype(F32)).astype(F32)
    first = is_hot * (slot[:, :1] % capacity == 0).astype(F32)
    hot_token = jnp.sum(named * first, 0, keepdims=True)
    hot_rank = jnp.sum(rank * first, 0, keepdims=True)
    hot_row = lax.broadcasted_iota(I32, (HOT_PAD, tok_rows), 0).astype(F32)
    hot = hot_token * (hot_rank == hot_row).astype(F32)
    hottest = jnp.sum(first * expert[:, :1].astype(F32), 0, keepdims=True)
    return cold, hot, expert, is_hot, hottest


def route_kernel(
    capacity, ids_ref, tok_ref, cot_ref, up_ref, down_ref, out_ref, own_ref, pair_ref, hottest_ref,
    tok, cot, hot_tok, hot_cot, sems,
):
    slots, width = out_ref.shape[0], tok.shape[1]
    units = up_ref.shape[0]
    half = own_ref.shape[0] // 2
    loads = [pltpu.make_async_copy(tok_ref, tok, sems.at[0]), pltpu.make_async_copy(cot_ref, cot, sems.at[1])]
    copies = [
        pltpu.make_async_copy(up_ref, own_ref.at[pl.ds(0, units)], sems.at[2]),
        pltpu.make_async_copy(down_ref, own_ref.at[pl.ds(half, units)], sems.at[3]),
        pltpu.make_async_copy(up_ref, pair_ref.at[pl.ds(0, units)], sems.at[4]),
        pltpu.make_async_copy(down_ref, pair_ref.at[pl.ds(units, units)], sems.at[5]),
    ]
    for copy in loads + copies:
        copy.start()
    cold, hot, _, _, hottest = slot_maps(ids_ref[...], slots, capacity)
    cold, hot = cold.astype(BF16), hot.astype(BF16)
    hottest_ref[...] = jnp.broadcast_to(hottest, hottest_ref.shape).astype(I32)
    for copy in loads:
        copy.wait()
    hot_tok[...] = matmul(hot, tok[...]).astype(BF16)
    hot_cot[...] = matmul(hot, cot[...]).astype(BF16)
    stores = [
        pltpu.make_async_copy(hot_tok, own_ref.at[pl.ds(units, HOT_PAD)], sems.at[6]),
        pltpu.make_async_copy(hot_cot, own_ref.at[pl.ds(half + units, HOT_PAD)], sems.at[7]),
    ]
    for copy in stores:
        copy.start()
    out_ref[:, :width] = matmul(cold, tok[...]).astype(BF16)
    out_ref[:, width:] = matmul(cold, cot[...]).astype(BF16)
    for copy in copies + stores:
        copy.wait()


def route(ids, tokens, cotangent, up, down, slots, capacity):
    tok_rows, width = tokens.shape
    units = up.shape[0]
    anywhere = pl.BlockSpec(memory_space=pl.ANY)
    inside = pl.BlockSpec(memory_space=pltpu.VMEM)
    return pl.pallas_call(
        functools.partial(route_kernel, capacity),
        out_shape=(
            jax.ShapeDtypeStruct((slots, 2 * width), BF16),
            jax.ShapeDtypeStruct((2 * (units + HOT_PAD), width), BF16),
            jax.ShapeDtypeStruct((2 * units, width), BF16),
            jax.ShapeDtypeStruct((8, 128), I32),
        ),
        in_specs=[inside] + [anywhere] * 4,
        out_specs=(inside, anywhere, anywhere, inside),
        scratch_shapes=[
            pltpu.VMEM((tok_rows, width), BF16),
            pltpu.VMEM((tok_rows, width), BF16),
            pltpu.VMEM((HOT_PAD, width), BF16),
            pltpu.VMEM((HOT_PAD, width), BF16),
            pltpu.SemaphoreType.DMA((8,)),
        ],
        compiler_params=pltpu.CompilerParams(vmem_limit_bytes=VMEM_LIMIT),
        name="route",
    )(ids, *map(outside, (tokens, cotangent, up, down)))


def activations(pre_act, hidden_grad):
    gating = jax.nn.sigmoid(pre_act)
    hidden = (pre_act * gating).astype(BF16)
    act_grad = (hidden_grad * gating * (1.0 + pre_act * (1.0 - gating))).astype(BF16)
    return hidden, act_grad


def gathered_kernel(units, rows_ref, *refs):
    pieces, acc_ref, up, down, sems = refs[:-4], refs[-4], refs[-3], refs[-2], refs[-1]
    width = up.shape[1]
    half = pieces[0].shape[0] // 2
    copies = []
    for i, piece in enumerate(pieces):
        for j, whole in enumerate((up, down)):
            copy = pltpu.make_async_copy(
                piece.at[pl.ds(j * half, units)], whole.at[pl.ds(i * units, units)], sems.at[i, j]
            )
            copy.start()
            copies.append(copy)
    for copy in copies:
        copy.wait()
    tok, cot = rows_ref[:, :width], rows_ref[:, width:]
    hidden, act_grad = activations(matmul_nt(tok, up[...]), matmul_nt(cot, down[...]))
    acc_ref[:, :width] = matmul(hidden, down[...])
    acc_ref[:, width:] = matmul(act_grad, up[...])


def gathered(rows, pieces, units):
    width = rows.shape[1] // 2
    count = len(pieces)
    return pl.pallas_call(
        functools.partial(gathered_kernel, units),
        out_shape=jax.ShapeDtypeStruct(rows.shape, F32),
        in_specs=[pl.BlockSpec(memory_space=pltpu.VMEM)] + [pl.BlockSpec(memory_space=pl.ANY)] * count,
        out_specs=pl.BlockSpec(memory_space=pltpu.VMEM),
        scratch_shapes=[
            pltpu.VMEM((count * units, width), BF16),
            pltpu.VMEM((count * units, width), BF16),
            pltpu.SemaphoreType.DMA((count, 2)),
        ],
        compiler_params=pltpu.CompilerParams(vmem_limit_bytes=VMEM_LIMIT),
        cost_estimate=pl.CostEstimate(
            flops=8 * rows.shape[0] * count * units * width,
            bytes_accessed=4 * count * units * width,
            transcendentals=0,
        ),
        name="gathered",
    )(rows, *map(outside, pieces))


def last_kernel(units, rows_ref, acc_ref, up_ref, down_ref, out_ref):
    width = up_ref.shape[1]
    up, down = up_ref[:units, :], down_ref[:units, :]
    tok, cot = rows_ref[:, :width], rows_ref[:, width:]
    hidden, act_grad = activations(matmul_nt(tok, up), matmul_nt(cot, down))
    out_ref[:, :width] = (acc_ref[:, :width] + matmul(hidden, down)).astype(BF16)
    out_ref[:, width:] = (acc_ref[:, width:] + matmul(act_grad, up)).astype(BF16)


def last(rows, acc, up_half, down_half, units):
    return pl.pallas_call(
        functools.partial(last_kernel, units),
        out_shape=jax.ShapeDtypeStruct(rows.shape, BF16),
        compiler_params=pltpu.CompilerParams(vmem_limit_bytes=VMEM_LIMIT),
        name="last",
    )(rows, acc, up_half, down_half)


def hot_kernel(units, hot_rows, order, where_ref, weight_ref, *refs):
    blocks, out_ref, tok, cot, sems = refs[:-4], refs[-4], refs[-3], refs[-2], refs[-1]
    ring = len(blocks)
    width = tok.shape[1]
    here = where_ref[0]
    copies = []
    for i, block in enumerate(blocks):
        place = pl.multiple_of((here ^ lax.rem(here + i, ring)) * HOT_PAD, HOT_PAD)
        pair = block if isinstance(block, tuple) else (block, block)
        offset = 0 if isinstance(block, tuple) else units + HOT_PAD
        for j, whole in enumerate((tok, cot)):
            copy = pltpu.make_async_copy(
                pair[j].at[pl.ds(j * offset + units, HOT_PAD)], whole.at[pl.ds(place, HOT_PAD)], sems.at[i, j]
            )
            copy.start()
            copies.append(copy)
    for copy in copies:
        copy.wait()
    up, down = weight_ref[:units, :], weight_ref[units:, :]
    hidden, act_grad = activations(matmul_nt(tok[...], up), matmul_nt(cot[...], down))
    mixed = matmul(hidden, down).astype(BF16)
    grads = matmul(act_grad, up).astype(BF16)
    for i, place in enumerate(order):
        out_ref[i, :, :width] = mixed[place * HOT_PAD : place * HOT_PAD + hot_rows]
        out_ref[i, :, width:] = grads[place * HOT_PAD : place * HOT_PAD + hot_rows]


def hot_partials(here, weights, blocks, units, hot_rows, order):
    width = weights.shape[1]
    ring = len(blocks)
    flat, spans = [], []
    for block in blocks:
        spans.append(len(block) if isinstance(block, tuple) else 0)
        flat += list(block) if isinstance(block, tuple) else [block]

    def kernel(where_ref, weight_ref, *refs):
        refs, grouped = list(refs), []
        for span in spans:
            grouped.append(tuple(refs.pop(0) for _ in range(span)) if span else refs.pop(0))
        hot_kernel(units, hot_rows, order, where_ref, weight_ref, *grouped, *refs)

    return pl.pallas_call(
        kernel,
        out_shape=jax.ShapeDtypeStruct((ring, hot_rows, 2 * width), BF16),
        in_specs=[
            pl.BlockSpec(memory_space=pltpu.SMEM),
            pl.BlockSpec(memory_space=pltpu.VMEM),
        ]
        + [pl.BlockSpec(memory_space=pl.ANY)] * len(flat),
        out_specs=pl.BlockSpec(memory_space=pltpu.VMEM),
        scratch_shapes=[
            pltpu.VMEM((ring * HOT_PAD, width), BF16),
            pltpu.VMEM((ring * HOT_PAD, width), BF16),
            pltpu.SemaphoreType.DMA((ring, 2)),
        ],
        compiler_params=pltpu.CompilerParams(vmem_limit_bytes=VMEM_LIMIT),
        name="hot",
    )(here, weights, *map(outside, flat))


def thirds(x):
    first = x.astype(BF16)
    rest = x - first.astype(F32)
    second = rest.astype(BF16)
    third = (rest - second.astype(F32)).astype(BF16)
    return first, second, third


def combine_kernel(capacity, ids_ref, gate_ref, cot_ref, cold_ref, kept_ref, sent_ref, mix_ref, grad_ref, gate_grad_ref):
    ids, gates, cot = ids_ref[...], gate_ref[...], cot_ref[...]
    top_count, tok_rows = ids.shape
    slots = cold_ref.shape[0]
    width = cot.shape[1]
    hot_rows = kept_ref.shape[0]
    cold, hot, expert, is_hot, hottest = slot_maps(ids, slots, capacity)
    per_slot = jnp.zeros((slots, tok_rows), F32)
    hot_gate = jnp.zeros((1, tok_rows), F32)
    hottest = hottest.astype(I32)
    for k in range(top_count):
        per_slot = per_slot + jnp.where(ids[k : k + 1, :] == expert, gates[k : k + 1, :], 0.0)
        hot_gate = hot_gate + jnp.where(ids[k : k + 1, :] == hottest, gates[k : k + 1, :], 0.0)
    cold_scale = thirds(jnp.where(cold > 0, per_slot, 0.0))
    hot_scale = thirds(jnp.where(hot > 0, hot_gate, 0.0)[:hot_rows])
    hot_result = (kept_ref[...].astype(F32) + sent_ref[...].astype(F32)).astype(BF16)

    def weighted(lo):
        sums = jnp.zeros((tok_rows, width), F32)
        for part in cold_scale:
            sums = sums + matmul_tn(part, cold_ref[:, lo : lo + width])
        for part in hot_scale:
            sums = sums + matmul_tn(part, hot_result[:, lo : lo + width])
        return sums

    mix_ref[...] = weighted(0).astype(BF16)
    grad_ref[...] = weighted(width).astype(BF16)
    cold_dots = jnp.where(cold > 0, matmul_nt(cold_ref[:, :width], cot), 0.0)
    hot_dots = jnp.where(hot[:hot_rows] > 0, matmul_nt(hot_result[:, :width], cot), 0.0)
    hot_dot = jnp.sum(hot_dots, 0, keepdims=True)
    for k in range(top_count):
        mine = ids[k : k + 1, :]
        cold_part = jnp.sum(jnp.where(mine == expert, cold_dots, 0.0), 0, keepdims=True)
        gate_grad_ref[k : k + 1, :] = cold_part + jnp.where(mine == hottest, hot_dot, 0.0)


def combine(ids, gates, cotangent, cold_results, kept, sent, capacity):
    return pl.pallas_call(
        functools.partial(combine_kernel, capacity),
        out_shape=(
            jax.ShapeDtypeStruct(cotangent.shape, BF16),
            jax.ShapeDtypeStruct(cotangent.shape, BF16),
            jax.ShapeDtypeStruct(gates.shape, F32),
        ),
        compiler_params=pltpu.CompilerParams(vmem_limit_bytes=VMEM_LIMIT),
        name="combine",
    )(ids, gates, cotangent, cold_results, kept, sent)


def shift(x, by):
    ring = lax.axis_size("dp")
    return lax.ppermute(x, "dp", [(i, (i + by) % ring) for i in range(ring)])


def plane(experts):
    xs, zs, cores = 4, experts // 8, 2
    return xs, zs, cores


def swap(x, bit):
    ring = lax.axis_size("dp")
    return lax.ppermute(x, "dp", [(i, i ^ bit) for i in range(ring)])


def spread_hot(weights, hottest, after):
    experts = lax.axis_size("expert")
    xs, zs, cores = plane(experts)
    me = lax.axis_index("expert")
    line = [[(x * zs + z) * cores + c for x in range(xs) for c in range(cores)] for z in range(zs)]
    parts = xs * cores
    rows, width = weights.shape
    chunks = lax.all_to_all(
        weights.reshape(parts, rows // parts, width), "expert", 0, 0, axis_index_groups=line, tiled=True
    )
    hot_x, hot_z, hot_c = hottest // (zs * cores), (hottest // cores) % zs, hottest % cores
    z = (me // cores) % zs
    chunk = lax.dynamic_index_in_dim(chunks, hot_x * cores + hot_c, 0, keepdims=False)
    chunk = jnp.where(z == hot_z, chunk, jnp.zeros_like(chunk))
    step = 1
    while step < zs:
        pairs = [
            (e, (e // (zs * cores)) * zs * cores + ((((e // cores) % zs) ^ step) * cores) + e % cores)
            for e in range(experts)
        ]
        chunk = chunk + lax.ppermute(chunk, "expert", pairs)
        step *= 2
    chunk, after = lax.optimization_barrier((chunk, after))
    copies = jnp.broadcast_to(chunk[None], (parts,) + chunk.shape)
    whole = lax.all_to_all(copies, "expert", 0, 0, axis_index_groups=line, tiled=True)
    return whole.reshape(rows, width), after


def shards(tokens, cotangent, gate_probs, expert_ids, up_weight, down_weight):
    tok_rows, width = tokens.shape
    top_count = expert_ids.shape[1]
    experts = lax.axis_size("expert")
    hot_rows = 9 * tok_rows // 16
    capacity = (tok_rows * top_count - hot_rows + experts - 2) // (experts - 1)
    slots = experts * capacity
    up, down = up_weight[0], down_weight[0]
    units = up.shape[0]
    ids, gates = expert_ids.T, gate_probs.T

    outgoing, own, pair, hottest = route(ids, tokens, cotangent, up, down, slots, capacity)
    half = own.shape[0] // 2
    right, left = [own], [own]
    for _ in range(3):
        right.append(shift(right[-1], 1))
        left.append(shift(left[-1], -1))
    far_up, far_down = shift(right[-1][:half], 1), shift(left[-1][half:], -1)

    arrived = lax.all_to_all(
        outgoing.reshape(experts, capacity, 2 * width), "expert", 0, 0, tiled=True
    ).reshape(slots, 2 * width)
    hot_weights, arrived = spread_hot(pair, hottest[0, 0], arrived)

    acc = gathered(arrived, [own] + right[1:] + left[1:], units)
    results = last(arrived, acc, far_up, far_down, units)
    results, hot_weights = lax.optimization_barrier((results, hot_weights))
    came_back = lax.all_to_all(
        results.reshape(experts, capacity, 2 * width), "expert", 0, 0, tiled=True
    ).reshape(slots, 2 * width)

    blocks = left + [(far_up, far_down)] + right[:0:-1]
    here = lax.axis_index("dp").astype(I32).reshape(1)
    partials = hot_partials(here, hot_weights, blocks, units, hot_rows, (1, 3, 5, 7, 0, 4, 2, 6))

    def part(first, count):
        return partials[first : first + count].astype(F32)

    got = swap(partials[0:4], 1).astype(F32)
    onward = (part(6, 2) + got[1::2]).astype(BF16)
    stay = part(4, 2) + got[0::2]
    got = swap(onward, 2).astype(F32)
    stay = stay + got
    sent = swap(stay[1].astype(BF16), 4)
    mixture, input_grad, gate_grad = combine(ids, gates, cotangent, came_back, stay[0], sent, capacity)
    return mixture, input_grad, gate_grad.T


def solution(mesh):
    rows = P(("dp", "expert"), None)
    weights = P("expert", "dp", None)
    return jax.shard_map(
        shards,
        mesh=mesh,
        in_specs=(rows, rows, rows, rows, weights, weights),
        out_specs=(rows, rows, rows),
        check_vma=False,
    )
```

```python
import functools

import jax
import jax.numpy as jnp
from jax import lax
from jax.experimental import pallas as pl
from jax.experimental.pallas import tpu as pltpu
from jax.sharding import PartitionSpec as P

BF16, F32, I32 = jnp.bfloat16, jnp.float32, jnp.int32
HOT_PAD = 16
VMEM_LIMIT = 16 * 1024 * 1024


def outside(x):
    return pltpu.with_memory_space_constraint(x, pltpu.HBM)


def matmul(a, b):
    return lax.dot_general(a, b, (((1,), (0,)), ((), ())), preferred_element_type=F32)


def matmul_nt(a, b):
    return lax.dot_general(a, b, (((1,), (1,)), ((), ())), preferred_element_type=F32)


def matmul_tn(a, b):
    return lax.dot_general(a, b, (((0,), (0,)), ((), ())), preferred_element_type=F32)


def slot_maps(ids, slots, capacity):
    top_count, tok_rows = ids.shape
    slot = lax.broadcasted_iota(I32, (slots, tok_rows), 0)
    expert = slot // capacity
    named = jnp.zeros((slots, tok_rows), F32)
    for k in range(top_count):
        named = named + (ids[k : k + 1, :] == expert).astype(F32)
    counts = jnp.sum(named, 1, keepdims=True)
    is_hot = (counts == jnp.max(counts)).astype(F32)
    earlier = (
        lax.broadcasted_iota(I32, (tok_rows, tok_rows), 0)
        < lax.broadcasted_iota(I32, (tok_rows, tok_rows), 1)
    ).astype(BF16)
    rank = matmul(named.astype(BF16), earlier)
    cold = named * (1.0 - is_hot) * (rank == (slot % capacity).astype(F32)).astype(F32)
    first = is_hot * (slot[:, :1] % capacity == 0).astype(F32)
    hot_token = jnp.sum(named * first, 0, keepdims=True)
    hot_rank = jnp.sum(rank * first, 0, keepdims=True)
    hot_row = lax.broadcasted_iota(I32, (HOT_PAD, tok_rows), 0).astype(F32)
    hot = hot_token * (hot_rank == hot_row).astype(F32)
    hottest = jnp.sum(first * expert[:, :1].astype(F32), 0, keepdims=True)
    return cold, hot, expert, is_hot, hottest


def route_kernel(
    capacity, ids_ref, tok_ref, cot_ref, up_ref, down_ref, out_ref, own_ref, hottest_ref, tok, cot, sems
):
    slots, width = out_ref.shape[0], tok.shape[1]
    units = up_ref.shape[0]
    half = own_ref.shape[0] // 2
    loads = [pltpu.make_async_copy(tok_ref, tok, sems.at[0]), pltpu.make_async_copy(cot_ref, cot, sems.at[1])]
    copies = [
        pltpu.make_async_copy(up_ref, own_ref.at[pl.ds(0, units)], sems.at[2]),
        pltpu.make_async_copy(down_ref, own_ref.at[pl.ds(half, units)], sems.at[3]),
    ]
    for copy in loads + copies:
        copy.start()
    cold, hot, _, _, hottest = slot_maps(ids_ref[...], slots, capacity)
    cold, hot = cold.astype(BF16), hot.astype(BF16)
    hottest_ref[...] = jnp.broadcast_to(hottest, hottest_ref.shape).astype(I32)
    for copy in loads:
        copy.wait()
    own_ref[units:half, :] = matmul(hot, tok[...]).astype(BF16)
    own_ref[half + units :, :] = matmul(hot, cot[...]).astype(BF16)
    out_ref[:, :width] = matmul(cold, tok[...]).astype(BF16)
    out_ref[:, width:] = matmul(cold, cot[...]).astype(BF16)
    for copy in copies:
        copy.wait()


def route(ids, tokens, cotangent, up, down, slots, capacity):
    tok_rows, width = tokens.shape
    units = up.shape[0]
    anywhere = pl.BlockSpec(memory_space=pl.ANY)
    inside = pl.BlockSpec(memory_space=pltpu.VMEM)
    return pl.pallas_call(
        functools.partial(route_kernel, capacity),
        out_shape=(
            jax.ShapeDtypeStruct((slots, 2 * width), BF16),
            jax.ShapeDtypeStruct((2 * (units + HOT_PAD), width), BF16),
            jax.ShapeDtypeStruct((8, 128), I32),
        ),
        in_specs=[inside] + [anywhere] * 4,
        out_specs=(inside, inside, inside),
        scratch_shapes=[
            pltpu.VMEM((tok_rows, width), BF16),
            pltpu.VMEM((tok_rows, width), BF16),
            pltpu.SemaphoreType.DMA((4,)),
        ],
        compiler_params=pltpu.CompilerParams(vmem_limit_bytes=VMEM_LIMIT),
        name="route",
    )(ids, *map(outside, (tokens, cotangent, up, down)))


def activations(pre_act, hidden_grad):
    gating = jax.nn.sigmoid(pre_act)
    hidden = (pre_act * gating).astype(BF16)
    act_grad = (hidden_grad * gating * (1.0 + pre_act * (1.0 - gating))).astype(BF16)
    return hidden, act_grad


def gathered_kernel(units, rows_ref, *refs):
    pieces, acc_ref, up, down, sems = refs[:-4], refs[-4], refs[-3], refs[-2], refs[-1]
    width = up.shape[1]
    half = pieces[0].shape[0] // 2
    copies = []
    for i, piece in enumerate(pieces):
        for j, whole in enumerate((up, down)):
            copy = pltpu.make_async_copy(
                piece.at[pl.ds(j * half, units)], whole.at[pl.ds(i * units, units)], sems.at[i, j]
            )
            copy.start()
            copies.append(copy)
    for copy in copies:
        copy.wait()
    tok, cot = rows_ref[:, :width], rows_ref[:, width:]
    hidden, act_grad = activations(matmul_nt(tok, up[...]), matmul_nt(cot, down[...]))
    acc_ref[:, :width] = matmul(hidden, down[...])
    acc_ref[:, width:] = matmul(act_grad, up[...])


def gathered(rows, pieces, units):
    width = rows.shape[1] // 2
    count = len(pieces)
    return pl.pallas_call(
        functools.partial(gathered_kernel, units),
        out_shape=jax.ShapeDtypeStruct(rows.shape, F32),
        in_specs=[pl.BlockSpec(memory_space=pltpu.VMEM)] + [pl.BlockSpec(memory_space=pl.ANY)] * count,
        out_specs=pl.BlockSpec(memory_space=pltpu.VMEM),
        scratch_shapes=[
            pltpu.VMEM((count * units, width), BF16),
            pltpu.VMEM((count * units, width), BF16),
            pltpu.SemaphoreType.DMA((count, 2)),
        ],
        compiler_params=pltpu.CompilerParams(vmem_limit_bytes=VMEM_LIMIT),
        cost_estimate=pl.CostEstimate(
            flops=8 * rows.shape[0] * count * units * width,
            bytes_accessed=4 * count * units * width,
            transcendentals=0,
        ),
        name="gathered",
    )(rows, *map(outside, pieces))


def last_kernel(units, rows_ref, acc_ref, up_ref, down_ref, out_ref):
    width = up_ref.shape[1]
    up, down = up_ref[:units, :], down_ref[:units, :]
    tok, cot = rows_ref[:, :width], rows_ref[:, width:]
    hidden, act_grad = activations(matmul_nt(tok, up), matmul_nt(cot, down))
    out_ref[:, :width] = (acc_ref[:, :width] + matmul(hidden, down)).astype(BF16)
    out_ref[:, width:] = (acc_ref[:, width:] + matmul(act_grad, up)).astype(BF16)


def last(rows, acc, up_half, down_half, units):
    return pl.pallas_call(
        functools.partial(last_kernel, units),
        out_shape=jax.ShapeDtypeStruct(rows.shape, BF16),
        compiler_params=pltpu.CompilerParams(vmem_limit_bytes=VMEM_LIMIT),
        name="last",
    )(rows, acc, up_half, down_half)


def hot_kernel(units, hot_rows, order, where_ref, weight_ref, *refs):
    blocks, out_ref, tok, cot, sems = refs[:-4], refs[-4], refs[-3], refs[-2], refs[-1]
    ring = len(blocks)
    width = tok.shape[1]
    here = where_ref[0]
    copies = []
    for i, block in enumerate(blocks):
        place = pl.multiple_of((here ^ lax.rem(here + i, ring)) * HOT_PAD, HOT_PAD)
        pair = block if isinstance(block, tuple) else (block, block)
        offset = 0 if isinstance(block, tuple) else units + HOT_PAD
        for j, whole in enumerate((tok, cot)):
            copy = pltpu.make_async_copy(
                pair[j].at[pl.ds(j * offset + units, HOT_PAD)], whole.at[pl.ds(place, HOT_PAD)], sems.at[i, j]
            )
            copy.start()
            copies.append(copy)
    for copy in copies:
        copy.wait()
    up, down = weight_ref[:units, :], weight_ref[units:, :]
    hidden, act_grad = activations(matmul_nt(tok[...], up), matmul_nt(cot[...], down))
    mixed = matmul(hidden, down).astype(BF16)
    grads = matmul(act_grad, up).astype(BF16)
    for i, place in enumerate(order):
        out_ref[i, :, :width] = mixed[place * HOT_PAD : place * HOT_PAD + hot_rows]
        out_ref[i, :, width:] = grads[place * HOT_PAD : place * HOT_PAD + hot_rows]


def hot_partials(here, weights, blocks, units, hot_rows, order):
    width = weights.shape[1]
    ring = len(blocks)
    flat, spans = [], []
    for block in blocks:
        spans.append(len(block) if isinstance(block, tuple) else 0)
        flat += list(block) if isinstance(block, tuple) else [block]

    def kernel(where_ref, weight_ref, *refs):
        refs, grouped = list(refs), []
        for span in spans:
            grouped.append(tuple(refs.pop(0) for _ in range(span)) if span else refs.pop(0))
        hot_kernel(units, hot_rows, order, where_ref, weight_ref, *grouped, *refs)

    return pl.pallas_call(
        kernel,
        out_shape=jax.ShapeDtypeStruct((ring, hot_rows, 2 * width), BF16),
        in_specs=[
            pl.BlockSpec(memory_space=pltpu.SMEM),
            pl.BlockSpec(memory_space=pltpu.VMEM),
        ]
        + [pl.BlockSpec(memory_space=pl.ANY)] * len(flat),
        out_specs=pl.BlockSpec(memory_space=pltpu.VMEM),
        scratch_shapes=[
            pltpu.VMEM((ring * HOT_PAD, width), BF16),
            pltpu.VMEM((ring * HOT_PAD, width), BF16),
            pltpu.SemaphoreType.DMA((ring, 2)),
        ],
        compiler_params=pltpu.CompilerParams(vmem_limit_bytes=VMEM_LIMIT),
        name="hot",
    )(here, weights, *map(outside, flat))


def thirds(x):
    first = x.astype(BF16)
    rest = x - first.astype(F32)
    second = rest.astype(BF16)
    third = (rest - second.astype(F32)).astype(BF16)
    return first, second, third


def cold_kernel(capacity, ids_ref, gate_ref, cot_ref, cold_ref, sum_ref, dots_ref):
    ids, gates, cot = ids_ref[...], gate_ref[...], cot_ref[...]
    top_count = ids.shape[0]
    slots = cold_ref.shape[0]
    width = cot.shape[1]
    cold, _, expert, _, _ = slot_maps(ids, slots, capacity)
    per_slot = jnp.zeros(cold.shape, F32)
    for k in range(top_count):
        per_slot = per_slot + jnp.where(ids[k : k + 1, :] == expert, gates[k : k + 1, :], 0.0)
    scale = thirds(jnp.where(cold > 0, per_slot, 0.0))
    for lo in (0, width):
        rows = cold_ref[:, lo : lo + width]
        sum_ref[:, lo : lo + width] = matmul_tn(scale[0], rows) + matmul_tn(scale[1], rows) + matmul_tn(scale[2], rows)
    dots = jnp.where(cold > 0, matmul_nt(cold_ref[:, :width], cot), 0.0)
    for k in range(top_count):
        dots_ref[k : k + 1, :] = jnp.sum(jnp.where(ids[k : k + 1, :] == expert, dots, 0.0), 0, keepdims=True)


def cold_combine(ids, gates, cotangent, results, capacity):
    tok_rows, width = cotangent.shape
    return pl.pallas_call(
        functools.partial(cold_kernel, capacity),
        out_shape=(
            jax.ShapeDtypeStruct((tok_rows, 2 * width), F32),
            jax.ShapeDtypeStruct(gates.shape, F32),
        ),
        compiler_params=pltpu.CompilerParams(vmem_limit_bytes=VMEM_LIMIT),
        cost_estimate=pl.CostEstimate(flops=1 << 36, bytes_accessed=1 << 26, transcendentals=0),
        name="cold_combine",
    )(ids, gates, cotangent, results)


def final_kernel(
    capacity, slots, ids_ref, gate_ref, cot_ref, sum_ref, dots_ref, kept_ref, sent_ref, mix_ref, grad_ref, gate_grad_ref
):
    ids, gates, cot = ids_ref[...], gate_ref[...], cot_ref[...]
    top_count, tok_rows = ids.shape
    width = cot.shape[1]
    hot_rows = kept_ref.shape[0]
    _, hot, _, _, hottest = slot_maps(ids, slots, capacity)
    hottest = hottest.astype(I32)
    gate = jnp.zeros((1, tok_rows), F32)
    for k in range(top_count):
        gate = gate + jnp.where(ids[k : k + 1, :] == hottest, gates[k : k + 1, :], 0.0)
    hot = hot[:hot_rows]
    scale = thirds(jnp.where(hot > 0, gate, 0.0))
    result = (kept_ref[...] + sent_ref[...].astype(F32)).astype(BF16)
    for lo, out_ref in ((0, mix_ref), (width, grad_ref)):
        rows = result[:, lo : lo + width]
        total = matmul_tn(scale[0], rows) + matmul_tn(scale[1], rows) + matmul_tn(scale[2], rows)
        out_ref[...] = (sum_ref[:, lo : lo + width] + total).astype(BF16)
    dots = jnp.where(hot > 0, matmul_nt(result[:, :width], cot), 0.0)
    dot = jnp.sum(dots, 0, keepdims=True)
    gate_grad_ref[...] = dots_ref[...] + jnp.where(ids == hottest, dot, 0.0)


def final_combine(ids, gates, cotangent, sums, dots, kept, sent, slots, capacity):
    return pl.pallas_call(
        functools.partial(final_kernel, capacity, slots),
        out_shape=(
            jax.ShapeDtypeStruct(cotangent.shape, BF16),
            jax.ShapeDtypeStruct(cotangent.shape, BF16),
            jax.ShapeDtypeStruct(gates.shape, F32),
        ),
        compiler_params=pltpu.CompilerParams(vmem_limit_bytes=VMEM_LIMIT),
        name="final_combine",
    )(ids, gates, cotangent, sums, dots, kept, sent)


def tick_kernel(token_ref, *refs):
    refs[-1][...] = token_ref[...]


def tick(token, *after, through=False):
    count = len(after) if through else 0
    anywhere, inside = pl.BlockSpec(memory_space=pl.ANY), pl.BlockSpec(memory_space=pltpu.VMEM)
    out = pl.pallas_call(
        tick_kernel,
        out_shape=tuple(jax.ShapeDtypeStruct(x.shape, x.dtype) for x in after[:count] + (token,)),
        in_specs=[inside] + [anywhere] * len(after),
        out_specs=tuple([anywhere] * count + [inside]),
        input_output_aliases={i + 1: i for i in range(count)},
        compiler_params=pltpu.CompilerParams(vmem_limit_bytes=1 << 20),
        cost_estimate=pl.CostEstimate(flops=1 << 35, bytes_accessed=1 << 25, transcendentals=0),
        name="tick",
    )(token, *after)
    return out if through else out[0]


def shift(x, by):
    ring = lax.axis_size("dp")
    return lax.ppermute(x, "dp", [(i, (i + by) % ring) for i in range(ring)])


def swap(x, bit):
    ring = lax.axis_size("dp")
    pairs = [[i, i ^ bit] for i in range(ring) if not i & bit]
    both = lax.all_gather(x, "dp", axis=0, axis_index_groups=pairs, tiled=False)
    return jnp.where(lax.axis_index("dp") & bit == 0, both[1], both[0])


def shards(tokens, cotangent, gate_probs, expert_ids, up_weight, down_weight):
    tok_rows, width = tokens.shape
    top_count = expert_ids.shape[1]
    experts = lax.axis_size("expert")
    hot_rows = 9 * tok_rows // 16
    capacity = (tok_rows * top_count - hot_rows + experts - 2) // (experts - 1)
    slots = experts * capacity
    up, down = up_weight[0], down_weight[0]
    units = up.shape[0]
    ids, gates = expert_ids.T, gate_probs.T

    outgoing, own, hottest = route(ids, tokens, cotangent, up, down, slots, capacity)
    half = own.shape[0] // 2
    right, left = [own], [own]
    for step in range(3):
        r, l = shift(right[-1], 1), shift(left[-1], -1)
        if step == 0:
            token = tick(hottest, r, l)
        if step == 1:
            r, l, _ = tick(hottest, r, l, through=True)
        right.append(r)
        left.append(l)
    far_up, far_down = shift(right[-1][:half], 1), shift(left[-1][half:], -1)

    piece = 2 * units * width // (experts * capacity)
    pieces = jnp.concatenate([up, down], 0).reshape(experts, capacity, piece)
    dealt = lax.all_to_all(pieces, "expert", 0, 0, tiled=True)
    mine = lax.dynamic_index_in_dim(dealt, token[0, 0], 0)
    outgoing = jnp.concatenate(
        [outgoing.reshape(experts, capacity, 2 * width), jnp.broadcast_to(mine, pieces.shape)], 2
    )
    arrived = lax.all_to_all(outgoing, "expert", 0, 0, tiled=True)
    hot_weights = arrived[:, :, 2 * width :].reshape(2 * units, width)
    arrived = arrived[:, :, : 2 * width].reshape(slots, 2 * width)

    acc = gathered(arrived, [own] + right[1:] + left[1:], units)
    results = last(arrived, acc, far_up, far_down, units)
    results, hot_weights = lax.optimization_barrier((results, hot_weights))
    came_back = lax.all_to_all(
        results.reshape(experts, capacity, 2 * width), "expert", 0, 0, tiled=True
    ).reshape(slots, 2 * width)

    blocks = left + [(far_up, far_down)] + right[:0:-1]
    here = lax.axis_index("dp").astype(I32).reshape(1)
    partials = hot_partials(here, hot_weights, blocks, units, hot_rows, (1, 3, 5, 7, 0, 4, 2, 6))

    def part(first, count):
        return partials[first : first + count].astype(F32)

    got = swap(partials[0:4], 1).astype(F32)
    onward = (part(6, 2) + got[1::2]).astype(BF16)
    stay = part(4, 2) + got[0::2]
    got = swap(onward, 2).astype(F32)
    stay = stay + got
    sent = swap(stay[1].astype(BF16), 4)
    sums, dots = cold_combine(ids, gates, cotangent, came_back, capacity)
    mixture, input_grad, gate_grad = final_combine(
        ids, gates, cotangent, sums, dots, stay[0], sent, slots, capacity
    )
    return mixture, input_grad, gate_grad.T


def solution(mesh):
    rows = P(("dp", "expert"), None)
    weights = P("expert", "dp", None)
    return jax.shard_map(
        shards,
        mesh=mesh,
        in_specs=(rows, rows, rows, rows, weights, weights),
        out_specs=(rows, rows, rows),
        check_vma=False,
    )
```

```python
import functools

import jax
import jax.numpy as jnp
from jax import lax
from jax.experimental import pallas as pl
from jax.experimental.pallas import tpu as pltpu
from jax.sharding import PartitionSpec as P

BF16, F32, I32 = jnp.bfloat16, jnp.float32, jnp.int32
HOT_PAD = 16
VMEM_LIMIT = 16 * 1024 * 1024


def outside(x):
    return pltpu.with_memory_space_constraint(x, pltpu.HBM)


def matmul(a, b):
    return lax.dot_general(a, b, (((1,), (0,)), ((), ())), preferred_element_type=F32)


def matmul_nt(a, b):
    return lax.dot_general(a, b, (((1,), (1,)), ((), ())), preferred_element_type=F32)


def matmul_tn(a, b):
    return lax.dot_general(a, b, (((0,), (0,)), ((), ())), preferred_element_type=F32)


def slot_maps(ids, slots, capacity):
    top_count, tok_rows = ids.shape
    slot = lax.broadcasted_iota(I32, (slots, tok_rows), 0)
    expert = slot // capacity
    named = jnp.zeros((slots, tok_rows), F32)
    for k in range(top_count):
        named = named + (ids[k : k + 1, :] == expert).astype(F32)
    counts = jnp.sum(named, 1, keepdims=True)
    is_hot = (counts == jnp.max(counts)).astype(F32)
    earlier = (
        lax.broadcasted_iota(I32, (tok_rows, tok_rows), 0)
        < lax.broadcasted_iota(I32, (tok_rows, tok_rows), 1)
    ).astype(BF16)
    rank = matmul(named.astype(BF16), earlier)
    cold = named * (1.0 - is_hot) * (rank == (slot % capacity).astype(F32)).astype(F32)
    first = is_hot * (slot[:, :1] % capacity == 0).astype(F32)
    hot_token = jnp.sum(named * first, 0, keepdims=True)
    hot_rank = jnp.sum(rank * first, 0, keepdims=True)
    hot_row = lax.broadcasted_iota(I32, (HOT_PAD, tok_rows), 0).astype(F32)
    hot = hot_token * (hot_rank == hot_row).astype(F32)
    hottest = jnp.sum(first * expert[:, :1].astype(F32), 0, keepdims=True)
    return cold, hot, expert, is_hot, hottest


def route_kernel(
    capacity, ids_ref, tok_ref, cot_ref, up_ref, down_ref, out_ref, own_ref, hottest_ref, tok, cot, sems
):
    slots, width = out_ref.shape[0], tok.shape[1]
    units = up_ref.shape[0]
    half = own_ref.shape[0] // 2
    loads = [pltpu.make_async_copy(tok_ref, tok, sems.at[0]), pltpu.make_async_copy(cot_ref, cot, sems.at[1])]
    copies = [
        pltpu.make_async_copy(up_ref, own_ref.at[pl.ds(0, units)], sems.at[2]),
        pltpu.make_async_copy(down_ref, own_ref.at[pl.ds(half, units)], sems.at[3]),
    ]
    for copy in loads + copies:
        copy.start()
    cold, hot, _, _, hottest = slot_maps(ids_ref[...], slots, capacity)
    cold, hot = cold.astype(BF16), hot.astype(BF16)
    hottest_ref[0, 0] = jnp.max(hottest).astype(I32)
    for copy in loads:
        copy.wait()
    own_ref[units:half, :] = matmul(hot, tok[...]).astype(BF16)
    own_ref[half + units :, :] = matmul(hot, cot[...]).astype(BF16)
    out_ref[:, :width] = matmul(cold, tok[...]).astype(BF16)
    out_ref[:, width:] = matmul(cold, cot[...]).astype(BF16)
    for copy in copies:
        copy.wait()


def route(ids, tokens, cotangent, up, down, slots, capacity):
    tok_rows, width = tokens.shape
    units = up.shape[0]
    anywhere = pl.BlockSpec(memory_space=pl.ANY)
    inside = pl.BlockSpec(memory_space=pltpu.VMEM)
    return pl.pallas_call(
        functools.partial(route_kernel, capacity),
        out_shape=(
            jax.ShapeDtypeStruct((slots, 2 * width), BF16),
            jax.ShapeDtypeStruct((2 * (units + HOT_PAD), width), BF16),
            jax.ShapeDtypeStruct((1, 1), I32),
        ),
        in_specs=[inside] + [anywhere] * 4,
        out_specs=(inside, inside, pl.BlockSpec(memory_space=pltpu.SMEM)),
        scratch_shapes=[
            pltpu.VMEM((tok_rows, width), BF16),
            pltpu.VMEM((tok_rows, width), BF16),
            pltpu.SemaphoreType.DMA((4,)),
        ],
        compiler_params=pltpu.CompilerParams(vmem_limit_bytes=VMEM_LIMIT),
        name="route",
    )(ids, *map(outside, (tokens, cotangent, up, down)))


def deal_kernel(tall, up_ref, down_ref, out_ref, up, down, sems):
    columns = up.shape[1] // 128
    copies = []
    for i, (source, here) in enumerate(((up_ref, up), (down_ref, down))):
        copy = pltpu.make_async_copy(source, here, sems.at[i])
        copy.start()
        copies.append(copy)
    groups = up.shape[0] // tall
    for i, here in enumerate((up, down)):
        copies[i].wait()
        for g in range(groups):
            for j in range(columns):
                out_ref[(i * groups + g) * columns + j] = here[g * tall : (g + 1) * tall, j * 128 : (j + 1) * 128]


def deal(up, down, experts):
    units, width = up.shape
    tall = 2 * units * width // (experts * 128)
    return pl.pallas_call(
        functools.partial(deal_kernel, tall),
        out_shape=jax.ShapeDtypeStruct((experts, tall, 128), BF16),
        in_specs=[pl.BlockSpec(memory_space=pl.ANY)] * 2,
        out_specs=pl.BlockSpec(memory_space=pltpu.VMEM),
        scratch_shapes=[
            pltpu.VMEM((units, width), BF16),
            pltpu.VMEM((units, width), BF16),
            pltpu.SemaphoreType.DMA((2,)),
        ],
        compiler_params=pltpu.CompilerParams(vmem_limit_bytes=VMEM_LIMIT),
        name="deal",
    )(outside(up), outside(down))


def assemble_kernel(hottest_ref, rows_ref, dealt_ref, out_ref, mine, sem):
    copy = pltpu.make_async_copy(dealt_ref.at[hottest_ref[0, 0]], mine, sem)
    copy.start()
    lines = rows_ref.shape[1]
    out_ref[:, :lines, :] = rows_ref[...]
    copy.wait()
    out_ref[:, lines:, :] = jnp.broadcast_to(mine[...][None], (out_ref.shape[0],) + mine.shape)


def assemble(hottest, rows, dealt):
    experts, lines, lanes = rows.shape
    tall = dealt.shape[1]
    return pl.pallas_call(
        assemble_kernel,
        out_shape=jax.ShapeDtypeStruct((experts, lines + tall, lanes), BF16),
        in_specs=[
            pl.BlockSpec(memory_space=pltpu.SMEM),
            pl.BlockSpec(memory_space=pltpu.VMEM),
            pl.BlockSpec(memory_space=pl.ANY),
        ],
        out_specs=pl.BlockSpec(memory_space=pltpu.VMEM),
        scratch_shapes=[pltpu.VMEM((tall, lanes), BF16), pltpu.SemaphoreType.DMA],
        compiler_params=pltpu.CompilerParams(vmem_limit_bytes=VMEM_LIMIT),
        name="assemble",
    )(hottest, rows, dealt)


def activations(pre_act, hidden_grad):
    gating = jax.nn.sigmoid(pre_act)
    hidden = (pre_act * gating).astype(BF16)
    act_grad = (hidden_grad * gating * (1.0 + pre_act * (1.0 - gating))).astype(BF16)
    return hidden, act_grad


def gathered_kernel(units, lines, arrived_ref, *refs):
    pieces, (acc_ref, rows_ref, up, down, wide, sems) = refs[:-6], refs[-6:]
    width = up.shape[1]
    half = pieces[0].shape[0] // 2
    experts = arrived_ref.shape[0]
    capacity = rows_ref.shape[0] // experts
    copies = []
    for i, piece in enumerate(pieces):
        for j, whole in enumerate((up, down)):
            copy = pltpu.make_async_copy(
                piece.at[pl.ds(j * half, units)], whole.at[pl.ds(i * units, units)], sems.at[i, j]
            )
            copy.start()
            copies.append(copy)
    for e in range(experts):
        wide[e * lines : (e + 1) * lines, :] = arrived_ref[e, :lines, :].astype(F32)
    blocks = lines // capacity
    for r in range(capacity):
        for b in range(blocks):
            line = wide[pl.ds(r * blocks + b, experts, stride=lines), :]
            rows_ref[r * experts : (r + 1) * experts, b * 128 : (b + 1) * 128] = line.astype(BF16)
    for copy in copies:
        copy.wait()
    tok, cot = rows_ref[:, :width], rows_ref[:, width:]
    hidden, act_grad = activations(matmul_nt(tok, up[...]), matmul_nt(cot, down[...]))
    acc_ref[:, :width] = matmul(hidden, down[...])
    acc_ref[:, width:] = matmul(act_grad, up[...])


def gathered(arrived, pieces, units, slots):
    experts = arrived.shape[0]
    width = pieces[0].shape[1]
    lines = slots * 2 * width // (experts * 128)
    count = len(pieces)
    return pl.pallas_call(
        functools.partial(gathered_kernel, units, lines),
        out_shape=(
            jax.ShapeDtypeStruct((slots, 2 * width), F32),
            jax.ShapeDtypeStruct((slots, 2 * width), BF16),
        ),
        in_specs=[pl.BlockSpec(memory_space=pltpu.VMEM)] + [pl.BlockSpec(memory_space=pl.ANY)] * count,
        out_specs=(pl.BlockSpec(memory_space=pltpu.VMEM), pl.BlockSpec(memory_space=pltpu.VMEM)),
        scratch_shapes=[
            pltpu.VMEM((count * units, width), BF16),
            pltpu.VMEM((count * units, width), BF16),
            pltpu.VMEM((experts * lines, 128), F32),
            pltpu.SemaphoreType.DMA((count, 2)),
        ],
        compiler_params=pltpu.CompilerParams(vmem_limit_bytes=VMEM_LIMIT + (4 << 20)),
        cost_estimate=pl.CostEstimate(
            flops=8 * slots * count * units * width,
            bytes_accessed=4 * count * units * width,
            transcendentals=0,
        ),
        name="gathered",
    )(arrived, *map(outside, pieces))


def last_kernel(units, rows_ref, acc_ref, up_ref, down_ref, out_ref):
    width = up_ref.shape[1]
    up, down = up_ref[:units, :], down_ref[:units, :]
    tok, cot = rows_ref[:, :width], rows_ref[:, width:]
    hidden, act_grad = activations(matmul_nt(tok, up), matmul_nt(cot, down))
    out_ref[:, :width] = (acc_ref[:, :width] + matmul(hidden, down)).astype(BF16)
    out_ref[:, width:] = (acc_ref[:, width:] + matmul(act_grad, up)).astype(BF16)


def last(rows, acc, up_half, down_half, units):
    return pl.pallas_call(
        functools.partial(last_kernel, units),
        out_shape=jax.ShapeDtypeStruct(rows.shape, BF16),
        compiler_params=pltpu.CompilerParams(vmem_limit_bytes=VMEM_LIMIT),
        name="last",
    )(rows, acc, up_half, down_half)


def hot_kernel(units, lines, hot_rows, where_ref, arrived_ref, *refs):
    blocks, (send_ref, keep_ref, tok, cot, weights, sems) = refs[:-6], refs[-6:]
    ring = len(blocks)
    width = tok.shape[1]
    here = where_ref[0]
    copies = []
    for i, block in enumerate(blocks):
        place = pl.multiple_of((here ^ lax.rem(here + i, ring)) * HOT_PAD, HOT_PAD)
        pair = block if isinstance(block, tuple) else (block, block)
        offset = 0 if isinstance(block, tuple) else units + HOT_PAD
        for j, whole in enumerate((tok, cot)):
            copy = pltpu.make_async_copy(
                pair[j].at[pl.ds(j * offset + units, HOT_PAD)], whole.at[pl.ds(place, HOT_PAD)], sems.at[i, j]
            )
            copy.start()
            copies.append(copy)
    columns = width // 128
    tall = arrived_ref.shape[1] - lines
    for k in range(arrived_ref.shape[0]):
        i, j = k // columns, k % columns
        weights[i * tall : (i + 1) * tall, j * 128 : (j + 1) * 128] = arrived_ref[k, lines:, :]
    for copy in copies:
        copy.wait()
    up, down = weights[:units, :], weights[units:, :]
    hidden, act_grad = activations(matmul_nt(tok[...], up), matmul_nt(cot[...], down))
    packed = send_ref.shape[0]
    row = lax.broadcasted_iota(I32, (packed, ring * HOT_PAD), 0)
    column = lax.broadcasted_iota(I32, (packed, ring * HOT_PAD), 1)
    group = row // hot_rows
    place = (group % 2) * 4 + (group // 2) * 2
    within = place * HOT_PAD + row % hot_rows
    for odd, out_ref in ((1, send_ref), (0, keep_ref)):
        chosen = (column == within + odd * HOT_PAD).astype(F32).astype(BF16)
        picked_hidden = matmul(chosen, hidden).astype(BF16)
        picked_grad = matmul(chosen, act_grad).astype(BF16)
        out_ref[:, :width] = matmul(picked_hidden, down).astype(BF16)
        out_ref[:, width:] = matmul(picked_grad, up).astype(BF16)


def hot_partials(here, arrived, blocks, units, lines, hot_rows, after):
    ring = len(blocks)
    flat, spans = [], []
    for block in blocks:
        spans.append(len(block) if isinstance(block, tuple) else 0)
        flat += list(block) if isinstance(block, tuple) else [block]
    width = flat[0].shape[1]

    def kernel(where_ref, arrived_ref, after_ref, *refs):
        refs, grouped = list(refs), []
        for span in spans:
            grouped.append(tuple(refs.pop(0) for _ in range(span)) if span else refs.pop(0))
        hot_kernel(units, lines, hot_rows, where_ref, arrived_ref, *grouped, *refs)

    inside = pl.BlockSpec(memory_space=pltpu.VMEM)
    packed = jax.ShapeDtypeStruct((ring // 2 * hot_rows, 2 * width), BF16)
    return pl.pallas_call(
        kernel,
        out_shape=(packed, packed),
        in_specs=[pl.BlockSpec(memory_space=pltpu.SMEM), inside]
        + [pl.BlockSpec(memory_space=pl.ANY)] * (1 + len(flat)),
        out_specs=(inside, inside),
        scratch_shapes=[
            pltpu.VMEM((ring * HOT_PAD, width), BF16),
            pltpu.VMEM((ring * HOT_PAD, width), BF16),
            pltpu.VMEM((2 * units, width), BF16),
            pltpu.SemaphoreType.DMA((ring, 2)),
        ],
        compiler_params=pltpu.CompilerParams(vmem_limit_bytes=VMEM_LIMIT),
        name="hot",
    )(here, arrived, after, *map(outside, flat))


def thirds(x):
    first = x.astype(BF16)
    rest = x - first.astype(F32)
    second = rest.astype(BF16)
    third = (rest - second.astype(F32)).astype(BF16)
    return first, second, third


def cold_kernel(capacity, ids_ref, gate_ref, cot_ref, cold_ref, sum_ref, dots_ref):
    ids, gates, cot = ids_ref[...], gate_ref[...], cot_ref[...]
    top_count = ids.shape[0]
    slots = cold_ref.shape[0]
    width = cot.shape[1]
    cold, _, expert, _, _ = slot_maps(ids, slots, capacity)
    per_slot = jnp.zeros(cold.shape, F32)
    for k in range(top_count):
        per_slot = per_slot + jnp.where(ids[k : k + 1, :] == expert, gates[k : k + 1, :], 0.0)
    scale = thirds(jnp.where(cold > 0, per_slot, 0.0))
    for lo in (0, width):
        rows = cold_ref[:, lo : lo + width]
        sum_ref[:, lo : lo + width] = matmul_tn(scale[0], rows) + matmul_tn(scale[1], rows) + matmul_tn(scale[2], rows)
    dots = jnp.where(cold > 0, matmul_nt(cold_ref[:, :width], cot), 0.0)
    for k in range(top_count):
        dots_ref[k : k + 1, :] = jnp.sum(jnp.where(ids[k : k + 1, :] == expert, dots, 0.0), 0, keepdims=True)


def cold_combine(ids, gates, cotangent, results, capacity):
    tok_rows, width = cotangent.shape
    return pl.pallas_call(
        functools.partial(cold_kernel, capacity),
        out_shape=(
            jax.ShapeDtypeStruct((tok_rows, 2 * width), F32),
            jax.ShapeDtypeStruct(gates.shape, F32),
        ),
        compiler_params=pltpu.CompilerParams(vmem_limit_bytes=VMEM_LIMIT),
        cost_estimate=pl.CostEstimate(flops=1 << 36, bytes_accessed=1 << 26, transcendentals=0),
        name="cold_combine",
    )(ids, gates, cotangent, results)


def final_kernel(
    capacity, slots, ids_ref, gate_ref, cot_ref, sum_ref, dots_ref, kept_ref, sent_ref, mix_ref, grad_ref, gate_grad_ref
):
    ids, gates, cot = ids_ref[...], gate_ref[...], cot_ref[...]
    top_count, tok_rows = ids.shape
    width = cot.shape[1]
    hot_rows = kept_ref.shape[0]
    _, hot, _, _, hottest = slot_maps(ids, slots, capacity)
    hottest = hottest.astype(I32)
    gate = jnp.zeros((1, tok_rows), F32)
    for k in range(top_count):
        gate = gate + jnp.where(ids[k : k + 1, :] == hottest, gates[k : k + 1, :], 0.0)
    hot = hot[:hot_rows]
    scale = thirds(jnp.where(hot > 0, gate, 0.0))
    result = (kept_ref[...] + sent_ref[...].astype(F32)).astype(BF16)
    for lo, out_ref in ((0, mix_ref), (width, grad_ref)):
        rows = result[:, lo : lo + width]
        total = matmul_tn(scale[0], rows) + matmul_tn(scale[1], rows) + matmul_tn(scale[2], rows)
        out_ref[...] = (sum_ref[:, lo : lo + width] + total).astype(BF16)
    dots = jnp.where(hot > 0, matmul_nt(result[:, :width], cot), 0.0)
    dot = jnp.sum(dots, 0, keepdims=True)
    gate_grad_ref[...] = dots_ref[...] + jnp.where(ids == hottest, dot, 0.0)


def final_combine(ids, gates, cotangent, sums, dots, kept, sent, slots, capacity):
    return pl.pallas_call(
        functools.partial(final_kernel, capacity, slots),
        out_shape=(
            jax.ShapeDtypeStruct(cotangent.shape, BF16),
            jax.ShapeDtypeStruct(cotangent.shape, BF16),
            jax.ShapeDtypeStruct(gates.shape, F32),
        ),
        compiler_params=pltpu.CompilerParams(vmem_limit_bytes=VMEM_LIMIT),
        name="final_combine",
    )(ids, gates, cotangent, sums, dots, kept, sent)


def tick_kernel(token_ref, *refs):
    refs[-1][0, 0] = token_ref[0, 0]


def tick(token, *after, through=False):
    count = len(after) if through else 0
    anywhere, scalar = pl.BlockSpec(memory_space=pl.ANY), pl.BlockSpec(memory_space=pltpu.SMEM)
    out = pl.pallas_call(
        tick_kernel,
        out_shape=tuple(jax.ShapeDtypeStruct(x.shape, x.dtype) for x in after[:count] + (token,)),
        in_specs=[scalar] + [anywhere] * len(after),
        out_specs=tuple([anywhere] * count + [scalar]),
        input_output_aliases={i + 1: i for i in range(count)},
        compiler_params=pltpu.CompilerParams(vmem_limit_bytes=1 << 20),
        cost_estimate=pl.CostEstimate(flops=1 << 35, bytes_accessed=1 << 25, transcendentals=0),
        name="tick",
    )(token, *after)
    return out if through else out[0]


def shift(x, by):
    ring = lax.axis_size("dp")
    return lax.ppermute(x, "dp", [(i, (i + by) % ring) for i in range(ring)])


def swap(x, bit):
    ring = lax.axis_size("dp")
    pairs = [[i, i ^ bit] for i in range(ring) if not i & bit]
    both = lax.all_gather(x, "dp", axis=0, axis_index_groups=pairs, tiled=False)
    return jnp.where(lax.axis_index("dp") & bit == 0, both[1], both[0])


def shards(tokens, cotangent, gate_probs, expert_ids, up_weight, down_weight):
    tok_rows, width = tokens.shape
    top_count = expert_ids.shape[1]
    experts = lax.axis_size("expert")
    hot_rows = 9 * tok_rows // 16
    capacity = (tok_rows * top_count - hot_rows + experts - 2) // (experts - 1)
    slots = experts * capacity
    up, down = up_weight[0], down_weight[0]
    units = up.shape[0]
    ids, gates = expert_ids.T, gate_probs.T

    outgoing, own, hottest = route(ids, tokens, cotangent, up, down, slots, capacity)
    half = own.shape[0] // 2
    right, left = [own], [own]
    for step in range(3):
        r, l = shift(right[-1], 1), shift(left[-1], -1)
        if step == 0:
            token = tick(hottest, r, l)
        if step == 1:
            r, l, _ = tick(hottest, r, l, through=True)
        right.append(r)
        left.append(l)
    far_up, far_down = shift(right[-1][:half], 1), shift(left[-1][half:], -1)

    dealt = lax.all_to_all(deal(up, down, experts), "expert", 0, 0, tiled=True)
    lines = capacity * 2 * width // 128
    outgoing = assemble(token, outgoing.reshape(experts, lines, 128), dealt)
    arrived = lax.all_to_all(outgoing, "expert", 0, 0, tiled=True)

    acc, rows = gathered(arrived, [own] + right[1:] + left[1:], units, slots)
    results = last(rows, acc, far_up, far_down, units)
    results = results.reshape(capacity, experts, 2 * width).transpose(1, 0, 2)
    came_back = lax.all_to_all(results, "expert", 0, 0, tiled=True).reshape(slots, 2 * width)

    blocks = left + [(far_up, far_down)] + right[:0:-1]
    here = lax.axis_index("dp").astype(I32).reshape(1)
    send, keep = hot_partials(here, arrived, blocks, units, lines, hot_rows, results)
    both = keep.astype(F32) + swap(send, 1).astype(F32)
    stay = both[: 2 * hot_rows] + swap(both[2 * hot_rows :].astype(BF16), 2).astype(F32)
    sent = swap(stay[hot_rows:].astype(BF16), 4)
    kept = stay[:hot_rows]
    sums, dots = cold_combine(ids, gates, cotangent, came_back, capacity)
    mixture, input_grad, gate_grad = final_combine(
        ids, gates, cotangent, sums, dots, kept, sent, slots, capacity
    )
    return mixture, input_grad, gate_grad.T


def solution(mesh):
    rows = P(("dp", "expert"), None)
    weights = P("expert", "dp", None)
    return jax.shard_map(
        shards,
        mesh=mesh,
        in_specs=(rows, rows, rows, rows, weights, weights),
        out_specs=(rows, rows, rows),
        check_vma=False,
    )
```

```python
import functools

import jax
import jax.numpy as jnp
from jax import lax
from jax.experimental import pallas as pl
from jax.experimental.pallas import tpu as pltpu
from jax.sharding import PartitionSpec as P

BF16, F32, I32 = jnp.bfloat16, jnp.float32, jnp.int32
HOT_PAD = 16
VMEM_LIMIT = 16 * 1024 * 1024


def outside(x):
    return pltpu.with_memory_space_constraint(x, pltpu.HBM)


def matmul(a, b):
    return lax.dot_general(a, b, (((1,), (0,)), ((), ())), preferred_element_type=F32)


def matmul_nt(a, b):
    return lax.dot_general(a, b, (((1,), (1,)), ((), ())), preferred_element_type=F32)


def matmul_tn(a, b):
    return lax.dot_general(a, b, (((0,), (0,)), ((), ())), preferred_element_type=F32)


def slot_maps(ids, slots, capacity):
    top_count, tok_rows = ids.shape
    slot = lax.broadcasted_iota(I32, (slots, tok_rows), 0)
    expert = slot // capacity
    named = jnp.zeros((slots, tok_rows), F32)
    for k in range(top_count):
        named = named + (ids[k : k + 1, :] == expert).astype(F32)
    counts = jnp.sum(named, 1, keepdims=True)
    is_hot = (counts == jnp.max(counts)).astype(F32)
    earlier = (
        lax.broadcasted_iota(I32, (tok_rows, tok_rows), 0)
        < lax.broadcasted_iota(I32, (tok_rows, tok_rows), 1)
    ).astype(BF16)
    rank = matmul(named.astype(BF16), earlier)
    cold = named * (1.0 - is_hot) * (rank == (slot % capacity).astype(F32)).astype(F32)
    first = is_hot * (slot[:, :1] % capacity == 0).astype(F32)
    hot_token = jnp.sum(named * first, 0, keepdims=True)
    hot_rank = jnp.sum(rank * first, 0, keepdims=True)
    hot_row = lax.broadcasted_iota(I32, (HOT_PAD, tok_rows), 0).astype(F32)
    hot = hot_token * (hot_rank == hot_row).astype(F32)
    hottest = jnp.sum(first * expert[:, :1].astype(F32), 0, keepdims=True)
    return cold, hot, expert, is_hot, hottest


def route_kernel(
    capacity, ids_ref, tok_ref, cot_ref, up_ref, down_ref, out_ref, own_ref, hottest_ref, tok, cot, sems
):
    slots, width = out_ref.shape[0], tok.shape[1]
    units = up_ref.shape[0]
    half = own_ref.shape[0] // 2
    loads = [pltpu.make_async_copy(tok_ref, tok, sems.at[0]), pltpu.make_async_copy(cot_ref, cot, sems.at[1])]
    copies = [
        pltpu.make_async_copy(up_ref, own_ref.at[pl.ds(0, units)], sems.at[2]),
        pltpu.make_async_copy(down_ref, own_ref.at[pl.ds(half, units)], sems.at[3]),
    ]
    for copy in loads + copies:
        copy.start()
    cold, hot, _, _, hottest = slot_maps(ids_ref[...], slots, capacity)
    cold, hot = cold.astype(BF16), hot.astype(BF16)
    hottest_ref[0, 0] = jnp.max(hottest).astype(I32)
    for copy in loads:
        copy.wait()
    own_ref[units:half, :] = matmul(hot, tok[...]).astype(BF16)
    own_ref[half + units :, :] = matmul(hot, cot[...]).astype(BF16)
    out_ref[:, :width] = matmul(cold, tok[...]).astype(BF16)
    out_ref[:, width:] = matmul(cold, cot[...]).astype(BF16)
    for copy in copies:
        copy.wait()


def route(ids, tokens, cotangent, up, down, slots, capacity):
    tok_rows, width = tokens.shape
    units = up.shape[0]
    anywhere = pl.BlockSpec(memory_space=pl.ANY)
    inside = pl.BlockSpec(memory_space=pltpu.VMEM)
    return pl.pallas_call(
        functools.partial(route_kernel, capacity),
        out_shape=(
            jax.ShapeDtypeStruct((slots, 2 * width), BF16),
            jax.ShapeDtypeStruct((2 * (units + HOT_PAD), width), BF16),
            jax.ShapeDtypeStruct((1, 1), I32),
        ),
        in_specs=[inside] + [anywhere] * 4,
        out_specs=(inside, inside, pl.BlockSpec(memory_space=pltpu.SMEM)),
        scratch_shapes=[
            pltpu.VMEM((tok_rows, width), BF16),
            pltpu.VMEM((tok_rows, width), BF16),
            pltpu.SemaphoreType.DMA((4,)),
        ],
        compiler_params=pltpu.CompilerParams(vmem_limit_bytes=VMEM_LIMIT),
        name="route",
    )(ids, *map(outside, (tokens, cotangent, up, down)))


def assemble_kernel(tall, rows_ref, up_ref, down_ref, out_ref, up, down, sems):
    copies = []
    for i, (source, here) in enumerate(((up_ref, up), (down_ref, down))):
        copy = pltpu.make_async_copy(source, here, sems.at[i])
        copy.start()
        copies.append(copy)
    lines = rows_ref.shape[1]
    out_ref[:, :lines, :] = rows_ref[...]
    columns = up.shape[1] // 128
    groups = up.shape[0] // tall
    for i, here in enumerate((up, down)):
        copies[i].wait()
        for g in range(groups):
            for j in range(columns):
                out_ref[(i * groups + g) * columns + j, lines:, :] = here[
                    g * tall : (g + 1) * tall, j * 128 : (j + 1) * 128
                ]


def assemble(rows, up, down):
    experts, lines, lanes = rows.shape
    units, width = up.shape
    tall = 2 * units * width // (experts * lanes)
    return pl.pallas_call(
        functools.partial(assemble_kernel, tall),
        out_shape=jax.ShapeDtypeStruct((experts, lines + tall, lanes), BF16),
        in_specs=[pl.BlockSpec(memory_space=pltpu.VMEM)] + [pl.BlockSpec(memory_space=pl.ANY)] * 2,
        out_specs=pl.BlockSpec(memory_space=pltpu.VMEM),
        scratch_shapes=[
            pltpu.VMEM((units, width), BF16),
            pltpu.VMEM((units, width), BF16),
            pltpu.SemaphoreType.DMA((2,)),
        ],
        compiler_params=pltpu.CompilerParams(vmem_limit_bytes=VMEM_LIMIT),
        name="assemble",
    )(rows, outside(up), outside(down))


def repeat_kernel(lines, hottest_ref, arrived_ref, out_ref):
    mine = arrived_ref[hottest_ref[0, 0], lines:, :]
    out_ref[...] = jnp.broadcast_to(mine[None], out_ref.shape)


def repeat(hottest, arrived, lines):
    experts, height, lanes = arrived.shape
    inside = pl.BlockSpec(memory_space=pltpu.VMEM)
    return pl.pallas_call(
        functools.partial(repeat_kernel, lines),
        out_shape=jax.ShapeDtypeStruct((experts, height - lines, lanes), BF16),
        in_specs=[pl.BlockSpec(memory_space=pltpu.SMEM), inside],
        out_specs=inside,
        compiler_params=pltpu.CompilerParams(vmem_limit_bytes=VMEM_LIMIT),
        name="repeat",
    )(hottest, arrived)


def activations(pre_act, hidden_grad):
    gating = jax.nn.sigmoid(pre_act)
    hidden = (pre_act * gating).astype(BF16)
    act_grad = (hidden_grad * gating * (1.0 + pre_act * (1.0 - gating))).astype(BF16)
    return hidden, act_grad


def gathered_kernel(units, lines, arrived_ref, *refs):
    pieces, (acc_ref, rows_ref, up, down, wide, sems) = refs[:-6], refs[-6:]
    width = up.shape[1]
    half = pieces[0].shape[0] // 2
    experts = arrived_ref.shape[0]
    capacity = rows_ref.shape[0] // experts
    copies = []
    for i, piece in enumerate(pieces):
        for j, whole in enumerate((up, down)):
            copy = pltpu.make_async_copy(
                piece.at[pl.ds(j * half, units)], whole.at[pl.ds(i * units, units)], sems.at[i, j]
            )
            copy.start()
            copies.append(copy)
    for e in range(experts):
        wide[e * lines : (e + 1) * lines, :] = arrived_ref[e, :lines, :].astype(F32)
    blocks = lines // capacity
    for r in range(capacity):
        for b in range(blocks):
            line = wide[pl.ds(r * blocks + b, experts, stride=lines), :]
            rows_ref[r * experts : (r + 1) * experts, b * 128 : (b + 1) * 128] = line.astype(BF16)
    for copy in copies:
        copy.wait()
    tok, cot = rows_ref[:, :width], rows_ref[:, width:]
    hidden, act_grad = activations(matmul_nt(tok, up[...]), matmul_nt(cot, down[...]))
    acc_ref[:, :width] = matmul(hidden, down[...])
    acc_ref[:, width:] = matmul(act_grad, up[...])


def gathered(arrived, pieces, units, slots):
    experts = arrived.shape[0]
    width = pieces[0].shape[1]
    lines = slots * 2 * width // (experts * 128)
    count = len(pieces)
    return pl.pallas_call(
        functools.partial(gathered_kernel, units, lines),
        out_shape=(
            jax.ShapeDtypeStruct((slots, 2 * width), F32),
            jax.ShapeDtypeStruct((slots, 2 * width), BF16),
        ),
        in_specs=[pl.BlockSpec(memory_space=pltpu.VMEM)] + [pl.BlockSpec(memory_space=pl.ANY)] * count,
        out_specs=(pl.BlockSpec(memory_space=pltpu.VMEM), pl.BlockSpec(memory_space=pltpu.VMEM)),
        scratch_shapes=[
            pltpu.VMEM((count * units, width), BF16),
            pltpu.VMEM((count * units, width), BF16),
            pltpu.VMEM((experts * lines, 128), F32),
            pltpu.SemaphoreType.DMA((count, 2)),
        ],
        compiler_params=pltpu.CompilerParams(vmem_limit_bytes=VMEM_LIMIT + (4 << 20)),
        cost_estimate=pl.CostEstimate(
            flops=8 * slots * count * units * width,
            bytes_accessed=4 * count * units * width,
            transcendentals=0,
        ),
        name="gathered",
    )(arrived, *map(outside, pieces))


def last_kernel(units, rows_ref, acc_ref, up_ref, down_ref, out_ref):
    width = up_ref.shape[1]
    up, down = up_ref[:units, :], down_ref[:units, :]
    tok, cot = rows_ref[:, :width], rows_ref[:, width:]
    hidden, act_grad = activations(matmul_nt(tok, up), matmul_nt(cot, down))
    out_ref[:, :width] = (acc_ref[:, :width] + matmul(hidden, down)).astype(BF16)
    out_ref[:, width:] = (acc_ref[:, width:] + matmul(act_grad, up)).astype(BF16)


def last(rows, acc, up_half, down_half, units):
    return pl.pallas_call(
        functools.partial(last_kernel, units),
        out_shape=jax.ShapeDtypeStruct(rows.shape, BF16),
        compiler_params=pltpu.CompilerParams(vmem_limit_bytes=VMEM_LIMIT),
        name="last",
    )(rows, acc, up_half, down_half)


def hot_kernel(units, hot_rows, where_ref, pieces_ref, *refs):
    blocks, (send_ref, keep_ref, tok, cot, weights, sems) = refs[:-6], refs[-6:]
    ring = len(blocks)
    width = tok.shape[1]
    here = where_ref[0]
    copies = []
    for i, block in enumerate(blocks):
        place = pl.multiple_of((here ^ lax.rem(here + i, ring)) * HOT_PAD, HOT_PAD)
        pair = block if isinstance(block, tuple) else (block, block)
        offset = 0 if isinstance(block, tuple) else units + HOT_PAD
        for j, whole in enumerate((tok, cot)):
            copy = pltpu.make_async_copy(
                pair[j].at[pl.ds(j * offset + units, HOT_PAD)], whole.at[pl.ds(place, HOT_PAD)], sems.at[i, j]
            )
            copy.start()
            copies.append(copy)
    columns = width // 128
    tall = pieces_ref.shape[1]
    for k in range(pieces_ref.shape[0]):
        i, j = k // columns, k % columns
        weights[i * tall : (i + 1) * tall, j * 128 : (j + 1) * 128] = pieces_ref[k]
    for copy in copies:
        copy.wait()
    up, down = weights[:units, :], weights[units:, :]
    hidden, act_grad = activations(matmul_nt(tok[...], up), matmul_nt(cot[...], down))
    packed = send_ref.shape[0]
    row = lax.broadcasted_iota(I32, (packed, ring * HOT_PAD), 0)
    column = lax.broadcasted_iota(I32, (packed, ring * HOT_PAD), 1)
    group = row // hot_rows
    place = (group % 2) * 4 + (group // 2) * 2
    within = place * HOT_PAD + row % hot_rows
    for odd, out_ref in ((1, send_ref), (0, keep_ref)):
        chosen = (column == within + odd * HOT_PAD).astype(F32).astype(BF16)
        picked_hidden = matmul(chosen, hidden).astype(BF16)
        picked_grad = matmul(chosen, act_grad).astype(BF16)
        out_ref[:, :width] = matmul(picked_hidden, down).astype(BF16)
        out_ref[:, width:] = matmul(picked_grad, up).astype(BF16)


def hot_partials(here, pieces, blocks, units, hot_rows, after):
    ring = len(blocks)
    flat, spans = [], []
    for block in blocks:
        spans.append(len(block) if isinstance(block, tuple) else 0)
        flat += list(block) if isinstance(block, tuple) else [block]
    width = flat[0].shape[1]

    def kernel(where_ref, pieces_ref, after_ref, *refs):
        refs, grouped = list(refs), []
        for span in spans:
            grouped.append(tuple(refs.pop(0) for _ in range(span)) if span else refs.pop(0))
        hot_kernel(units, hot_rows, where_ref, pieces_ref, *grouped, *refs)

    inside = pl.BlockSpec(memory_space=pltpu.VMEM)
    packed = jax.ShapeDtypeStruct((ring // 2 * hot_rows, 2 * width), BF16)
    return pl.pallas_call(
        kernel,
        out_shape=(packed, packed),
        in_specs=[pl.BlockSpec(memory_space=pltpu.SMEM), inside]
        + [pl.BlockSpec(memory_space=pl.ANY)] * (1 + len(flat)),
        out_specs=(inside, inside),
        scratch_shapes=[
            pltpu.VMEM((ring * HOT_PAD, width), BF16),
            pltpu.VMEM((ring * HOT_PAD, width), BF16),
            pltpu.VMEM((2 * units, width), BF16),
            pltpu.SemaphoreType.DMA((ring, 2)),
        ],
        compiler_params=pltpu.CompilerParams(vmem_limit_bytes=VMEM_LIMIT),
        name="hot",
    )(here, pieces, after, *map(outside, flat))


def thirds(x):
    first = x.astype(BF16)
    rest = x - first.astype(F32)
    second = rest.astype(BF16)
    third = (rest - second.astype(F32)).astype(BF16)
    return first, second, third


def cold_kernel(capacity, ids_ref, gate_ref, cot_ref, cold_ref, sum_ref, dots_ref):
    ids, gates, cot = ids_ref[...], gate_ref[...], cot_ref[...]
    top_count = ids.shape[0]
    slots = cold_ref.shape[0]
    width = cot.shape[1]
    cold, _, expert, _, _ = slot_maps(ids, slots, capacity)
    per_slot = jnp.zeros(cold.shape, F32)
    for k in range(top_count):
        per_slot = per_slot + jnp.where(ids[k : k + 1, :] == expert, gates[k : k + 1, :], 0.0)
    scale = thirds(jnp.where(cold > 0, per_slot, 0.0))
    for lo in (0, width):
        rows = cold_ref[:, lo : lo + width]
        sum_ref[:, lo : lo + width] = matmul_tn(scale[0], rows) + matmul_tn(scale[1], rows) + matmul_tn(scale[2], rows)
    dots = jnp.where(cold > 0, matmul_nt(cold_ref[:, :width], cot), 0.0)
    for k in range(top_count):
        dots_ref[k : k + 1, :] = jnp.sum(jnp.where(ids[k : k + 1, :] == expert, dots, 0.0), 0, keepdims=True)


def cold_combine(ids, gates, cotangent, results, capacity):
    tok_rows, width = cotangent.shape
    return pl.pallas_call(
        functools.partial(cold_kernel, capacity),
        out_shape=(
            jax.ShapeDtypeStruct((tok_rows, 2 * width), F32),
            jax.ShapeDtypeStruct(gates.shape, F32),
        ),
        compiler_params=pltpu.CompilerParams(vmem_limit_bytes=VMEM_LIMIT),
        cost_estimate=pl.CostEstimate(flops=1 << 36, bytes_accessed=1 << 26, transcendentals=0),
        name="cold_combine",
    )(ids, gates, cotangent, results)


def final_kernel(
    capacity, slots, ids_ref, gate_ref, cot_ref, sum_ref, dots_ref, kept_ref, sent_ref, mix_ref, grad_ref, gate_grad_ref
):
    ids, gates, cot = ids_ref[...], gate_ref[...], cot_ref[...]
    top_count, tok_rows = ids.shape
    width = cot.shape[1]
    hot_rows = kept_ref.shape[0]
    _, hot, _, _, hottest = slot_maps(ids, slots, capacity)
    hottest = hottest.astype(I32)
    gate = jnp.zeros((1, tok_rows), F32)
    for k in range(top_count):
        gate = gate + jnp.where(ids[k : k + 1, :] == hottest, gates[k : k + 1, :], 0.0)
    hot = hot[:hot_rows]
    scale = thirds(jnp.where(hot > 0, gate, 0.0))
    result = (kept_ref[...] + sent_ref[...].astype(F32)).astype(BF16)
    for lo, out_ref in ((0, mix_ref), (width, grad_ref)):
        rows = result[:, lo : lo + width]
        total = matmul_tn(scale[0], rows) + matmul_tn(scale[1], rows) + matmul_tn(scale[2], rows)
        out_ref[...] = (sum_ref[:, lo : lo + width] + total).astype(BF16)
    dots = jnp.where(hot > 0, matmul_nt(result[:, :width], cot), 0.0)
    dot = jnp.sum(dots, 0, keepdims=True)
    gate_grad_ref[...] = dots_ref[...] + jnp.where(ids == hottest, dot, 0.0)


def final_combine(ids, gates, cotangent, sums, dots, kept, sent, slots, capacity):
    return pl.pallas_call(
        functools.partial(final_kernel, capacity, slots),
        out_shape=(
            jax.ShapeDtypeStruct(cotangent.shape, BF16),
            jax.ShapeDtypeStruct(cotangent.shape, BF16),
            jax.ShapeDtypeStruct(gates.shape, F32),
        ),
        compiler_params=pltpu.CompilerParams(vmem_limit_bytes=VMEM_LIMIT),
        name="final_combine",
    )(ids, gates, cotangent, sums, dots, kept, sent)


TICK = pl.CostEstimate(flops=1 << 35, bytes_accessed=1 << 25, transcendentals=0)


def tick_kernel(token_ref, *refs):
    refs[-1][0, 0] = token_ref[0, 0]


def tick(token, *after):
    scalar = pl.BlockSpec(memory_space=pltpu.SMEM)
    return pl.pallas_call(
        tick_kernel,
        out_shape=jax.ShapeDtypeStruct(token.shape, token.dtype),
        in_specs=[scalar] + [pl.BlockSpec(memory_space=pl.ANY)] * len(after),
        out_specs=scalar,
        compiler_params=pltpu.CompilerParams(vmem_limit_bytes=1 << 20),
        cost_estimate=pl.CostEstimate(flops=22 << 30, bytes_accessed=1 << 10, transcendentals=0),
        name="tick",
    )(token, *after)


def gate_kernel(*refs):
    pass


def gate(*arrays):
    anywhere = pl.BlockSpec(memory_space=pl.ANY)
    return pl.pallas_call(
        gate_kernel,
        out_shape=tuple(jax.ShapeDtypeStruct(x.shape, x.dtype) for x in arrays),
        in_specs=[anywhere] * len(arrays),
        out_specs=tuple([anywhere] * len(arrays)),
        input_output_aliases={i: i for i in range(len(arrays))},
        compiler_params=pltpu.CompilerParams(vmem_limit_bytes=1 << 20),
        cost_estimate=TICK,
        name="gate",
    )(*arrays)


def shift(x, by):
    ring = lax.axis_size("dp")
    return lax.ppermute(x, "dp", [(i, (i + by) % ring) for i in range(ring)])


def swap(x, bit):
    ring = lax.axis_size("dp")
    pairs = [[i, i ^ bit] for i in range(ring) if not i & bit]
    both = lax.all_gather(x, "dp", axis=0, axis_index_groups=pairs, tiled=False)
    return jnp.where(lax.axis_index("dp") & bit == 0, both[1], both[0])


def shards(tokens, cotangent, gate_probs, expert_ids, up_weight, down_weight):
    tok_rows, width = tokens.shape
    top_count = expert_ids.shape[1]
    experts = lax.axis_size("expert")
    hot_rows = 9 * tok_rows // 16
    capacity = (tok_rows * top_count - hot_rows + experts - 2) // (experts - 1)
    slots = experts * capacity
    up, down = up_weight[0], down_weight[0]
    units = up.shape[0]
    ids, gates = expert_ids.T, gate_probs.T

    outgoing, own, hottest = route(ids, tokens, cotangent, up, down, slots, capacity)
    half = own.shape[0] // 2
    right, left = [own], [own]
    for step in range(3):
        r, l = shift(right[-1], 1), shift(left[-1], -1)
        if step == 1:
            token = tick(hottest, r, l)
        if step in (2,):
            r, l = gate(r, l)
        right.append(r)
        left.append(l)
    far_up, far_down = shift(right[-1][:half], 1), shift(left[-1][half:], -1)

    lines = capacity * 2 * width // 128
    outgoing = assemble(outgoing.reshape(experts, lines, 128), up, down)
    arrived = lax.all_to_all(outgoing, "expert", 0, 0, tiled=True)
    hot_pieces = lax.all_to_all(repeat(token, arrived, lines), "expert", 0, 0, tiled=True)

    acc, rows = gathered(arrived, [own] + right[1:] + left[1:], units, slots)
    results = last(rows, acc, far_up, far_down, units)
    results = results.reshape(capacity, experts, 2 * width).transpose(1, 0, 2)
    came_back = lax.all_to_all(results, "expert", 0, 0, tiled=True).reshape(slots, 2 * width)

    blocks = left + [(far_up, far_down)] + right[:0:-1]
    here = lax.axis_index("dp").astype(I32).reshape(1)
    send, keep = hot_partials(here, hot_pieces, blocks, units, hot_rows, results)
    both = keep.astype(F32) + swap(send, 1).astype(F32)
    kept, onward = both[:hot_rows], both[hot_rows:].astype(BF16)
    ring = lax.axis_size("dp")
    parity = [[i for i in range(ring) if i % 2 == odd] for odd in range(2)]
    quad = lax.all_gather(onward, "dp", axis=0, axis_index_groups=parity, tiled=False)
    sent = jnp.zeros(kept.shape, F32)
    for i, place in enumerate((4, 2, 6)):
        theirs = lax.dynamic_index_in_dim(quad, (here[0] ^ place) // 2, 0, keepdims=False)
        sent = sent + theirs[i * hot_rows : (i + 1) * hot_rows].astype(F32)
    sums, dots = cold_combine(ids, gates, cotangent, came_back, capacity)
    mixture, input_grad, gate_grad = final_combine(
        ids, gates, cotangent, sums, dots, kept, sent, slots, capacity
    )
    return mixture, input_grad, gate_grad.T


def solution(mesh):
    rows = P(("dp", "expert"), None)
    weights = P("expert", "dp", None)
    return jax.shard_map(
        shards,
        mesh=mesh,
        in_specs=(rows, rows, rows, rows, weights, weights),
        out_specs=(rows, rows, rows),
        check_vma=False,
    )
```

```python
import functools

import jax
import jax.numpy as jnp
from jax import lax
from jax.experimental import pallas as pl
from jax.experimental.pallas import tpu as pltpu
from jax.sharding import PartitionSpec as P

BF16, F32, I32 = jnp.bfloat16, jnp.float32, jnp.int32
HOT_PAD = 16
VMEM_LIMIT = 16 * 1024 * 1024


def outside(x):
    return pltpu.with_memory_space_constraint(x, pltpu.HBM)


def matmul(a, b):
    return lax.dot_general(a, b, (((1,), (0,)), ((), ())), preferred_element_type=F32)


def matmul_nt(a, b):
    return lax.dot_general(a, b, (((1,), (1,)), ((), ())), preferred_element_type=F32)


def matmul_tn(a, b):
    return lax.dot_general(a, b, (((0,), (0,)), ((), ())), preferred_element_type=F32)


def slot_maps(ids, slots, capacity, slot_major=False):
    top_count, tok_rows = ids.shape
    slot = lax.broadcasted_iota(I32, (slots, tok_rows), 0)
    experts = slots // capacity
    expert, within = (slot % experts, slot // experts) if slot_major else (slot // capacity, slot % capacity)
    named = jnp.zeros((slots, tok_rows), F32)
    for k in range(top_count):
        named = named + (ids[k : k + 1, :] == expert).astype(F32)
    counts = jnp.sum(named, 1, keepdims=True)
    is_hot = (counts == jnp.max(counts)).astype(F32)
    earlier = (
        lax.broadcasted_iota(I32, (tok_rows, tok_rows), 0)
        < lax.broadcasted_iota(I32, (tok_rows, tok_rows), 1)
    ).astype(BF16)
    rank = matmul(named.astype(BF16), earlier)
    cold = named * (1.0 - is_hot) * (rank == within.astype(F32)).astype(F32)
    first = is_hot * (within[:, :1] == 0).astype(F32)
    hot_token = jnp.sum(named * first, 0, keepdims=True)
    hot_rank = jnp.sum(rank * first, 0, keepdims=True)
    hot_row = lax.broadcasted_iota(I32, (HOT_PAD, tok_rows), 0).astype(F32)
    hot = hot_token * (hot_rank == hot_row).astype(F32)
    hottest = jnp.sum(first * expert[:, :1].astype(F32), 0, keepdims=True)
    return cold, hot, expert, is_hot, hottest


def route_kernel(
    capacity, ids_ref, tok_ref, cot_ref, up_ref, down_ref, out_ref, own_ref, hottest_ref, tok, cot, sems
):
    slots, width = out_ref.shape[0], tok.shape[1]
    units = up_ref.shape[0]
    half = own_ref.shape[0] // 2
    loads = [pltpu.make_async_copy(tok_ref, tok, sems.at[0]), pltpu.make_async_copy(cot_ref, cot, sems.at[1])]
    copies = [
        pltpu.make_async_copy(up_ref, own_ref.at[pl.ds(0, units)], sems.at[2]),
        pltpu.make_async_copy(down_ref, own_ref.at[pl.ds(half, units)], sems.at[3]),
    ]
    for copy in loads + copies:
        copy.start()
    cold, hot, _, _, hottest = slot_maps(ids_ref[...], slots, capacity)
    cold, hot = cold.astype(BF16), hot.astype(BF16)
    hottest_ref[0, 0] = jnp.max(hottest).astype(I32)
    for copy in loads:
        copy.wait()
    own_ref[units:half, :] = matmul(hot, tok[...]).astype(BF16)
    own_ref[half + units :, :] = matmul(hot, cot[...]).astype(BF16)
    out_ref[:, :width] = matmul(cold, tok[...]).astype(BF16)
    out_ref[:, width:] = matmul(cold, cot[...]).astype(BF16)
    for copy in copies:
        copy.wait()


def route(ids, tokens, cotangent, up, down, slots, capacity):
    tok_rows, width = tokens.shape
    units = up.shape[0]
    anywhere = pl.BlockSpec(memory_space=pl.ANY)
    inside = pl.BlockSpec(memory_space=pltpu.VMEM)
    return pl.pallas_call(
        functools.partial(route_kernel, capacity),
        out_shape=(
            jax.ShapeDtypeStruct((slots, 2 * width), BF16),
            jax.ShapeDtypeStruct((2 * (units + HOT_PAD), width), BF16),
            jax.ShapeDtypeStruct((1, 1), I32),
        ),
        in_specs=[inside] + [anywhere] * 4,
        out_specs=(inside, inside, pl.BlockSpec(memory_space=pltpu.SMEM)),
        scratch_shapes=[
            pltpu.VMEM((tok_rows, width), BF16),
            pltpu.VMEM((tok_rows, width), BF16),
            pltpu.SemaphoreType.DMA((4,)),
        ],
        compiler_params=pltpu.CompilerParams(vmem_limit_bytes=VMEM_LIMIT),
        name="route",
    )(ids, *map(outside, (tokens, cotangent, up, down)))


def assemble_kernel(tall, rows_ref, up_ref, down_ref, out_ref, up, down, sems):
    copies = []
    for i, (source, here) in enumerate(((up_ref, up), (down_ref, down))):
        copy = pltpu.make_async_copy(source, here, sems.at[i])
        copy.start()
        copies.append(copy)
    lines = rows_ref.shape[1]
    out_ref[:, :lines, :] = rows_ref[...]
    columns = up.shape[1] // 128
    groups = up.shape[0] // tall
    for i, here in enumerate((up, down)):
        copies[i].wait()
        for g in range(groups):
            for j in range(columns):
                out_ref[(i * groups + g) * columns + j, lines:, :] = here[
                    g * tall : (g + 1) * tall, j * 128 : (j + 1) * 128
                ]


def assemble(rows, up, down):
    experts, lines, lanes = rows.shape
    units, width = up.shape
    tall = 2 * units * width // (experts * lanes)
    return pl.pallas_call(
        functools.partial(assemble_kernel, tall),
        out_shape=jax.ShapeDtypeStruct((experts, lines + tall, lanes), BF16),
        in_specs=[pl.BlockSpec(memory_space=pltpu.VMEM)] + [pl.BlockSpec(memory_space=pl.ANY)] * 2,
        out_specs=pl.BlockSpec(memory_space=pltpu.VMEM),
        scratch_shapes=[
            pltpu.VMEM((units, width), BF16),
            pltpu.VMEM((units, width), BF16),
            pltpu.SemaphoreType.DMA((2,)),
        ],
        compiler_params=pltpu.CompilerParams(vmem_limit_bytes=VMEM_LIMIT),
        name="assemble",
    )(rows, outside(up), outside(down))


def repeat_kernel(lines, hottest_ref, arrived_ref, out_ref):
    mine = arrived_ref[hottest_ref[0, 0], lines:, :]
    out_ref[...] = jnp.broadcast_to(mine[None], out_ref.shape)


def repeat(hottest, arrived, lines):
    experts, height, lanes = arrived.shape
    inside = pl.BlockSpec(memory_space=pltpu.VMEM)
    return pl.pallas_call(
        functools.partial(repeat_kernel, lines),
        out_shape=jax.ShapeDtypeStruct((experts, height - lines, lanes), BF16),
        in_specs=[pl.BlockSpec(memory_space=pltpu.SMEM), inside],
        out_specs=inside,
        compiler_params=pltpu.CompilerParams(vmem_limit_bytes=VMEM_LIMIT),
        name="repeat",
    )(hottest, arrived)


def activations(pre_act, hidden_grad):
    gating = jax.nn.sigmoid(pre_act)
    hidden = (pre_act * gating).astype(BF16)
    act_grad = (hidden_grad * gating * (1.0 + pre_act * (1.0 - gating))).astype(BF16)
    return hidden, act_grad


def gathered_kernel(units, lines, arrived_ref, *refs):
    pieces, (acc_ref, rows_ref, up, down, wide, sems) = refs[:-6], refs[-6:]
    width = up.shape[1]
    half = pieces[0].shape[0] // 2
    experts = arrived_ref.shape[0]
    capacity = rows_ref.shape[0] // experts
    copies = []
    for i, piece in enumerate(pieces):
        for j, whole in enumerate((up, down)):
            copy = pltpu.make_async_copy(
                piece.at[pl.ds(j * half, units)], whole.at[pl.ds(i * units, units)], sems.at[i, j]
            )
            copy.start()
            copies.append(copy)
    for e in range(experts):
        wide[e * lines : (e + 1) * lines, :] = arrived_ref[e, :lines, :].astype(F32)
    blocks = lines // capacity
    for r in range(capacity):
        for b in range(blocks):
            line = wide[pl.ds(r * blocks + b, experts, stride=lines), :]
            rows_ref[r * experts : (r + 1) * experts, b * 128 : (b + 1) * 128] = line.astype(BF16)
    for copy in copies:
        copy.wait()
    tok, cot = rows_ref[:, :width], rows_ref[:, width:]
    hidden, act_grad = activations(matmul_nt(tok, up[...]), matmul_nt(cot, down[...]))
    acc_ref[:, :width] = matmul(hidden, down[...])
    acc_ref[:, width:] = matmul(act_grad, up[...])


def gathered(arrived, pieces, units, slots):
    experts = arrived.shape[0]
    width = pieces[0].shape[1]
    lines = slots * 2 * width // (experts * 128)
    count = len(pieces)
    return pl.pallas_call(
        functools.partial(gathered_kernel, units, lines),
        out_shape=(
            jax.ShapeDtypeStruct((slots, 2 * width), F32),
            jax.ShapeDtypeStruct((slots, 2 * width), BF16),
        ),
        in_specs=[pl.BlockSpec(memory_space=pltpu.VMEM)] + [pl.BlockSpec(memory_space=pl.ANY)] * count,
        out_specs=(pl.BlockSpec(memory_space=pltpu.VMEM), pl.BlockSpec(memory_space=pltpu.VMEM)),
        scratch_shapes=[
            pltpu.VMEM((count * units, width), BF16),
            pltpu.VMEM((count * units, width), BF16),
            pltpu.VMEM((experts * lines, 128), F32),
            pltpu.SemaphoreType.DMA((count, 2)),
        ],
        compiler_params=pltpu.CompilerParams(vmem_limit_bytes=VMEM_LIMIT + (4 << 20)),
        cost_estimate=pl.CostEstimate(
            flops=8 * slots * count * units * width,
            bytes_accessed=4 * count * units * width,
            transcendentals=0,
        ),
        name="gathered",
    )(arrived, *map(outside, pieces))


def last_kernel(units, rows_ref, acc_ref, up_ref, down_ref, out_ref, wide):
    width = up_ref.shape[1]
    experts, lines, _ = out_ref.shape
    capacity = rows_ref.shape[0] // experts
    blocks = lines // capacity
    up, down = up_ref[:units, :], down_ref[:units, :]
    tok, cot = rows_ref[:, :width], rows_ref[:, width:]
    hidden, act_grad = activations(matmul_nt(tok, up), matmul_nt(cot, down))
    for part, (acts, weights) in enumerate(((hidden, down), (act_grad, up))):
        sums = acc_ref[:, part * width : (part + 1) * width] + matmul(acts, weights)
        for b in range(width // 128):
            line = part * (width // 128) + b
            for r in range(capacity):
                wide[pl.ds(r * blocks + line, experts, stride=lines), :] = sums[
                    r * experts : (r + 1) * experts, b * 128 : (b + 1) * 128
                ]
    for e in range(experts):
        out_ref[e] = wide[e * lines : (e + 1) * lines, :].astype(BF16)


def last(rows, acc, up_half, down_half, units, experts):
    lines = rows.shape[0] * rows.shape[1] // (experts * 128)
    return pl.pallas_call(
        functools.partial(last_kernel, units),
        out_shape=jax.ShapeDtypeStruct((experts, lines, 128), BF16),
        scratch_shapes=[pltpu.VMEM((experts * lines, 128), F32)],
        compiler_params=pltpu.CompilerParams(vmem_limit_bytes=VMEM_LIMIT),
        name="last",
    )(rows, acc, up_half, down_half)


def hot_kernel(units, hot_rows, where_ref, pieces_ref, *refs):
    blocks, (send_ref, keep_ref, tok, cot, weights, sems) = refs[:-6], refs[-6:]
    ring = len(blocks)
    width = tok.shape[1]
    here = where_ref[0]
    copies = []
    for i, block in enumerate(blocks):
        place = pl.multiple_of((here ^ lax.rem(here + i, ring)) * HOT_PAD, HOT_PAD)
        pair = block if isinstance(block, tuple) else (block, block)
        offset = 0 if isinstance(block, tuple) else units + HOT_PAD
        for j, whole in enumerate((tok, cot)):
            copy = pltpu.make_async_copy(
                pair[j].at[pl.ds(j * offset + units, HOT_PAD)], whole.at[pl.ds(place, HOT_PAD)], sems.at[i, j]
            )
            copy.start()
            copies.append(copy)
    columns = width // 128
    tall = pieces_ref.shape[1]
    for k in range(pieces_ref.shape[0]):
        i, j = k // columns, k % columns
        weights[i * tall : (i + 1) * tall, j * 128 : (j + 1) * 128] = pieces_ref[k]
    for copy in copies:
        copy.wait()
    up, down = weights[:units, :], weights[units:, :]
    hidden, act_grad = activations(matmul_nt(tok[...], up), matmul_nt(cot[...], down))
    packed = send_ref.shape[0]
    row = lax.broadcasted_iota(I32, (packed, ring * HOT_PAD), 0)
    column = lax.broadcasted_iota(I32, (packed, ring * HOT_PAD), 1)
    group = row // hot_rows
    place = (group % 2) * 4 + (group // 2) * 2
    within = place * HOT_PAD + row % hot_rows
    for odd, out_ref in ((1, send_ref), (0, keep_ref)):
        chosen = (column == within + odd * HOT_PAD).astype(F32).astype(BF16)
        picked_hidden = matmul(chosen, hidden).astype(BF16)
        picked_grad = matmul(chosen, act_grad).astype(BF16)
        out_ref[:, :width] = matmul(picked_hidden, down).astype(BF16)
        out_ref[:, width:] = matmul(picked_grad, up).astype(BF16)


def hot_partials(here, pieces, blocks, units, hot_rows, after):
    ring = len(blocks)
    flat, spans = [], []
    for block in blocks:
        spans.append(len(block) if isinstance(block, tuple) else 0)
        flat += list(block) if isinstance(block, tuple) else [block]
    width = flat[0].shape[1]

    def kernel(where_ref, pieces_ref, after_ref, *refs):
        refs, grouped = list(refs), []
        for span in spans:
            grouped.append(tuple(refs.pop(0) for _ in range(span)) if span else refs.pop(0))
        hot_kernel(units, hot_rows, where_ref, pieces_ref, *grouped, *refs)

    inside = pl.BlockSpec(memory_space=pltpu.VMEM)
    packed = jax.ShapeDtypeStruct((ring // 2 * hot_rows, 2 * width), BF16)
    return pl.pallas_call(
        kernel,
        out_shape=(packed, packed),
        in_specs=[pl.BlockSpec(memory_space=pltpu.SMEM), inside]
        + [pl.BlockSpec(memory_space=pl.ANY)] * (1 + len(flat)),
        out_specs=(inside, inside),
        scratch_shapes=[
            pltpu.VMEM((ring * HOT_PAD, width), BF16),
            pltpu.VMEM((ring * HOT_PAD, width), BF16),
            pltpu.VMEM((2 * units, width), BF16),
            pltpu.SemaphoreType.DMA((ring, 2)),
        ],
        compiler_params=pltpu.CompilerParams(vmem_limit_bytes=VMEM_LIMIT),
        name="hot",
    )(here, pieces, after, *map(outside, flat))


def thirds(x):
    first = x.astype(BF16)
    rest = x - first.astype(F32)
    second = rest.astype(BF16)
    third = (rest - second.astype(F32)).astype(BF16)
    return first, second, third


def cold_kernel(capacity, ids_ref, gate_ref, cot_ref, cold_ref, sum_ref, dots_ref, wide, rows):
    ids, gates, cot = ids_ref[...], gate_ref[...], cot_ref[...]
    top_count = ids.shape[0]
    experts, lines, _ = cold_ref.shape
    blocks = lines // capacity
    width = cot.shape[1]
    for e in range(experts):
        wide[e * lines : (e + 1) * lines, :] = cold_ref[e].astype(F32)
    for r in range(capacity):
        for b in range(blocks):
            line = wide[pl.ds(r * blocks + b, experts, stride=lines), :]
            rows[r * experts : (r + 1) * experts, b * 128 : (b + 1) * 128] = line.astype(BF16)
    cold, _, expert, _, _ = slot_maps(ids, experts * capacity, capacity, slot_major=True)
    per_slot = jnp.zeros(cold.shape, F32)
    for k in range(top_count):
        per_slot = per_slot + jnp.where(ids[k : k + 1, :] == expert, gates[k : k + 1, :], 0.0)
    scale = thirds(jnp.where(cold > 0, per_slot, 0.0))
    for lo in (0, width):
        part = rows[:, lo : lo + width]
        sum_ref[:, lo : lo + width] = matmul_tn(scale[0], part) + matmul_tn(scale[1], part) + matmul_tn(scale[2], part)
    dots = jnp.where(cold > 0, matmul_nt(rows[:, :width], cot), 0.0)
    for k in range(top_count):
        dots_ref[k : k + 1, :] = jnp.sum(jnp.where(ids[k : k + 1, :] == expert, dots, 0.0), 0, keepdims=True)


def cold_combine(ids, gates, cotangent, results, capacity):
    tok_rows, width = cotangent.shape
    experts, lines, _ = results.shape
    return pl.pallas_call(
        functools.partial(cold_kernel, capacity),
        out_shape=(
            jax.ShapeDtypeStruct((tok_rows, 2 * width), F32),
            jax.ShapeDtypeStruct(gates.shape, F32),
        ),
        scratch_shapes=[
            pltpu.VMEM((experts * lines, 128), F32),
            pltpu.VMEM((experts * capacity, 2 * width), BF16),
        ],
        compiler_params=pltpu.CompilerParams(vmem_limit_bytes=VMEM_LIMIT),
        cost_estimate=pl.CostEstimate(flops=1 << 36, bytes_accessed=1 << 26, transcendentals=0),
        name="cold_combine",
    )(ids, gates, cotangent, results)


def final_kernel(
    capacity, slots, ids_ref, gate_ref, cot_ref, sum_ref, dots_ref, kept_ref, *refs
):
    sent, (mix_ref, grad_ref, gate_grad_ref) = refs[:-3], refs[-3:]
    ids, gates, cot = ids_ref[...], gate_ref[...], cot_ref[...]
    top_count, tok_rows = ids.shape
    width = cot.shape[1]
    hot_rows = kept_ref.shape[0]
    _, hot, _, _, hottest = slot_maps(ids, slots, capacity)
    hottest = hottest.astype(I32)
    gate = jnp.zeros((1, tok_rows), F32)
    for k in range(top_count):
        gate = gate + jnp.where(ids[k : k + 1, :] == hottest, gates[k : k + 1, :], 0.0)
    hot = hot[:hot_rows]
    scale = thirds(jnp.where(hot > 0, gate, 0.0))
    result = kept_ref[...]
    for ref in sent:
        result = result + ref[...].astype(F32)
    result = result.astype(BF16)
    for lo, out_ref in ((0, mix_ref), (width, grad_ref)):
        rows = result[:, lo : lo + width]
        total = matmul_tn(scale[0], rows) + matmul_tn(scale[1], rows) + matmul_tn(scale[2], rows)
        out_ref[...] = (sum_ref[:, lo : lo + width] + total).astype(BF16)
    dots = jnp.where(hot > 0, matmul_nt(result[:, :width], cot), 0.0)
    dot = jnp.sum(dots, 0, keepdims=True)
    gate_grad_ref[...] = dots_ref[...] + jnp.where(ids == hottest, dot, 0.0)


def final_combine(ids, gates, cotangent, sums, dots, kept, sent, slots, capacity):
    return pl.pallas_call(
        functools.partial(final_kernel, capacity, slots),
        out_shape=(
            jax.ShapeDtypeStruct(cotangent.shape, BF16),
            jax.ShapeDtypeStruct(cotangent.shape, BF16),
            jax.ShapeDtypeStruct(gates.shape, F32),
        ),
        compiler_params=pltpu.CompilerParams(vmem_limit_bytes=VMEM_LIMIT),
        name="final_combine",
    )(ids, gates, cotangent, sums, dots, kept, *sent)


TICK = pl.CostEstimate(flops=1 << 35, bytes_accessed=1 << 25, transcendentals=0)


def tick_kernel(token_ref, *refs):
    refs[-1][0, 0] = token_ref[0, 0]


def tick(token, *after):
    scalar = pl.BlockSpec(memory_space=pltpu.SMEM)
    return pl.pallas_call(
        tick_kernel,
        out_shape=jax.ShapeDtypeStruct(token.shape, token.dtype),
        in_specs=[scalar] + [pl.BlockSpec(memory_space=pl.ANY)] * len(after),
        out_specs=scalar,
        compiler_params=pltpu.CompilerParams(vmem_limit_bytes=1 << 20),
        cost_estimate=pl.CostEstimate(flops=22 << 30, bytes_accessed=1 << 10, transcendentals=0),
        name="tick",
    )(token, *after)


def split_kernel(right_ref, left_ref, right_out, left_out, top_ref, bottom_ref, sems):
    half = top_ref.shape[0]
    copies = [
        pltpu.make_async_copy(right_ref.at[pl.ds(0, half)], top_ref, sems.at[0]),
        pltpu.make_async_copy(left_ref.at[pl.ds(half, half)], bottom_ref, sems.at[1]),
    ]
    for copy in copies:
        copy.start()
    for copy in copies:
        copy.wait()


def split(right, left):
    anywhere, inside = pl.BlockSpec(memory_space=pl.ANY), pl.BlockSpec(memory_space=pltpu.VMEM)
    whole = jax.ShapeDtypeStruct(right.shape, right.dtype)
    part = jax.ShapeDtypeStruct((right.shape[0] // 2, right.shape[1]), right.dtype)
    return pl.pallas_call(
        split_kernel,
        out_shape=(whole, whole, part, part),
        in_specs=[anywhere] * 2,
        out_specs=(anywhere, anywhere, inside, inside),
        input_output_aliases={0: 0, 1: 1},
        scratch_shapes=[pltpu.SemaphoreType.DMA((2,))],
        compiler_params=pltpu.CompilerParams(vmem_limit_bytes=1 << 22),
        cost_estimate=TICK,
        name="split",
    )(right, left)


def shift(x, by):
    ring = lax.axis_size("dp")
    return lax.ppermute(x, "dp", [(i, (i + by) % ring) for i in range(ring)])


def swap(x, bit):
    ring = lax.axis_size("dp")
    pairs = [[i, i ^ bit] for i in range(ring) if not i & bit]
    both = lax.all_gather(x, "dp", axis=0, axis_index_groups=pairs, tiled=False)
    return jnp.where(lax.axis_index("dp") & bit == 0, both[1], both[0])


def send_on(x, bits):
    ring = lax.axis_size("dp")
    return lax.ppermute(x, "dp", [(i, i ^ bits) for i in range(ring)])


def shards(tokens, cotangent, gate_probs, expert_ids, up_weight, down_weight):
    tok_rows, width = tokens.shape
    top_count = expert_ids.shape[1]
    experts = lax.axis_size("expert")
    hot_rows = 9 * tok_rows // 16
    capacity = (tok_rows * top_count - hot_rows + experts - 2) // (experts - 1)
    slots = experts * capacity
    up, down = up_weight[0], down_weight[0]
    units = up.shape[0]
    ids, gates = expert_ids.T, gate_probs.T

    outgoing, own, hottest = route(ids, tokens, cotangent, up, down, slots, capacity)
    half = own.shape[0] // 2
    right, left = [own], [own]
    for step in range(3):
        r, l = shift(right[-1], 1), shift(left[-1], -1)
        if step == 1:
            token = tick(hottest, r, l)
        if step == 2:
            r, l, top, bottom = split(r, l)
        right.append(r)
        left.append(l)
    far_up, far_down = shift(top, 1), shift(bottom, -1)

    lines = capacity * 2 * width // 128
    outgoing = assemble(outgoing.reshape(experts, lines, 128), up, down)
    arrived = lax.all_to_all(outgoing, "expert", 0, 0, tiled=True)
    hot_pieces = lax.all_to_all(repeat(token, arrived, lines), "expert", 0, 0, tiled=True)

    acc, rows = gathered(arrived, [own] + right[1:] + left[1:], units, slots)
    results = last(rows, acc, far_up, far_down, units, experts)
    came_back = lax.all_to_all(results, "expert", 0, 0, tiled=True)

    blocks = left + [(far_up, far_down)] + right[:0:-1]
    here = lax.axis_index("dp").astype(I32).reshape(1)
    send, keep = hot_partials(here, hot_pieces, blocks, units, hot_rows, results)
    both = keep.astype(F32) + swap(send, 1).astype(F32)
    kept = both[:hot_rows]
    sent = [
        send_on(both[i * hot_rows : (i + 1) * hot_rows].astype(BF16), place) for i, place in ((1, 4), (2, 2), (3, 6))
    ]
    sums, dots = cold_combine(ids, gates, cotangent, came_back, capacity)
    mixture, input_grad, gate_grad = final_combine(
        ids, gates, cotangent, sums, dots, kept, sent, slots, capacity
    )
    return mixture, input_grad, gate_grad.T


def solution(mesh):
    rows = P(("dp", "expert"), None)
    weights = P("expert", "dp", None)
    return jax.shard_map(
        shards,
        mesh=mesh,
        in_specs=(rows, rows, rows, rows, weights, weights),
        out_specs=(rows, rows, rows),
        check_vma=False,
    )
```

```python
import functools

import jax
import jax.numpy as jnp
from jax import lax
from jax.experimental import pallas as pl
from jax.experimental.pallas import tpu as pltpu
from jax.sharding import PartitionSpec as P

BF16, F32, I32 = jnp.bfloat16, jnp.float32, jnp.int32
HOT_PAD = 16
VMEM_LIMIT = 16 * 1024 * 1024


def outside(x):
    return pltpu.with_memory_space_constraint(x, pltpu.HBM)


def matmul(a, b):
    return lax.dot_general(a, b, (((1,), (0,)), ((), ())), preferred_element_type=F32)


def matmul_nt(a, b):
    return lax.dot_general(a, b, (((1,), (1,)), ((), ())), preferred_element_type=F32)


def matmul_tn(a, b):
    return lax.dot_general(a, b, (((0,), (0,)), ((), ())), preferred_element_type=F32)


def slot_maps(ids, slots, capacity, slot_major=False):
    top_count, tok_rows = ids.shape
    slot = lax.broadcasted_iota(I32, (slots, tok_rows), 0)
    experts = slots // capacity
    expert, within = (slot % experts, slot // experts) if slot_major else (slot // capacity, slot % capacity)
    named = jnp.zeros((slots, tok_rows), F32)
    for k in range(top_count):
        named = named + (ids[k : k + 1, :] == expert).astype(F32)
    counts = jnp.sum(named, 1, keepdims=True)
    is_hot = (counts == jnp.max(counts)).astype(F32)
    earlier = (
        lax.broadcasted_iota(I32, (tok_rows, tok_rows), 0)
        < lax.broadcasted_iota(I32, (tok_rows, tok_rows), 1)
    ).astype(BF16)
    rank = matmul(named.astype(BF16), earlier)
    cold = named * (1.0 - is_hot) * (rank == within.astype(F32)).astype(F32)
    first = is_hot * (within[:, :1] == 0).astype(F32)
    hot_token = jnp.sum(named * first, 0, keepdims=True)
    hot_rank = jnp.sum(rank * first, 0, keepdims=True)
    hot_row = lax.broadcasted_iota(I32, (HOT_PAD, tok_rows), 0).astype(F32)
    hot = hot_token * (hot_rank == hot_row).astype(F32)
    hottest = jnp.sum(first * expert[:, :1].astype(F32), 0, keepdims=True)
    return cold, hot, expert, is_hot, hottest


def route_kernel(
    capacity, ids_hbm, tok_ref, cot_ref, up_ref, down_ref, out_ref, own_ref, hottest_ref, ids_ref, tok, cot, sems
):
    slots, width = out_ref.shape[0], tok.shape[1]
    units = up_ref.shape[0]
    half = own_ref.shape[0] // 2
    loads = [pltpu.make_async_copy(tok_ref, tok, sems.at[0]), pltpu.make_async_copy(cot_ref, cot, sems.at[1])]
    copies = [
        pltpu.make_async_copy(up_ref, own_ref.at[pl.ds(0, units)], sems.at[2]),
        pltpu.make_async_copy(down_ref, own_ref.at[pl.ds(half, units)], sems.at[3]),
    ]
    first = pltpu.make_async_copy(ids_hbm, ids_ref, sems.at[4])
    for copy in [first] + loads + copies:
        copy.start()
    first.wait()
    cold, hot, _, _, hottest = slot_maps(ids_ref[...], slots, capacity)
    cold, hot = cold.astype(BF16), hot.astype(BF16)
    hottest_ref[0, 0] = jnp.max(hottest).astype(I32)
    for copy in loads:
        copy.wait()
    own_ref[units:half, :] = matmul(hot, tok[...]).astype(BF16)
    own_ref[half + units :, :] = matmul(hot, cot[...]).astype(BF16)
    out_ref[:, :width] = matmul(cold, tok[...]).astype(BF16)
    out_ref[:, width:] = matmul(cold, cot[...]).astype(BF16)
    for copy in copies:
        copy.wait()


def route(ids, tokens, cotangent, up, down, slots, capacity):
    tok_rows, width = tokens.shape
    units = up.shape[0]
    anywhere = pl.BlockSpec(memory_space=pl.ANY)
    inside = pl.BlockSpec(memory_space=pltpu.VMEM)
    return pl.pallas_call(
        functools.partial(route_kernel, capacity),
        out_shape=(
            jax.ShapeDtypeStruct((slots, 2 * width), BF16),
            jax.ShapeDtypeStruct((2 * (units + HOT_PAD), width), BF16),
            jax.ShapeDtypeStruct((1, 1), I32),
        ),
        in_specs=[anywhere] * 5,
        out_specs=(inside, inside, pl.BlockSpec(memory_space=pltpu.SMEM)),
        scratch_shapes=[
            pltpu.VMEM(ids.shape, I32),
            pltpu.VMEM((tok_rows, width), BF16),
            pltpu.VMEM((tok_rows, width), BF16),
            pltpu.SemaphoreType.DMA((5,)),
        ],
        compiler_params=pltpu.CompilerParams(vmem_limit_bytes=VMEM_LIMIT),
        name="route",
    )(*map(outside, (ids, tokens, cotangent, up, down)))


def assemble_kernel(tall, rows_ref, up_ref, down_ref, out_ref, up, down, sems):
    copies = []
    for i, (source, here) in enumerate(((up_ref, up), (down_ref, down))):
        copy = pltpu.make_async_copy(source, here, sems.at[i])
        copy.start()
        copies.append(copy)
    lines = rows_ref.shape[1]
    out_ref[:, :lines, :] = rows_ref[...]
    columns = up.shape[1] // 128
    groups = up.shape[0] // tall
    for i, here in enumerate((up, down)):
        copies[i].wait()
        for g in range(groups):
            for j in range(columns):
                out_ref[(i * groups + g) * columns + j, lines:, :] = here[
                    g * tall : (g + 1) * tall, j * 128 : (j + 1) * 128
                ]


def assemble(rows, up, down):
    experts, lines, lanes = rows.shape
    units, width = up.shape
    tall = 2 * units * width // (experts * lanes)
    return pl.pallas_call(
        functools.partial(assemble_kernel, tall),
        out_shape=jax.ShapeDtypeStruct((experts, lines + tall, lanes), BF16),
        in_specs=[pl.BlockSpec(memory_space=pltpu.VMEM)] + [pl.BlockSpec(memory_space=pl.ANY)] * 2,
        out_specs=pl.BlockSpec(memory_space=pltpu.VMEM),
        scratch_shapes=[
            pltpu.VMEM((units, width), BF16),
            pltpu.VMEM((units, width), BF16),
            pltpu.SemaphoreType.DMA((2,)),
        ],
        compiler_params=pltpu.CompilerParams(vmem_limit_bytes=VMEM_LIMIT),
        name="assemble",
    )(rows, outside(up), outside(down))


def repeat_kernel(lines, hottest_ref, arrived_ref, out_ref):
    mine = arrived_ref[hottest_ref[0, 0], lines:, :]
    out_ref[...] = jnp.broadcast_to(mine[None], out_ref.shape)


def repeat(hottest, arrived, lines):
    experts, height, lanes = arrived.shape
    inside = pl.BlockSpec(memory_space=pltpu.VMEM)
    return pl.pallas_call(
        functools.partial(repeat_kernel, lines),
        out_shape=jax.ShapeDtypeStruct((experts, height - lines, lanes), BF16),
        in_specs=[pl.BlockSpec(memory_space=pltpu.SMEM), inside],
        out_specs=inside,
        compiler_params=pltpu.CompilerParams(vmem_limit_bytes=VMEM_LIMIT),
        name="repeat",
    )(hottest, arrived)


def activations(pre_act, hidden_grad):
    gating = jax.nn.sigmoid(pre_act)
    hidden = (pre_act * gating).astype(BF16)
    act_grad = (hidden_grad * gating * (1.0 + pre_act * (1.0 - gating))).astype(BF16)
    return hidden, act_grad


def gathered_kernel(units, lines, arrived_ref, *refs):
    pieces, (acc_ref, rows_ref, up, down, wide, sems) = refs[:-6], refs[-6:]
    width = up.shape[1]
    half = pieces[0].shape[0] // 2
    experts = arrived_ref.shape[0]
    capacity = rows_ref.shape[0] // experts
    copies = []
    for i, piece in enumerate(pieces):
        for j, whole in enumerate((up, down)):
            copy = pltpu.make_async_copy(
                piece.at[pl.ds(j * half, units)], whole.at[pl.ds(i * units, units)], sems.at[i, j]
            )
            copy.start()
            copies.append(copy)
    for e in range(experts):
        wide[e * lines : (e + 1) * lines, :] = arrived_ref[e, :lines, :].astype(F32)
    blocks = lines // capacity
    for r in range(capacity):
        for b in range(blocks):
            line = wide[pl.ds(r * blocks + b, experts, stride=lines), :]
            rows_ref[r * experts : (r + 1) * experts, b * 128 : (b + 1) * 128] = line.astype(BF16)
    for copy in copies:
        copy.wait()
    tok, cot = rows_ref[:, :width], rows_ref[:, width:]
    hidden, act_grad = activations(matmul_nt(tok, up[...]), matmul_nt(cot, down[...]))
    acc_ref[:, :width] = matmul(hidden, down[...])
    acc_ref[:, width:] = matmul(act_grad, up[...])


def gathered(arrived, pieces, units, slots):
    experts = arrived.shape[0]
    width = pieces[0].shape[1]
    lines = slots * 2 * width // (experts * 128)
    count = len(pieces)
    return pl.pallas_call(
        functools.partial(gathered_kernel, units, lines),
        out_shape=(
            jax.ShapeDtypeStruct((slots, 2 * width), F32),
            jax.ShapeDtypeStruct((slots, 2 * width), BF16),
        ),
        in_specs=[pl.BlockSpec(memory_space=pltpu.VMEM)] + [pl.BlockSpec(memory_space=pl.ANY)] * count,
        out_specs=(pl.BlockSpec(memory_space=pltpu.VMEM), pl.BlockSpec(memory_space=pltpu.VMEM)),
        scratch_shapes=[
            pltpu.VMEM((count * units, width), BF16),
            pltpu.VMEM((count * units, width), BF16),
            pltpu.VMEM((experts * lines, 128), F32),
            pltpu.SemaphoreType.DMA((count, 2)),
        ],
        compiler_params=pltpu.CompilerParams(vmem_limit_bytes=VMEM_LIMIT + (4 << 20)),
        cost_estimate=pl.CostEstimate(
            flops=8 * slots * count * units * width,
            bytes_accessed=4 * count * units * width,
            transcendentals=0,
        ),
        name="gathered",
    )(arrived, *map(outside, pieces))


def last_kernel(units, rows_ref, acc_ref, up_ref, down_ref, out_ref, wide):
    width = up_ref.shape[1]
    experts, lines, _ = out_ref.shape
    capacity = rows_ref.shape[0] // experts
    blocks = lines // capacity
    up, down = up_ref[:units, :], down_ref[:units, :]
    tok, cot = rows_ref[:, :width], rows_ref[:, width:]
    hidden, act_grad = activations(matmul_nt(tok, up), matmul_nt(cot, down))
    for part, (acts, weights) in enumerate(((hidden, down), (act_grad, up))):
        sums = acc_ref[:, part * width : (part + 1) * width] + matmul(acts, weights)
        for b in range(width // 128):
            line = part * (width // 128) + b
            for r in range(capacity):
                wide[pl.ds(r * blocks + line, experts, stride=lines), :] = sums[
                    r * experts : (r + 1) * experts, b * 128 : (b + 1) * 128
                ]
    for e in range(experts):
        out_ref[e] = wide[e * lines : (e + 1) * lines, :].astype(BF16)


def last(rows, acc, up_half, down_half, units, experts):
    lines = rows.shape[0] * rows.shape[1] // (experts * 128)
    return pl.pallas_call(
        functools.partial(last_kernel, units),
        out_shape=jax.ShapeDtypeStruct((experts, lines, 128), BF16),
        scratch_shapes=[pltpu.VMEM((experts * lines, 128), F32)],
        compiler_params=pltpu.CompilerParams(vmem_limit_bytes=VMEM_LIMIT),
        name="last",
    )(rows, acc, up_half, down_half)


def hot_kernel(units, hot_rows, where_ref, pieces_ref, *refs):
    blocks, out_refs, (tok, cot, weights, sems) = refs[:-8], refs[-8:-4], refs[-4:]
    ring = len(blocks)
    width = tok.shape[1]
    here = where_ref[0]
    copies = []
    for i, block in enumerate(blocks):
        place = pl.multiple_of((here ^ lax.rem(here + i, ring)) * HOT_PAD, HOT_PAD)
        pair = block if isinstance(block, tuple) else (block, block)
        offset = 0 if isinstance(block, tuple) else units + HOT_PAD
        for j, whole in enumerate((tok, cot)):
            copy = pltpu.make_async_copy(
                pair[j].at[pl.ds(j * offset + units, HOT_PAD)], whole.at[pl.ds(place, HOT_PAD)], sems.at[i, j]
            )
            copy.start()
            copies.append(copy)
    columns = width // 128
    tall = pieces_ref.shape[1]
    for k in range(pieces_ref.shape[0]):
        i, j = k // columns, k % columns
        weights[i * tall : (i + 1) * tall, j * 128 : (j + 1) * 128] = pieces_ref[k]
    for copy in copies:
        copy.wait()
    up, down = weights[:units, :], weights[units:, :]
    hidden, act_grad = activations(matmul_nt(tok[...], up), matmul_nt(cot[...], down))
    groups, stride = len(out_refs), 24
    row = lax.broadcasted_iota(I32, (groups * stride, ring * HOT_PAD), 0)
    column = lax.broadcasted_iota(I32, (groups * stride, ring * HOT_PAD), 1)
    group, within = row // stride, row % stride
    place = (group % 2) * 4 + (group // 2) * 2 + within // hot_rows
    chosen = (column == place * HOT_PAD + within % hot_rows) & (within < 2 * hot_rows)
    chosen = chosen.astype(F32).astype(BF16)
    picked_hidden = matmul(chosen, hidden).astype(BF16)
    picked_grad = matmul(chosen, act_grad).astype(BF16)
    for lo, sums in ((0, matmul(picked_hidden, down)), (width, matmul(picked_grad, up))):
        for g, out_ref in enumerate(out_refs):
            out_ref[:, lo : lo + width] = sums[g * stride : g * stride + 2 * hot_rows].astype(BF16)


def hot_partials(here, pieces, blocks, units, hot_rows, after):
    ring = len(blocks)
    flat, spans = [], []
    for block in blocks:
        spans.append(len(block) if isinstance(block, tuple) else 0)
        flat += list(block) if isinstance(block, tuple) else [block]
    width = flat[0].shape[1]

    def kernel(where_ref, pieces_ref, after_ref, *refs):
        refs, grouped = list(refs), []
        for span in spans:
            grouped.append(tuple(refs.pop(0) for _ in range(span)) if span else refs.pop(0))
        hot_kernel(units, hot_rows, where_ref, pieces_ref, *grouped, *refs)

    inside = pl.BlockSpec(memory_space=pltpu.VMEM)
    packed = jax.ShapeDtypeStruct((2 * hot_rows, 2 * width), BF16)
    return pl.pallas_call(
        kernel,
        out_shape=(packed,) * 4,
        in_specs=[pl.BlockSpec(memory_space=pltpu.SMEM), inside]
        + [pl.BlockSpec(memory_space=pl.ANY)] * (1 + len(flat)),
        out_specs=(inside,) * 4,
        scratch_shapes=[
            pltpu.VMEM((ring * HOT_PAD, width), BF16),
            pltpu.VMEM((ring * HOT_PAD, width), BF16),
            pltpu.VMEM((2 * units, width), BF16),
            pltpu.SemaphoreType.DMA((ring, 2)),
        ],
        compiler_params=pltpu.CompilerParams(vmem_limit_bytes=VMEM_LIMIT),
        name="hot",
    )(here, pieces, after, *map(outside, flat))


def thirds(x):
    first = x.astype(BF16)
    rest = x - first.astype(F32)
    second = rest.astype(BF16)
    third = (rest - second.astype(F32)).astype(BF16)
    return first, second, third


def cold_kernel(capacity, ids_ref, gate_ref, cot_ref, cold_ref, sum_ref, dots_ref, wide, rows):
    ids, gates, cot = ids_ref[...], gate_ref[...], cot_ref[...]
    top_count = ids.shape[0]
    experts, lines, _ = cold_ref.shape
    blocks = lines // capacity
    width = cot.shape[1]
    for e in range(experts):
        wide[e * lines : (e + 1) * lines, :] = cold_ref[e].astype(F32)
    for r in range(capacity):
        for b in range(blocks):
            line = wide[pl.ds(r * blocks + b, experts, stride=lines), :]
            rows[r * experts : (r + 1) * experts, b * 128 : (b + 1) * 128] = line.astype(BF16)
    cold, _, expert, _, _ = slot_maps(ids, experts * capacity, capacity, slot_major=True)
    per_slot = jnp.zeros(cold.shape, F32)
    for k in range(top_count):
        per_slot = per_slot + jnp.where(ids[k : k + 1, :] == expert, gates[k : k + 1, :], 0.0)
    scale = thirds(jnp.where(cold > 0, per_slot, 0.0))
    for lo in (0, width):
        part = rows[:, lo : lo + width]
        sum_ref[:, lo : lo + width] = matmul_tn(scale[0], part) + matmul_tn(scale[1], part) + matmul_tn(scale[2], part)
    dots = jnp.where(cold > 0, matmul_nt(rows[:, :width], cot), 0.0)
    for k in range(top_count):
        dots_ref[k : k + 1, :] = jnp.sum(jnp.where(ids[k : k + 1, :] == expert, dots, 0.0), 0, keepdims=True)


def cold_combine(ids, gates, cotangent, results, capacity):
    tok_rows, width = cotangent.shape
    experts, lines, _ = results.shape
    return pl.pallas_call(
        functools.partial(cold_kernel, capacity),
        out_shape=(
            jax.ShapeDtypeStruct((tok_rows, 2 * width), F32),
            jax.ShapeDtypeStruct(gates.shape, F32),
        ),
        scratch_shapes=[
            pltpu.VMEM((experts * lines, 128), F32),
            pltpu.VMEM((experts * capacity, 2 * width), BF16),
        ],
        compiler_params=pltpu.CompilerParams(vmem_limit_bytes=VMEM_LIMIT),
        cost_estimate=pl.CostEstimate(flops=1 << 36, bytes_accessed=1 << 26, transcendentals=0),
        name="cold_combine",
    )(ids, gates, cotangent, results)


def final_kernel(
    capacity, slots, ids_ref, gate_ref, cot_ref, sum_ref, dots_ref, kept_ref, *refs
):
    sent, (mix_ref, grad_ref, gate_grad_ref) = refs[:-3], refs[-3:]
    ids, gates, cot = ids_ref[...], gate_ref[...], cot_ref[...]
    top_count, tok_rows = ids.shape
    width = cot.shape[1]
    hot_rows = kept_ref.shape[0]
    _, hot, _, _, hottest = slot_maps(ids, slots, capacity)
    hottest = hottest.astype(I32)
    gate = jnp.zeros((1, tok_rows), F32)
    for k in range(top_count):
        gate = gate + jnp.where(ids[k : k + 1, :] == hottest, gates[k : k + 1, :], 0.0)
    hot = hot[:hot_rows]
    scale = thirds(jnp.where(hot > 0, gate, 0.0))
    result = kept_ref[...]
    for ref in sent:
        result = result + ref[...].astype(F32)
    result = result.astype(BF16)
    for lo, out_ref in ((0, mix_ref), (width, grad_ref)):
        rows = result[:, lo : lo + width]
        total = matmul_tn(scale[0], rows) + matmul_tn(scale[1], rows) + matmul_tn(scale[2], rows)
        out_ref[...] = (sum_ref[:, lo : lo + width] + total).astype(BF16)
    dots = jnp.where(hot > 0, matmul_nt(result[:, :width], cot), 0.0)
    dot = jnp.sum(dots, 0, keepdims=True)
    gate_grad_ref[...] = dots_ref[...] + jnp.where(ids == hottest, dot, 0.0)


def final_combine(ids, gates, cotangent, sums, dots, kept, sent, slots, capacity):
    return pl.pallas_call(
        functools.partial(final_kernel, capacity, slots),
        out_shape=(
            jax.ShapeDtypeStruct(cotangent.shape, BF16),
            jax.ShapeDtypeStruct(cotangent.shape, BF16),
            jax.ShapeDtypeStruct(gates.shape, F32),
        ),
        compiler_params=pltpu.CompilerParams(vmem_limit_bytes=VMEM_LIMIT),
        name="final_combine",
    )(ids, gates, cotangent, sums, dots, kept, *sent)


TICK = pl.CostEstimate(flops=1 << 35, bytes_accessed=1 << 25, transcendentals=0)


def tick_kernel(token_ref, *refs):
    refs[-1][0, 0] = token_ref[0, 0]


def tick(token, *after):
    scalar = pl.BlockSpec(memory_space=pltpu.SMEM)
    return pl.pallas_call(
        tick_kernel,
        out_shape=jax.ShapeDtypeStruct(token.shape, token.dtype),
        in_specs=[scalar] + [pl.BlockSpec(memory_space=pl.ANY)] * len(after),
        out_specs=scalar,
        compiler_params=pltpu.CompilerParams(vmem_limit_bytes=1 << 20),
        cost_estimate=pl.CostEstimate(flops=22 << 30, bytes_accessed=1 << 10, transcendentals=0),
        name="tick",
    )(token, *after)


def split_kernel(right_ref, left_ref, right_out, left_out, top_ref, bottom_ref, sems):
    half = top_ref.shape[0]
    copies = [
        pltpu.make_async_copy(right_ref.at[pl.ds(0, half)], top_ref, sems.at[0]),
        pltpu.make_async_copy(left_ref.at[pl.ds(half, half)], bottom_ref, sems.at[1]),
    ]
    for copy in copies:
        copy.start()
    for copy in copies:
        copy.wait()


def split(right, left):
    anywhere, inside = pl.BlockSpec(memory_space=pl.ANY), pl.BlockSpec(memory_space=pltpu.VMEM)
    whole = jax.ShapeDtypeStruct(right.shape, right.dtype)
    part = jax.ShapeDtypeStruct((right.shape[0] // 2, right.shape[1]), right.dtype)
    return pl.pallas_call(
        split_kernel,
        out_shape=(whole, whole, part, part),
        in_specs=[anywhere] * 2,
        out_specs=(anywhere, anywhere, inside, inside),
        input_output_aliases={0: 0, 1: 1},
        scratch_shapes=[pltpu.SemaphoreType.DMA((2,))],
        compiler_params=pltpu.CompilerParams(vmem_limit_bytes=1 << 22),
        cost_estimate=TICK,
        name="split",
    )(right, left)


def shift(x, by):
    ring = lax.axis_size("dp")
    return lax.ppermute(x, "dp", [(i, (i + by) % ring) for i in range(ring)])


def send_on(x, bits):
    ring = lax.axis_size("dp")
    return lax.ppermute(x, "dp", [(i, i ^ bits) for i in range(ring)])


def shards(tokens, cotangent, gate_probs, expert_ids, up_weight, down_weight):
    tok_rows, width = tokens.shape
    top_count = expert_ids.shape[1]
    experts = lax.axis_size("expert")
    hot_rows = 9 * tok_rows // 16
    capacity = (tok_rows * top_count - hot_rows + experts - 2) // (experts - 1)
    slots = experts * capacity
    up, down = up_weight[0], down_weight[0]
    units = up.shape[0]
    ids, gates = expert_ids.T, gate_probs.T

    outgoing, own, hottest = route(ids, tokens, cotangent, up, down, slots, capacity)
    half = own.shape[0] // 2
    right, left = [own], [own]
    for step in range(3):
        r, l = shift(right[-1], 1), shift(left[-1], -1)
        if step == 1:
            token = tick(hottest, r, l)
        if step == 2:
            r, l, top, bottom = split(r, l)
        right.append(r)
        left.append(l)
    far_up, far_down = shift(top, 1), shift(bottom, -1)

    lines = capacity * 2 * width // 128
    outgoing = assemble(outgoing.reshape(experts, lines, 128), up, down)
    arrived = lax.all_to_all(outgoing, "expert", 0, 0, tiled=True)
    hot_pieces = lax.all_to_all(repeat(token, arrived, lines), "expert", 0, 0, tiled=True)

    acc, rows = gathered(arrived, [own] + right[1:] + left[1:], units, slots)
    results = last(rows, acc, far_up, far_down, units, experts)
    came_back = lax.all_to_all(results, "expert", 0, 0, tiled=True)

    blocks = left + [(far_up, far_down)] + right[:0:-1]
    here = lax.axis_index("dp").astype(I32).reshape(1)
    keep, *sends = hot_partials(here, hot_pieces, blocks, units, hot_rows, results)
    both = keep.astype(F32)
    for send, place in zip(sends, (4, 2, 6)):
        both = both + send_on(send, place).astype(F32)
    kept = both[:hot_rows]
    sent = [send_on(both[hot_rows:].astype(BF16), 1)]
    sums, dots = cold_combine(ids, gates, cotangent, came_back, capacity)
    mixture, input_grad, gate_grad = final_combine(
        ids, gates, cotangent, sums, dots, kept, sent, slots, capacity
    )
    return mixture, input_grad, gate_grad.T


def solution(mesh):
    rows = P(("dp", "expert"), None)
    weights = P("expert", "dp", None)
    return jax.shard_map(
        shards,
        mesh=mesh,
        in_specs=(rows, rows, rows, rows, weights, weights),
        out_specs=(rows, rows, rows),
        check_vma=False,
    )
```

```python
import functools

import jax
import jax.numpy as jnp
from jax import lax
from jax.experimental import pallas as pl
from jax.experimental.pallas import tpu as pltpu
from jax.sharding import PartitionSpec as P

BF16, F32, I32 = jnp.bfloat16, jnp.float32, jnp.int32
HOT_PAD = 16
VMEM_LIMIT = 16 * 1024 * 1024


def outside(x):
    return pltpu.with_memory_space_constraint(x, pltpu.HBM)


def matmul(a, b):
    return lax.dot_general(a, b, (((1,), (0,)), ((), ())), preferred_element_type=F32)


def matmul_nt(a, b):
    return lax.dot_general(a, b, (((1,), (1,)), ((), ())), preferred_element_type=F32)


def matmul_tn(a, b):
    return lax.dot_general(a, b, (((0,), (0,)), ((), ())), preferred_element_type=F32)


def slot_maps(ids, slots, capacity, slot_major=False):
    top_count, tok_rows = ids.shape
    slot = lax.broadcasted_iota(I32, (slots, tok_rows), 0)
    experts = slots // capacity
    expert, within = (slot % experts, slot // experts) if slot_major else (slot // capacity, slot % capacity)
    named = jnp.zeros((slots, tok_rows), F32)
    for k in range(top_count):
        named = named + (ids[k : k + 1, :] == expert).astype(F32)
    counts = jnp.sum(named, 1, keepdims=True)
    is_hot = (counts == jnp.max(counts)).astype(F32)
    earlier = (
        lax.broadcasted_iota(I32, (tok_rows, tok_rows), 0)
        < lax.broadcasted_iota(I32, (tok_rows, tok_rows), 1)
    ).astype(BF16)
    rank = matmul(named.astype(BF16), earlier)
    cold = named * (1.0 - is_hot) * (rank == within.astype(F32)).astype(F32)
    first = is_hot * (within[:, :1] == 0).astype(F32)
    hot_token = jnp.sum(named * first, 0, keepdims=True)
    hot_rank = jnp.sum(rank * first, 0, keepdims=True)
    hot_row = lax.broadcasted_iota(I32, (HOT_PAD, tok_rows), 0).astype(F32)
    hot = hot_token * (hot_rank == hot_row).astype(F32)
    hottest = jnp.sum(first * expert[:, :1].astype(F32), 0, keepdims=True)
    return cold, hot, expert, is_hot, hottest


def route_kernel(
    capacity, ids_ref, tok_ref, cot_ref, up_ref, down_ref, out_ref, own_up_ref, own_down_ref, hottest_ref, tok, cot, sems
):
    slots, width = out_ref.shape[0], tok.shape[1]
    units = up_ref.shape[0]
    loads = [pltpu.make_async_copy(tok_ref, tok, sems.at[0]), pltpu.make_async_copy(cot_ref, cot, sems.at[1])]
    copies = [
        pltpu.make_async_copy(up_ref, own_up_ref.at[pl.ds(0, units)], sems.at[2]),
        pltpu.make_async_copy(down_ref, own_down_ref.at[pl.ds(0, units)], sems.at[3]),
    ]
    for copy in loads + copies:
        copy.start()
    cold, hot, _, _, hottest = slot_maps(ids_ref[...], slots, capacity)
    cold, hot = cold.astype(BF16), hot.astype(BF16)
    hottest_ref[0, 0] = jnp.max(hottest).astype(I32)
    for copy in loads:
        copy.wait()
    own_up_ref[units:, :] = matmul(hot, tok[...]).astype(BF16)
    own_down_ref[units:, :] = matmul(hot, cot[...]).astype(BF16)
    out_ref[:, :width] = matmul(cold, tok[...]).astype(BF16)
    out_ref[:, width:] = matmul(cold, cot[...]).astype(BF16)
    for copy in copies:
        copy.wait()


def route(ids, tokens, cotangent, up, down, slots, capacity):
    tok_rows, width = tokens.shape
    units = up.shape[0]
    anywhere = pl.BlockSpec(memory_space=pl.ANY)
    inside = pl.BlockSpec(memory_space=pltpu.VMEM)
    return pl.pallas_call(
        functools.partial(route_kernel, capacity),
        out_shape=(
            jax.ShapeDtypeStruct((slots, 2 * width), BF16),
            jax.ShapeDtypeStruct((units + HOT_PAD, width), BF16),
            jax.ShapeDtypeStruct((units + HOT_PAD, width), BF16),
            jax.ShapeDtypeStruct((1, 1), I32),
        ),
        in_specs=[inside] + [anywhere] * 4,
        out_specs=(inside, inside, inside, pl.BlockSpec(memory_space=pltpu.SMEM)),
        scratch_shapes=[
            pltpu.VMEM((tok_rows, width), BF16),
            pltpu.VMEM((tok_rows, width), BF16),
            pltpu.SemaphoreType.DMA((4,)),
        ],
        compiler_params=pltpu.CompilerParams(vmem_limit_bytes=VMEM_LIMIT),
        name="route",
    )(ids, *map(outside, (tokens, cotangent, up, down)))


def assemble_kernel(tall, rows_ref, up_ref, down_ref, out_ref, up, down, sems):
    copies = []
    for i, (source, here) in enumerate(((up_ref, up), (down_ref, down))):
        copy = pltpu.make_async_copy(source, here, sems.at[i])
        copy.start()
        copies.append(copy)
    lines = rows_ref.shape[1]
    out_ref[:, :lines, :] = rows_ref[...]
    columns = up.shape[1] // 128
    groups = up.shape[0] // tall
    for i, here in enumerate((up, down)):
        copies[i].wait()
        for g in range(groups):
            for j in range(columns):
                out_ref[(i * groups + g) * columns + j, lines:, :] = here[
                    g * tall : (g + 1) * tall, j * 128 : (j + 1) * 128
                ]


def assemble(rows, up, down):
    experts, lines, lanes = rows.shape
    units, width = up.shape
    tall = 2 * units * width // (experts * lanes)
    return pl.pallas_call(
        functools.partial(assemble_kernel, tall),
        out_shape=jax.ShapeDtypeStruct((experts, lines + tall, lanes), BF16),
        in_specs=[pl.BlockSpec(memory_space=pltpu.VMEM)] + [pl.BlockSpec(memory_space=pl.ANY)] * 2,
        out_specs=pl.BlockSpec(memory_space=pltpu.VMEM),
        scratch_shapes=[
            pltpu.VMEM((units, width), BF16),
            pltpu.VMEM((units, width), BF16),
            pltpu.SemaphoreType.DMA((2,)),
        ],
        compiler_params=pltpu.CompilerParams(vmem_limit_bytes=VMEM_LIMIT),
        name="assemble",
    )(rows, outside(up), outside(down))


def repeat_kernel(lines, hottest_ref, arrived_ref, out_ref):
    mine = arrived_ref[hottest_ref[0, 0], lines:, :]
    out_ref[...] = jnp.broadcast_to(mine[None], out_ref.shape)


def repeat(hottest, arrived, lines):
    experts, height, lanes = arrived.shape
    inside = pl.BlockSpec(memory_space=pltpu.VMEM)
    return pl.pallas_call(
        functools.partial(repeat_kernel, lines),
        out_shape=jax.ShapeDtypeStruct((experts, height - lines, lanes), BF16),
        in_specs=[pl.BlockSpec(memory_space=pltpu.SMEM), inside],
        out_specs=inside,
        compiler_params=pltpu.CompilerParams(vmem_limit_bytes=VMEM_LIMIT),
        name="repeat",
    )(hottest, arrived)


def activations(pre_act, hidden_grad):
    gating = jax.nn.sigmoid(pre_act)
    hidden = (pre_act * gating).astype(BF16)
    act_grad = (hidden_grad * gating * (1.0 + pre_act * (1.0 - gating))).astype(BF16)
    return hidden, act_grad


def gathered_kernel(units, lines, arrived_ref, *refs):
    pieces, (acc_ref, rows_ref, up, down, wide, sems) = refs[:-6], refs[-6:]
    width = up.shape[1]
    experts = arrived_ref.shape[0]
    capacity = rows_ref.shape[0] // experts
    copies = []
    for i in range(len(pieces) // 2):
        for j, whole in enumerate((up, down)):
            copy = pltpu.make_async_copy(
                pieces[2 * i + j].at[pl.ds(0, units)], whole.at[pl.ds(i * units, units)], sems.at[i, j]
            )
            copy.start()
            copies.append(copy)
    for e in range(experts):
        wide[e * lines : (e + 1) * lines, :] = arrived_ref[e, :lines, :].astype(F32)
    blocks = lines // capacity
    for r in range(capacity):
        for b in range(blocks):
            line = wide[pl.ds(r * blocks + b, experts, stride=lines), :]
            rows_ref[r * experts : (r + 1) * experts, b * 128 : (b + 1) * 128] = line.astype(BF16)
    for copy in copies:
        copy.wait()
    tok, cot = rows_ref[:, :width], rows_ref[:, width:]
    hidden, act_grad = activations(matmul_nt(tok, up[...]), matmul_nt(cot, down[...]))
    acc_ref[:, :width] = matmul(hidden, down[...])
    acc_ref[:, width:] = matmul(act_grad, up[...])


def gathered(arrived, pieces, units, slots):
    experts = arrived.shape[0]
    width = pieces[0].shape[1]
    lines = slots * 2 * width // (experts * 128)
    count = len(pieces) // 2
    return pl.pallas_call(
        functools.partial(gathered_kernel, units, lines),
        out_shape=(
            jax.ShapeDtypeStruct((slots, 2 * width), F32),
            jax.ShapeDtypeStruct((slots, 2 * width), BF16),
        ),
        in_specs=[pl.BlockSpec(memory_space=pltpu.VMEM)] + [pl.BlockSpec(memory_space=pl.ANY)] * len(pieces),
        out_specs=(pl.BlockSpec(memory_space=pltpu.VMEM), pl.BlockSpec(memory_space=pltpu.VMEM)),
        scratch_shapes=[
            pltpu.VMEM((count * units, width), BF16),
            pltpu.VMEM((count * units, width), BF16),
            pltpu.VMEM((experts * lines, 128), F32),
            pltpu.SemaphoreType.DMA((count, 2)),
        ],
        compiler_params=pltpu.CompilerParams(vmem_limit_bytes=VMEM_LIMIT + (4 << 20)),
        cost_estimate=pl.CostEstimate(
            flops=8 * slots * count * units * width,
            bytes_accessed=4 * count * units * width,
            transcendentals=0,
        ),
        name="gathered",
    )(arrived, *map(outside, pieces))


def last_kernel(units, rows_ref, acc_ref, up_ref, down_ref, out_ref, wide):
    width = up_ref.shape[1]
    experts, lines, _ = out_ref.shape
    capacity = rows_ref.shape[0] // experts
    blocks = lines // capacity
    up, down = up_ref[:units, :], down_ref[:units, :]
    tok, cot = rows_ref[:, :width], rows_ref[:, width:]
    hidden, act_grad = activations(matmul_nt(tok, up), matmul_nt(cot, down))
    for part, (acts, weights) in enumerate(((hidden, down), (act_grad, up))):
        sums = acc_ref[:, part * width : (part + 1) * width] + matmul(acts, weights)
        for b in range(width // 128):
            line = part * (width // 128) + b
            for r in range(capacity):
                wide[pl.ds(r * blocks + line, experts, stride=lines), :] = sums[
                    r * experts : (r + 1) * experts, b * 128 : (b + 1) * 128
                ]
    for e in range(experts):
        out_ref[e] = wide[e * lines : (e + 1) * lines, :].astype(BF16)


def last(rows, acc, up_half, down_half, units, experts):
    lines = rows.shape[0] * rows.shape[1] // (experts * 128)
    return pl.pallas_call(
        functools.partial(last_kernel, units),
        out_shape=jax.ShapeDtypeStruct((experts, lines, 128), BF16),
        scratch_shapes=[pltpu.VMEM((experts * lines, 128), F32)],
        compiler_params=pltpu.CompilerParams(vmem_limit_bytes=VMEM_LIMIT),
        name="last",
    )(rows, acc, up_half, down_half)


def hot_kernel(units, hot_rows, where_ref, pieces_ref, *refs):
    blocks, (send_ref, keep_ref, tok, cot, weights, sems) = refs[:-6], refs[-6:]
    ring = len(blocks)
    width = tok.shape[1]
    here = where_ref[0]
    copies = []
    for i, block in enumerate(blocks):
        place = pl.multiple_of((here ^ lax.rem(here + i, ring)) * HOT_PAD, HOT_PAD)
        pair = block if isinstance(block, tuple) else (block, block)
        offset = 0 if isinstance(block, tuple) else units + HOT_PAD
        for j, whole in enumerate((tok, cot)):
            copy = pltpu.make_async_copy(
                pair[j].at[pl.ds(j * offset + units, HOT_PAD)], whole.at[pl.ds(place, HOT_PAD)], sems.at[i, j]
            )
            copy.start()
            copies.append(copy)
    columns = width // 128
    tall = pieces_ref.shape[1]
    for k in range(pieces_ref.shape[0]):
        i, j = k // columns, k % columns
        weights[i * tall : (i + 1) * tall, j * 128 : (j + 1) * 128] = pieces_ref[k]
    for copy in copies:
        copy.wait()
    up, down = weights[:units, :], weights[units:, :]
    hidden, act_grad = activations(matmul_nt(tok[...], up), matmul_nt(cot[...], down))
    packed = send_ref.shape[0]
    row = lax.broadcasted_iota(I32, (packed, ring * HOT_PAD), 0)
    column = lax.broadcasted_iota(I32, (packed, ring * HOT_PAD), 1)
    group = row // hot_rows
    place = (group % 2) * 4 + (group // 2) * 2
    within = place * HOT_PAD + row % hot_rows
    for odd, out_ref in ((1, send_ref), (0, keep_ref)):
        chosen = (column == within + odd * HOT_PAD).astype(F32).astype(BF16)
        picked_hidden = matmul(chosen, hidden).astype(BF16)
        picked_grad = matmul(chosen, act_grad).astype(BF16)
        out_ref[:, :width] = matmul(picked_hidden, down).astype(BF16)
        out_ref[:, width:] = matmul(picked_grad, up).astype(BF16)


def hot_partials(here, pieces, blocks, units, hot_rows, after):
    ring = len(blocks)
    flat, spans = [], []
    for block in blocks:
        spans.append(len(block) if isinstance(block, tuple) else 0)
        flat += list(block) if isinstance(block, tuple) else [block]
    width = flat[0].shape[1]

    def kernel(where_ref, pieces_ref, after_ref, *refs):
        refs, grouped = list(refs), []
        for span in spans:
            grouped.append(tuple(refs.pop(0) for _ in range(span)) if span else refs.pop(0))
        hot_kernel(units, hot_rows, where_ref, pieces_ref, *grouped, *refs)

    inside = pl.BlockSpec(memory_space=pltpu.VMEM)
    packed = jax.ShapeDtypeStruct((ring // 2 * hot_rows, 2 * width), BF16)
    return pl.pallas_call(
        kernel,
        out_shape=(packed, packed),
        in_specs=[pl.BlockSpec(memory_space=pltpu.SMEM), inside]
        + [pl.BlockSpec(memory_space=pl.ANY)] * (1 + len(flat)),
        out_specs=(inside, inside),
        scratch_shapes=[
            pltpu.VMEM((ring * HOT_PAD, width), BF16),
            pltpu.VMEM((ring * HOT_PAD, width), BF16),
            pltpu.VMEM((2 * units, width), BF16),
            pltpu.SemaphoreType.DMA((ring, 2)),
        ],
        compiler_params=pltpu.CompilerParams(vmem_limit_bytes=VMEM_LIMIT),
        name="hot",
    )(here, pieces, after, *map(outside, flat))


def thirds(x):
    first = x.astype(BF16)
    rest = x - first.astype(F32)
    second = rest.astype(BF16)
    third = (rest - second.astype(F32)).astype(BF16)
    return first, second, third


def cold_kernel(capacity, ids_ref, gate_ref, cot_ref, cold_ref, sum_ref, dots_ref, wide, rows):
    ids, gates, cot = ids_ref[...], gate_ref[...], cot_ref[...]
    top_count = ids.shape[0]
    experts, lines, _ = cold_ref.shape
    blocks = lines // capacity
    width = cot.shape[1]
    for e in range(experts):
        wide[e * lines : (e + 1) * lines, :] = cold_ref[e].astype(F32)
    for r in range(capacity):
        for b in range(blocks):
            line = wide[pl.ds(r * blocks + b, experts, stride=lines), :]
            rows[r * experts : (r + 1) * experts, b * 128 : (b + 1) * 128] = line.astype(BF16)
    cold, _, expert, _, _ = slot_maps(ids, experts * capacity, capacity, slot_major=True)
    per_slot = jnp.zeros(cold.shape, F32)
    for k in range(top_count):
        per_slot = per_slot + jnp.where(ids[k : k + 1, :] == expert, gates[k : k + 1, :], 0.0)
    scale = thirds(jnp.where(cold > 0, per_slot, 0.0))
    for lo in (0, width):
        part = rows[:, lo : lo + width]
        sum_ref[:, lo : lo + width] = matmul_tn(scale[0], part) + matmul_tn(scale[1], part) + matmul_tn(scale[2], part)
    dots = jnp.where(cold > 0, matmul_nt(rows[:, :width], cot), 0.0)
    for k in range(top_count):
        dots_ref[k : k + 1, :] = jnp.sum(jnp.where(ids[k : k + 1, :] == expert, dots, 0.0), 0, keepdims=True)


def cold_combine(ids, gates, cotangent, results, capacity):
    tok_rows, width = cotangent.shape
    experts, lines, _ = results.shape
    return pl.pallas_call(
        functools.partial(cold_kernel, capacity),
        out_shape=(
            jax.ShapeDtypeStruct((tok_rows, 2 * width), F32),
            jax.ShapeDtypeStruct(gates.shape, F32),
        ),
        scratch_shapes=[
            pltpu.VMEM((experts * lines, 128), F32),
            pltpu.VMEM((experts * capacity, 2 * width), BF16),
        ],
        compiler_params=pltpu.CompilerParams(vmem_limit_bytes=VMEM_LIMIT),
        cost_estimate=pl.CostEstimate(flops=1 << 36, bytes_accessed=1 << 26, transcendentals=0),
        name="cold_combine",
    )(ids, gates, cotangent, results)


def final_kernel(
    capacity, slots, ids_ref, gate_ref, cot_ref, sum_ref, dots_ref, kept_ref, *refs
):
    sent, (mix_ref, grad_ref, gate_grad_ref) = refs[:-3], refs[-3:]
    ids, gates, cot = ids_ref[...], gate_ref[...], cot_ref[...]
    top_count, tok_rows = ids.shape
    width = cot.shape[1]
    hot_rows = kept_ref.shape[0]
    _, hot, _, _, hottest = slot_maps(ids, slots, capacity)
    hottest = hottest.astype(I32)
    gate = jnp.zeros((1, tok_rows), F32)
    for k in range(top_count):
        gate = gate + jnp.where(ids[k : k + 1, :] == hottest, gates[k : k + 1, :], 0.0)
    hot = hot[:hot_rows]
    scale = thirds(jnp.where(hot > 0, gate, 0.0))
    result = kept_ref[...]
    for ref in sent:
        result = result + ref[...].astype(F32)
    result = result.astype(BF16)
    for lo, out_ref in ((0, mix_ref), (width, grad_ref)):
        rows = result[:, lo : lo + width]
        total = matmul_tn(scale[0], rows) + matmul_tn(scale[1], rows) + matmul_tn(scale[2], rows)
        out_ref[...] = (sum_ref[:, lo : lo + width] + total).astype(BF16)
    dots = jnp.where(hot > 0, matmul_nt(result[:, :width], cot), 0.0)
    dot = jnp.sum(dots, 0, keepdims=True)
    gate_grad_ref[...] = dots_ref[...] + jnp.where(ids == hottest, dot, 0.0)


def final_combine(ids, gates, cotangent, sums, dots, kept, sent, slots, capacity):
    return pl.pallas_call(
        functools.partial(final_kernel, capacity, slots),
        out_shape=(
            jax.ShapeDtypeStruct(cotangent.shape, BF16),
            jax.ShapeDtypeStruct(cotangent.shape, BF16),
            jax.ShapeDtypeStruct(gates.shape, F32),
        ),
        compiler_params=pltpu.CompilerParams(vmem_limit_bytes=VMEM_LIMIT),
        name="final_combine",
    )(ids, gates, cotangent, sums, dots, kept, *sent)


TICK = pl.CostEstimate(flops=1 << 35, bytes_accessed=1 << 25, transcendentals=0)


def tick_kernel(token_ref, *refs):
    refs[-1][0, 0] = token_ref[0, 0]


def tick(token, *after):
    scalar = pl.BlockSpec(memory_space=pltpu.SMEM)
    return pl.pallas_call(
        tick_kernel,
        out_shape=jax.ShapeDtypeStruct(token.shape, token.dtype),
        in_specs=[scalar] + [pl.BlockSpec(memory_space=pl.ANY)] * len(after),
        out_specs=scalar,
        compiler_params=pltpu.CompilerParams(vmem_limit_bytes=1 << 20),
        cost_estimate=pl.CostEstimate(flops=22 << 30, bytes_accessed=1 << 10, transcendentals=0),
        name="tick",
    )(token, *after)


def gate_kernel(*refs):
    pass


def gate(*arrays):
    anywhere = pl.BlockSpec(memory_space=pl.ANY)
    return pl.pallas_call(
        gate_kernel,
        out_shape=tuple(jax.ShapeDtypeStruct(x.shape, x.dtype) for x in arrays),
        in_specs=[anywhere] * len(arrays),
        out_specs=tuple([anywhere] * len(arrays)),
        input_output_aliases={i: i for i in range(len(arrays))},
        compiler_params=pltpu.CompilerParams(vmem_limit_bytes=1 << 20),
        cost_estimate=TICK,
        name="gate",
    )(*arrays)


def shift(x, by):
    ring = lax.axis_size("dp")
    return lax.ppermute(x, "dp", [(i, (i + by) % ring) for i in range(ring)])


def swap(x, bit):
    ring = lax.axis_size("dp")
    pairs = [[i, i ^ bit] for i in range(ring) if not i & bit]
    both = lax.all_gather(x, "dp", axis=0, axis_index_groups=pairs, tiled=False)
    return jnp.where(lax.axis_index("dp") & bit == 0, both[1], both[0])


def send_on(x, bits):
    ring = lax.axis_size("dp")
    return lax.ppermute(x, "dp", [(i, i ^ bits) for i in range(ring)])


def shards(tokens, cotangent, gate_probs, expert_ids, up_weight, down_weight):
    tok_rows, width = tokens.shape
    top_count = expert_ids.shape[1]
    experts = lax.axis_size("expert")
    hot_rows = 9 * tok_rows // 16
    capacity = (tok_rows * top_count - hot_rows + experts - 2) // (experts - 1)
    slots = experts * capacity
    up, down = up_weight[0], down_weight[0]
    units = up.shape[0]
    ids, gates = expert_ids.T, gate_probs.T

    outgoing, own_up, own_down, hottest = route(ids, tokens, cotangent, up, down, slots, capacity)
    right, left = [(own_up, own_down)], [(own_up, own_down)]
    for step in range(3):
        r = [shift(x, 1) for x in right[-1]]
        l = [shift(x, -1) for x in left[-1]]
        if step == 1:
            token = tick(hottest, *r, *l)
        if step == 2:
            r[0], l[1] = gate(r[0], l[1])
        right.append(tuple(r))
        left.append(tuple(l))
    far_up, far_down = shift(right[-1][0], 1), shift(left[-1][1], -1)

    lines = capacity * 2 * width // 128
    outgoing = assemble(outgoing.reshape(experts, lines, 128), up, down)
    arrived = lax.all_to_all(outgoing, "expert", 0, 0, tiled=True)
    hot_pieces = lax.all_to_all(repeat(token, arrived, lines), "expert", 0, 0, tiled=True)

    acc, rows = gathered(arrived, [x for pair in right + left[1:] for x in pair], units, slots)
    results = last(rows, acc, far_up, far_down, units, experts)
    came_back = lax.all_to_all(results, "expert", 0, 0, tiled=True)

    blocks = left + [(far_up, far_down)] + right[:0:-1]
    here = lax.axis_index("dp").astype(I32).reshape(1)
    send, keep = hot_partials(here, hot_pieces, blocks, units, hot_rows, results)
    both = keep.astype(F32) + swap(send, 1).astype(F32)
    kept = both[:hot_rows]
    sent = [
        send_on(both[i * hot_rows : (i + 1) * hot_rows].astype(BF16), place) for i, place in ((1, 4), (2, 2), (3, 6))
    ]
    sums, dots = cold_combine(ids, gates, cotangent, came_back, capacity)
    mixture, input_grad, gate_grad = final_combine(
        ids, gates, cotangent, sums, dots, kept, sent, slots, capacity
    )
    return mixture, input_grad, gate_grad.T


def solution(mesh):
    rows = P(("dp", "expert"), None)
    weights = P("expert", "dp", None)
    return jax.shard_map(
        shards,
        mesh=mesh,
        in_specs=(rows, rows, rows, rows, weights, weights),
        out_specs=(rows, rows, rows),
        check_vma=False,
    )
```

```python
import functools

import jax
import jax.numpy as jnp
from jax import lax
from jax.experimental import pallas as pl
from jax.experimental.pallas import tpu as pltpu
from jax.sharding import PartitionSpec as P

BF16, F32, I32 = jnp.bfloat16, jnp.float32, jnp.int32
HOT_PAD = 16
LANES = 1024
VMEM_LIMIT = 16 * 1024 * 1024


def outside(x):
    return pltpu.with_memory_space_constraint(x, pltpu.HBM)


def matmul(a, b):
    return lax.dot_general(a, b, (((1,), (0,)), ((), ())), preferred_element_type=F32)


def matmul_nt(a, b):
    return lax.dot_general(a, b, (((1,), (1,)), ((), ())), preferred_element_type=F32)


def matmul_tn(a, b):
    return lax.dot_general(a, b, (((0,), (0,)), ((), ())), preferred_element_type=F32)


def slot_maps(ids, slots, capacity, slot_major=False):
    top_count, tok_rows = ids.shape
    slot = lax.broadcasted_iota(I32, (slots, tok_rows), 0)
    experts = slots // capacity
    expert, within = (slot % experts, slot // experts) if slot_major else (slot // capacity, slot % capacity)
    named = jnp.zeros((slots, tok_rows), F32)
    for k in range(top_count):
        named = named + (ids[k : k + 1, :] == expert).astype(F32)
    counts = jnp.sum(named, 1, keepdims=True)
    is_hot = (counts == jnp.max(counts)).astype(F32)
    earlier = (
        lax.broadcasted_iota(I32, (tok_rows, tok_rows), 0)
        < lax.broadcasted_iota(I32, (tok_rows, tok_rows), 1)
    ).astype(BF16)
    rank = matmul(named.astype(BF16), earlier)
    cold = named * (1.0 - is_hot) * (rank == within.astype(F32)).astype(F32)
    first = is_hot * (within[:, :1] == 0).astype(F32)
    hot_token = jnp.sum(named * first, 0, keepdims=True)
    hot_rank = jnp.sum(rank * first, 0, keepdims=True)
    hot_row = lax.broadcasted_iota(I32, (HOT_PAD, tok_rows), 0).astype(F32)
    hot = hot_token * (hot_rank == hot_row).astype(F32)
    hottest = jnp.sum(first * expert[:, :1].astype(F32), 0, keepdims=True)
    return cold, hot, expert, is_hot, hottest


def route_kernel(
    capacity, ids_ref, tok_ref, cot_ref, up_ref, down_ref, out_ref, own_ref, hottest_ref, tok, cot, sems
):
    slots, width = out_ref.shape[0], tok.shape[1]
    units = up_ref.shape[0]
    half = own_ref.shape[0] // 2
    loads = [pltpu.make_async_copy(tok_ref, tok, sems.at[0]), pltpu.make_async_copy(cot_ref, cot, sems.at[1])]
    copies = [
        pltpu.make_async_copy(up_ref, own_ref.at[pl.ds(0, units)], sems.at[2]),
        pltpu.make_async_copy(down_ref, own_ref.at[pl.ds(half, units)], sems.at[3]),
    ]
    for copy in loads + copies:
        copy.start()
    cold, hot, _, _, hottest = slot_maps(ids_ref[...], slots, capacity)
    cold, hot = cold.astype(BF16), hot.astype(BF16)
    hottest_ref[0, 0] = jnp.max(hottest).astype(I32)
    for copy in loads:
        copy.wait()
    own_ref[units:half, :] = matmul(hot, tok[...]).astype(BF16)
    own_ref[half + units :, :] = matmul(hot, cot[...]).astype(BF16)
    out_ref[:, :width] = matmul(cold, tok[...]).astype(BF16)
    out_ref[:, width:] = matmul(cold, cot[...]).astype(BF16)
    for copy in copies:
        copy.wait()


def route(ids, tokens, cotangent, up, down, slots, capacity):
    tok_rows, width = tokens.shape
    units = up.shape[0]
    anywhere = pl.BlockSpec(memory_space=pl.ANY)
    inside = pl.BlockSpec(memory_space=pltpu.VMEM)
    return pl.pallas_call(
        functools.partial(route_kernel, capacity),
        out_shape=(
            jax.ShapeDtypeStruct((slots, 2 * width), BF16),
            jax.ShapeDtypeStruct((2 * (units + HOT_PAD), width), BF16),
            jax.ShapeDtypeStruct((1, 1), I32),
        ),
        in_specs=[inside] + [anywhere] * 4,
        out_specs=(inside, inside, pl.BlockSpec(memory_space=pltpu.SMEM)),
        scratch_shapes=[
            pltpu.VMEM((tok_rows, width), BF16),
            pltpu.VMEM((tok_rows, width), BF16),
            pltpu.SemaphoreType.DMA((4,)),
        ],
        compiler_params=pltpu.CompilerParams(vmem_limit_bytes=VMEM_LIMIT),
        name="route",
    )(ids, *map(outside, (tokens, cotangent, up, down)))


def assemble_kernel(tall, rows_ref, up_ref, down_ref, out_ref, up, down, sems):
    copies = []
    for i, (source, here) in enumerate(((up_ref, up), (down_ref, down))):
        copy = pltpu.make_async_copy(source, here, sems.at[i])
        copy.start()
        copies.append(copy)
    lines = rows_ref.shape[1]
    out_ref[:, :lines, :] = rows_ref[...]
    columns = up.shape[1] // 128
    groups = up.shape[0] // tall
    for i, here in enumerate((up, down)):
        copies[i].wait()
        for g in range(groups):
            for j in range(columns):
                out_ref[(i * groups + g) * columns + j, lines:, :] = here[
                    g * tall : (g + 1) * tall, j * 128 : (j + 1) * 128
                ]


def assemble(rows, up, down):
    experts, lines, lanes = rows.shape
    units, width = up.shape
    tall = 2 * units * width // (experts * lanes)
    return pl.pallas_call(
        functools.partial(assemble_kernel, tall),
        out_shape=jax.ShapeDtypeStruct((experts, lines + tall, lanes), BF16),
        in_specs=[pl.BlockSpec(memory_space=pltpu.VMEM)] + [pl.BlockSpec(memory_space=pl.ANY)] * 2,
        out_specs=pl.BlockSpec(memory_space=pltpu.VMEM),
        scratch_shapes=[
            pltpu.VMEM((units, width), BF16),
            pltpu.VMEM((units, width), BF16),
            pltpu.SemaphoreType.DMA((2,)),
        ],
        compiler_params=pltpu.CompilerParams(vmem_limit_bytes=VMEM_LIMIT),
        name="assemble",
    )(rows, outside(up), outside(down))


def repeat_kernel(lines, hottest_ref, arrived_ref, out_ref):
    mine = arrived_ref[hottest_ref[0, 0], lines:, :]
    out_ref[...] = jnp.broadcast_to(mine[None], out_ref.shape)


def repeat(hottest, arrived, lines):
    experts, height, lanes = arrived.shape
    inside = pl.BlockSpec(memory_space=pltpu.VMEM)
    return pl.pallas_call(
        functools.partial(repeat_kernel, lines),
        out_shape=jax.ShapeDtypeStruct((experts, height - lines, lanes), BF16),
        in_specs=[pl.BlockSpec(memory_space=pltpu.SMEM), inside],
        out_specs=inside,
        compiler_params=pltpu.CompilerParams(vmem_limit_bytes=VMEM_LIMIT),
        name="repeat",
    )(hottest, arrived)


def activations(pre_act, hidden_grad):
    gating = jax.nn.sigmoid(pre_act)
    hidden = (pre_act * gating).astype(BF16)
    act_grad = (hidden_grad * gating * (1.0 + pre_act * (1.0 - gating))).astype(BF16)
    return hidden, act_grad


def gathered_kernel(units, lines, arrived_ref, *refs):
    pieces, (acc_ref, rows_ref, up, down, wide, sems) = refs[:-6], refs[-6:]
    width = up.shape[1]
    half = pieces[0].shape[0] // 2
    experts = arrived_ref.shape[0]
    capacity = rows_ref.shape[0] // experts
    copies = []
    for i, piece in enumerate(pieces):
        for j, whole in enumerate((up, down)):
            copy = pltpu.make_async_copy(
                piece.at[pl.ds(j * half, units)], whole.at[pl.ds(i * units, units)], sems.at[i, j]
            )
            copy.start()
            copies.append(copy)
    for e in range(experts):
        wide[e * lines : (e + 1) * lines, :] = arrived_ref[e, :lines, :].astype(F32)
    blocks = lines // capacity
    for r in range(capacity):
        for b in range(blocks):
            line = wide[pl.ds(r * blocks + b, experts, stride=lines), :]
            rows_ref[r * experts : (r + 1) * experts, b * 128 : (b + 1) * 128] = line.astype(BF16)
    for copy in copies:
        copy.wait()
    tok, cot = rows_ref[:, :width], rows_ref[:, width:]
    hidden, act_grad = activations(matmul_nt(tok, up[...]), matmul_nt(cot, down[...]))
    acc_ref[:, :width] = matmul(hidden, down[...])
    acc_ref[:, width:] = matmul(act_grad, up[...])


def gathered(arrived, pieces, units, slots):
    experts = arrived.shape[0]
    width = pieces[0].shape[1]
    lines = slots * 2 * width // (experts * 128)
    count = len(pieces)
    return pl.pallas_call(
        functools.partial(gathered_kernel, units, lines),
        out_shape=(
            jax.ShapeDtypeStruct((slots, 2 * width), F32),
            jax.ShapeDtypeStruct((slots, 2 * width), BF16),
        ),
        in_specs=[pl.BlockSpec(memory_space=pltpu.VMEM)] + [pl.BlockSpec(memory_space=pl.ANY)] * count,
        out_specs=(pl.BlockSpec(memory_space=pltpu.VMEM), pl.BlockSpec(memory_space=pltpu.VMEM)),
        scratch_shapes=[
            pltpu.VMEM((count * units, width), BF16),
            pltpu.VMEM((count * units, width), BF16),
            pltpu.VMEM((experts * lines, 128), F32),
            pltpu.SemaphoreType.DMA((count, 2)),
        ],
        compiler_params=pltpu.CompilerParams(vmem_limit_bytes=VMEM_LIMIT + (4 << 20)),
        cost_estimate=pl.CostEstimate(
            flops=8 * slots * count * units * width,
            bytes_accessed=4 * count * units * width,
            transcendentals=0,
        ),
        name="gathered",
    )(arrived, *map(outside, pieces))


def last_kernel(units, rows_ref, acc_ref, up_ref, down_ref, out_ref, wide):
    width = up_ref.shape[1]
    experts, lines, _ = out_ref.shape
    capacity = rows_ref.shape[0] // experts
    blocks = lines // capacity
    up, down = up_ref[:units, :], down_ref[:units, :]
    tok, cot = rows_ref[:, :width], rows_ref[:, width:]
    hidden, act_grad = activations(matmul_nt(tok, up), matmul_nt(cot, down))
    for part, (acts, weights) in enumerate(((hidden, down), (act_grad, up))):
        sums = acc_ref[:, part * width : (part + 1) * width] + matmul(acts, weights)
        for b in range(width // 128):
            line = part * (width // 128) + b
            for r in range(capacity):
                wide[pl.ds(r * blocks + line, experts, stride=lines), :] = sums[
                    r * experts : (r + 1) * experts, b * 128 : (b + 1) * 128
                ]
    for e in range(experts):
        out_ref[e] = wide[e * lines : (e + 1) * lines, :].astype(BF16)


def last(rows, acc, up_half, down_half, units, experts):
    lines = rows.shape[0] * rows.shape[1] // (experts * 128)
    return pl.pallas_call(
        functools.partial(last_kernel, units),
        out_shape=jax.ShapeDtypeStruct((experts, lines, 128), BF16),
        scratch_shapes=[pltpu.VMEM((experts * lines, 128), F32)],
        compiler_params=pltpu.CompilerParams(vmem_limit_bytes=VMEM_LIMIT),
        name="last",
    )(rows, acc, up_half, down_half)


def hot_kernel(units, hot_rows, where_ref, pieces_ref, *refs):
    blocks, (send_ref, keep_ref, tok, cot, weights, sems) = refs[:-6], refs[-6:]
    ring = len(blocks)
    width = tok.shape[1]
    here = where_ref[0]
    copies = []
    for i, block in enumerate(blocks):
        place = pl.multiple_of((here ^ lax.rem(here + i, ring)) * HOT_PAD, HOT_PAD)
        pair = block if isinstance(block, tuple) else (block, block)
        offset = 0 if isinstance(block, tuple) else units + HOT_PAD
        for j, whole in enumerate((tok, cot)):
            copy = pltpu.make_async_copy(
                pair[j].at[pl.ds(j * offset + units, HOT_PAD)], whole.at[pl.ds(place, HOT_PAD)], sems.at[i, j]
            )
            copy.start()
            copies.append(copy)
    columns = width // 128
    tall = pieces_ref.shape[1]
    for k in range(pieces_ref.shape[0]):
        i, j = k // columns, k % columns
        weights[i * tall : (i + 1) * tall, j * 128 : (j + 1) * 128] = pieces_ref[k]
    for copy in copies:
        copy.wait()
    up, down = weights[:units, :], weights[units:, :]
    hidden, act_grad = activations(matmul_nt(tok[...], up), matmul_nt(cot[...], down))
    packed, lanes = send_ref.shape
    blocks_of = 2 * width // lanes
    row = lax.broadcasted_iota(I32, (packed, ring * HOT_PAD), 0)
    column = lax.broadcasted_iota(I32, (packed, ring * HOT_PAD), 1)
    group = row // (blocks_of * hot_rows)
    block_of = row // hot_rows % blocks_of
    within = ((group % 2) * 4 + (group // 2) * 2) * HOT_PAD + row % hot_rows
    for odd, out_ref in ((1, send_ref), (0, keep_ref)):
        total = jnp.zeros((packed, lanes), F32)
        for b in range(blocks_of):
            chosen = ((column == within + odd * HOT_PAD) & (block_of == b)).astype(F32).astype(BF16)
            acts, matrix = (hidden, down) if b * lanes < width else (act_grad, up)
            lo = b * lanes % width
            total = total + matmul(matmul(chosen, acts).astype(BF16), matrix[:, lo : lo + lanes])
        out_ref[...] = total.astype(BF16)


def hot_partials(here, pieces, blocks, units, hot_rows, after):
    ring = len(blocks)
    flat, spans = [], []
    for block in blocks:
        spans.append(len(block) if isinstance(block, tuple) else 0)
        flat += list(block) if isinstance(block, tuple) else [block]
    width = flat[0].shape[1]

    def kernel(where_ref, pieces_ref, after_ref, *refs):
        refs, grouped = list(refs), []
        for span in spans:
            grouped.append(tuple(refs.pop(0) for _ in range(span)) if span else refs.pop(0))
        hot_kernel(units, hot_rows, where_ref, pieces_ref, *grouped, *refs)

    inside = pl.BlockSpec(memory_space=pltpu.VMEM)
    packed = jax.ShapeDtypeStruct((ring // 2 * hot_rows * (2 * width // LANES), LANES), BF16)
    return pl.pallas_call(
        kernel,
        out_shape=(packed, packed),
        in_specs=[pl.BlockSpec(memory_space=pltpu.SMEM), inside]
        + [pl.BlockSpec(memory_space=pl.ANY)] * (1 + len(flat)),
        out_specs=(inside, inside),
        scratch_shapes=[
            pltpu.VMEM((ring * HOT_PAD, width), BF16),
            pltpu.VMEM((ring * HOT_PAD, width), BF16),
            pltpu.VMEM((2 * units, width), BF16),
            pltpu.SemaphoreType.DMA((ring, 2)),
        ],
        compiler_params=pltpu.CompilerParams(vmem_limit_bytes=VMEM_LIMIT),
        name="hot",
    )(here, pieces, after, *map(outside, flat))


def thirds(x):
    first = x.astype(BF16)
    rest = x - first.astype(F32)
    second = rest.astype(BF16)
    third = (rest - second.astype(F32)).astype(BF16)
    return first, second, third


def cold_kernel(capacity, ids_ref, gate_ref, cot_ref, cold_ref, sum_ref, dots_ref, wide, rows):
    ids, gates, cot = ids_ref[...], gate_ref[...], cot_ref[...]
    top_count = ids.shape[0]
    experts, lines, _ = cold_ref.shape
    blocks = lines // capacity
    width = cot.shape[1]
    for e in range(experts):
        wide[e * lines : (e + 1) * lines, :] = cold_ref[e].astype(F32)
    for r in range(capacity):
        for b in range(blocks):
            line = wide[pl.ds(r * blocks + b, experts, stride=lines), :]
            rows[r * experts : (r + 1) * experts, b * 128 : (b + 1) * 128] = line.astype(BF16)
    cold, _, expert, _, _ = slot_maps(ids, experts * capacity, capacity, slot_major=True)
    per_slot = jnp.zeros(cold.shape, F32)
    for k in range(top_count):
        per_slot = per_slot + jnp.where(ids[k : k + 1, :] == expert, gates[k : k + 1, :], 0.0)
    scale = thirds(jnp.where(cold > 0, per_slot, 0.0))
    for lo in (0, width):
        part = rows[:, lo : lo + width]
        sum_ref[:, lo : lo + width] = matmul_tn(scale[0], part) + matmul_tn(scale[1], part) + matmul_tn(scale[2], part)
    dots = jnp.where(cold > 0, matmul_nt(rows[:, :width], cot), 0.0)
    for k in range(top_count):
        dots_ref[k : k + 1, :] = jnp.sum(jnp.where(ids[k : k + 1, :] == expert, dots, 0.0), 0, keepdims=True)


def cold_combine(ids, gates, cotangent, results, capacity):
    tok_rows, width = cotangent.shape
    experts, lines, _ = results.shape
    return pl.pallas_call(
        functools.partial(cold_kernel, capacity),
        out_shape=(
            jax.ShapeDtypeStruct((tok_rows, 2 * width), F32),
            jax.ShapeDtypeStruct(gates.shape, F32),
        ),
        scratch_shapes=[
            pltpu.VMEM((experts * lines, 128), F32),
            pltpu.VMEM((experts * capacity, 2 * width), BF16),
        ],
        compiler_params=pltpu.CompilerParams(vmem_limit_bytes=VMEM_LIMIT),
        cost_estimate=pl.CostEstimate(flops=1 << 36, bytes_accessed=1 << 26, transcendentals=0),
        name="cold_combine",
    )(ids, gates, cotangent, results)


def final_kernel(
    capacity, slots, ids_ref, gate_ref, cot_ref, sum_ref, dots_ref, kept_ref, *refs
):
    sent, (mix_ref, grad_ref, gate_grad_ref) = refs[:-3], refs[-3:]
    ids, gates, cot = ids_ref[...], gate_ref[...], cot_ref[...]
    top_count, tok_rows = ids.shape
    width = cot.shape[1]
    lanes = kept_ref.shape[1]
    hot_rows = kept_ref.shape[0] * lanes // (2 * width)
    _, hot, _, _, hottest = slot_maps(ids, slots, capacity)
    hottest = hottest.astype(I32)
    gate = jnp.zeros((1, tok_rows), F32)
    for k in range(top_count):
        gate = gate + jnp.where(ids[k : k + 1, :] == hottest, gates[k : k + 1, :], 0.0)
    hot = hot[:hot_rows]
    scale = thirds(jnp.where(hot > 0, gate, 0.0))
    result = kept_ref[...]
    for ref in sent:
        result = result + ref[...].astype(F32)
    dots = jnp.zeros(hot.shape, F32)
    for b in range(2 * width // lanes):
        rows = result[b * hot_rows : (b + 1) * hot_rows].astype(BF16)
        lo, at = b * lanes, b * lanes % width
        total = matmul_tn(scale[0], rows) + matmul_tn(scale[1], rows) + matmul_tn(scale[2], rows)
        out_ref = mix_ref if lo < width else grad_ref
        out_ref[:, at : at + lanes] = (sum_ref[:, lo : lo + lanes] + total).astype(BF16)
        if lo < width:
            dots = dots + matmul_nt(rows, cot[:, at : at + lanes])
    dot = jnp.sum(jnp.where(hot > 0, dots, 0.0), 0, keepdims=True)
    gate_grad_ref[...] = dots_ref[...] + jnp.where(ids == hottest, dot, 0.0)


def final_combine(ids, gates, cotangent, sums, dots, kept, sent, slots, capacity):
    return pl.pallas_call(
        functools.partial(final_kernel, capacity, slots),
        out_shape=(
            jax.ShapeDtypeStruct(cotangent.shape, BF16),
            jax.ShapeDtypeStruct(cotangent.shape, BF16),
            jax.ShapeDtypeStruct(gates.shape, F32),
        ),
        compiler_params=pltpu.CompilerParams(vmem_limit_bytes=VMEM_LIMIT),
        name="final_combine",
    )(ids, gates, cotangent, sums, dots, kept, *sent)


TICK = pl.CostEstimate(flops=1 << 35, bytes_accessed=1 << 25, transcendentals=0)


def tick_kernel(token_ref, *refs):
    refs[-1][0, 0] = token_ref[0, 0]


def tick(token, *after):
    scalar = pl.BlockSpec(memory_space=pltpu.SMEM)
    return pl.pallas_call(
        tick_kernel,
        out_shape=jax.ShapeDtypeStruct(token.shape, token.dtype),
        in_specs=[scalar] + [pl.BlockSpec(memory_space=pl.ANY)] * len(after),
        out_specs=scalar,
        compiler_params=pltpu.CompilerParams(vmem_limit_bytes=1 << 20),
        cost_estimate=pl.CostEstimate(flops=22 << 30, bytes_accessed=1 << 10, transcendentals=0),
        name="tick",
    )(token, *after)


def split_kernel(right_ref, left_ref, right_out, left_out, top_ref, bottom_ref, sems):
    half = top_ref.shape[0]
    copies = [
        pltpu.make_async_copy(right_ref.at[pl.ds(0, half)], top_ref, sems.at[0]),
        pltpu.make_async_copy(left_ref.at[pl.ds(half, half)], bottom_ref, sems.at[1]),
    ]
    for copy in copies:
        copy.start()
    for copy in copies:
        copy.wait()


def split(right, left):
    anywhere, inside = pl.BlockSpec(memory_space=pl.ANY), pl.BlockSpec(memory_space=pltpu.VMEM)
    whole = jax.ShapeDtypeStruct(right.shape, right.dtype)
    part = jax.ShapeDtypeStruct((right.shape[0] // 2, right.shape[1]), right.dtype)
    return pl.pallas_call(
        split_kernel,
        out_shape=(whole, whole, part, part),
        in_specs=[anywhere] * 2,
        out_specs=(anywhere, anywhere, inside, inside),
        input_output_aliases={0: 0, 1: 1},
        scratch_shapes=[pltpu.SemaphoreType.DMA((2,))],
        compiler_params=pltpu.CompilerParams(vmem_limit_bytes=1 << 22),
        cost_estimate=TICK,
        name="split",
    )(right, left)


def shift(x, by):
    ring = lax.axis_size("dp")
    return lax.ppermute(x, "dp", [(i, (i + by) % ring) for i in range(ring)])


def swap(x, bit):
    ring = lax.axis_size("dp")
    pairs = [[i, i ^ bit] for i in range(ring) if not i & bit]
    both = lax.all_gather(x, "dp", axis=0, axis_index_groups=pairs, tiled=False)
    return jnp.where(lax.axis_index("dp") & bit == 0, both[1], both[0])


def send_on(x, bits):
    ring = lax.axis_size("dp")
    return lax.ppermute(x, "dp", [(i, i ^ bits) for i in range(ring)])


def shards(tokens, cotangent, gate_probs, expert_ids, up_weight, down_weight):
    tok_rows, width = tokens.shape
    top_count = expert_ids.shape[1]
    experts = lax.axis_size("expert")
    hot_rows = 9 * tok_rows // 16
    capacity = (tok_rows * top_count - hot_rows + experts - 2) // (experts - 1)
    slots = experts * capacity
    up, down = up_weight[0], down_weight[0]
    units = up.shape[0]
    ids, gates = expert_ids.T, gate_probs.T

    outgoing, own, hottest = route(ids, tokens, cotangent, up, down, slots, capacity)
    half = own.shape[0] // 2
    right, left = [own], [own]
    for step in range(3):
        r, l = shift(right[-1], 1), shift(left[-1], -1)
        if step == 1:
            token = tick(hottest, r, l)
        if step == 2:
            r, l, top, bottom = split(r, l)
        right.append(r)
        left.append(l)
    far_up, far_down = shift(top, 1), shift(bottom, -1)

    lines = capacity * 2 * width // 128
    outgoing = assemble(outgoing.reshape(experts, lines, 128), up, down)
    arrived = lax.all_to_all(outgoing, "expert", 0, 0, tiled=True)
    hot_pieces = lax.all_to_all(repeat(token, arrived, lines), "expert", 0, 0, tiled=True)

    acc, rows = gathered(arrived, [own] + right[1:] + left[1:], units, slots)
    results = last(rows, acc, far_up, far_down, units, experts)
    came_back = lax.all_to_all(results, "expert", 0, 0, tiled=True)

    blocks = left + [(far_up, far_down)] + right[:0:-1]
    here = lax.axis_index("dp").astype(I32).reshape(1)
    send, keep = hot_partials(here, hot_pieces, blocks, units, hot_rows, results)
    both = keep.astype(F32) + swap(send, 1).astype(F32)
    dense = both.shape[0] // 4
    kept = both[:dense]
    sent = [send_on(both[i * dense : (i + 1) * dense].astype(BF16), place) for i, place in ((1, 4), (2, 2), (3, 6))]
    sums, dots = cold_combine(ids, gates, cotangent, came_back, capacity)
    mixture, input_grad, gate_grad = final_combine(
        ids, gates, cotangent, sums, dots, kept, sent, slots, capacity
    )
    return mixture, input_grad, gate_grad.T


def solution(mesh):
    rows = P(("dp", "expert"), None)
    weights = P("expert", "dp", None)
    return jax.shard_map(
        shards,
        mesh=mesh,
        in_specs=(rows, rows, rows, rows, weights, weights),
        out_specs=(rows, rows, rows),
        check_vma=False,
    )
```

```python
import functools

import jax
import jax.numpy as jnp
from jax import lax
from jax.experimental import pallas as pl
from jax.experimental.pallas import tpu as pltpu
from jax.sharding import PartitionSpec as P

BF16, F32, I32 = jnp.bfloat16, jnp.float32, jnp.int32
HOT_PAD = 16
MOST_VMEM = 58 << 20
LANES = 1024
VMEM_LIMIT = 16 * 1024 * 1024


def outside(x):
    return pltpu.with_memory_space_constraint(x, pltpu.HBM)


def matmul(a, b):
    return lax.dot_general(a, b, (((1,), (0,)), ((), ())), preferred_element_type=F32)


def matmul_nt(a, b):
    return lax.dot_general(a, b, (((1,), (1,)), ((), ())), preferred_element_type=F32)


def matmul_tn(a, b):
    return lax.dot_general(a, b, (((0,), (0,)), ((), ())), preferred_element_type=F32)


def slot_maps(ids, slots, capacity, slot_major=False):
    top_count, tok_rows = ids.shape
    slot = lax.broadcasted_iota(I32, (slots, tok_rows), 0)
    experts = slots // capacity
    expert, within = (slot % experts, slot // experts) if slot_major else (slot // capacity, slot % capacity)
    named = jnp.zeros((slots, tok_rows), F32)
    for k in range(top_count):
        named = named + (ids[k : k + 1, :] == expert).astype(F32)
    counts = jnp.sum(named, 1, keepdims=True)
    is_hot = (counts == jnp.max(counts)).astype(F32)
    earlier = (
        lax.broadcasted_iota(I32, (tok_rows, tok_rows), 0)
        < lax.broadcasted_iota(I32, (tok_rows, tok_rows), 1)
    ).astype(BF16)
    rank = matmul(named.astype(BF16), earlier)
    cold = named * (1.0 - is_hot) * (rank == within.astype(F32)).astype(F32)
    first = is_hot * (within[:, :1] == 0).astype(F32)
    hot_token = jnp.sum(named * first, 0, keepdims=True)
    hot_rank = jnp.sum(rank * first, 0, keepdims=True)
    hot_row = lax.broadcasted_iota(I32, (HOT_PAD, tok_rows), 0).astype(F32)
    hot = hot_token * (hot_rank == hot_row).astype(F32)
    hottest = jnp.sum(first * expert[:, :1].astype(F32), 0, keepdims=True)
    return cold, hot, expert, is_hot, hottest


def route_kernel(
    capacity, ids_ref, tok_ref, cot_ref, up_ref, down_ref, out_ref, own_ref, hottest_ref, tok, cot, sems
):
    slots, width = out_ref.shape[0], tok.shape[1]
    units = up_ref.shape[0]
    half = own_ref.shape[0] // 2
    loads = [pltpu.make_async_copy(tok_ref, tok, sems.at[0]), pltpu.make_async_copy(cot_ref, cot, sems.at[1])]
    copies = [
        pltpu.make_async_copy(up_ref, own_ref.at[pl.ds(0, units)], sems.at[2]),
        pltpu.make_async_copy(down_ref, own_ref.at[pl.ds(half, units)], sems.at[3]),
    ]
    for copy in loads + copies:
        copy.start()
    cold, hot, _, _, hottest = slot_maps(ids_ref[...], slots, capacity)
    cold, hot = cold.astype(BF16), hot.astype(BF16)
    hottest_ref[0, 0] = jnp.max(hottest).astype(I32)
    for copy in loads:
        copy.wait()
    own_ref[units:half, :] = matmul(hot, tok[...]).astype(BF16)
    own_ref[half + units :, :] = matmul(hot, cot[...]).astype(BF16)
    out_ref[:, :width] = matmul(cold, tok[...]).astype(BF16)
    out_ref[:, width:] = matmul(cold, cot[...]).astype(BF16)
    for copy in copies:
        copy.wait()


def route(ids, tokens, cotangent, up, down, slots, capacity):
    tok_rows, width = tokens.shape
    units = up.shape[0]
    anywhere = pl.BlockSpec(memory_space=pl.ANY)
    inside = pl.BlockSpec(memory_space=pltpu.VMEM)
    return pl.pallas_call(
        functools.partial(route_kernel, capacity),
        out_shape=(
            jax.ShapeDtypeStruct((slots, 2 * width), BF16),
            jax.ShapeDtypeStruct((2 * (units + HOT_PAD), width), BF16),
            jax.ShapeDtypeStruct((1, 1), I32),
        ),
        in_specs=[inside] + [anywhere] * 4,
        out_specs=(inside, inside, pl.BlockSpec(memory_space=pltpu.SMEM)),
        scratch_shapes=[
            pltpu.VMEM((tok_rows, width), BF16),
            pltpu.VMEM((tok_rows, width), BF16),
            pltpu.SemaphoreType.DMA((4,)),
        ],
        compiler_params=pltpu.CompilerParams(vmem_limit_bytes=VMEM_LIMIT),
        name="route",
    )(ids, *map(outside, (tokens, cotangent, up, down)))


def assemble_kernel(tall, rows_ref, up_ref, down_ref, out_ref, up, down, sems):
    copies = []
    for i, (source, here) in enumerate(((up_ref, up), (down_ref, down))):
        copy = pltpu.make_async_copy(source, here, sems.at[i])
        copy.start()
        copies.append(copy)
    lines = rows_ref.shape[1]
    out_ref[:, :lines, :] = rows_ref[...]
    columns = up.shape[1] // 128
    groups = up.shape[0] // tall
    for i, here in enumerate((up, down)):
        copies[i].wait()
        for g in range(groups):
            for j in range(columns):
                out_ref[(i * groups + g) * columns + j, lines:, :] = here[
                    g * tall : (g + 1) * tall, j * 128 : (j + 1) * 128
                ]


def assemble(rows, up, down):
    experts, lines, lanes = rows.shape
    units, width = up.shape
    tall = 2 * units * width // (experts * lanes)
    return pl.pallas_call(
        functools.partial(assemble_kernel, tall),
        out_shape=jax.ShapeDtypeStruct((experts, lines + tall, lanes), BF16),
        in_specs=[pl.BlockSpec(memory_space=pltpu.VMEM)] + [pl.BlockSpec(memory_space=pl.ANY)] * 2,
        scratch_shapes=[
            pltpu.VMEM((units, width), BF16),
            pltpu.VMEM((units, width), BF16),
            pltpu.SemaphoreType.DMA((2,)),
        ],
        compiler_params=pltpu.CompilerParams(vmem_limit_bytes=MOST_VMEM),
        name="assemble",
    )(rows, outside(up), outside(down))


def repeat_kernel(lines, hottest_ref, arrived_ref, out_ref, mine, sem):
    copy = pltpu.make_async_copy(arrived_ref.at[hottest_ref[0, 0], pl.ds(lines, mine.shape[0])], mine, sem)
    copy.start()
    copy.wait()
    out_ref[...] = jnp.broadcast_to(mine[...][None], out_ref.shape)


def repeat(hottest, arrived, lines):
    experts, height, lanes = arrived.shape
    return pl.pallas_call(
        functools.partial(repeat_kernel, lines),
        out_shape=jax.ShapeDtypeStruct((experts, height - lines, lanes), BF16),
        in_specs=[pl.BlockSpec(memory_space=pltpu.SMEM), pl.BlockSpec(memory_space=pl.ANY)],
        scratch_shapes=[pltpu.VMEM((height - lines, lanes), BF16), pltpu.SemaphoreType.DMA],
        compiler_params=pltpu.CompilerParams(vmem_limit_bytes=MOST_VMEM),
        name="repeat",
    )(hottest, outside(arrived))


def activations(pre_act, hidden_grad):
    gating = jax.nn.sigmoid(pre_act)
    hidden = (pre_act * gating).astype(BF16)
    act_grad = (hidden_grad * gating * (1.0 + pre_act * (1.0 - gating))).astype(BF16)
    return hidden, act_grad


def gathered_kernel(units, lines, arrived_ref, *refs):
    pieces, (acc_ref, rows_ref, up, down, held, wide, sem, sems) = refs[:-8], refs[-8:]
    rows_copy = pltpu.make_async_copy(arrived_ref.at[:, pl.ds(0, lines)], held, sem)
    rows_copy.start()
    width = up.shape[1]
    half = pieces[0].shape[0] // 2
    experts = arrived_ref.shape[0]
    capacity = rows_ref.shape[0] // experts
    copies = []
    for i, piece in enumerate(pieces):
        for j, whole in enumerate((up, down)):
            copy = pltpu.make_async_copy(
                piece.at[pl.ds(j * half, units)], whole.at[pl.ds(i * units, units)], sems.at[i, j]
            )
            copy.start()
            copies.append(copy)
    rows_copy.wait()
    for e in range(experts):
        wide[e * lines : (e + 1) * lines, :] = held[e].astype(F32)
    blocks = lines // capacity
    for r in range(capacity):
        for b in range(blocks):
            line = wide[pl.ds(r * blocks + b, experts, stride=lines), :]
            rows_ref[r * experts : (r + 1) * experts, b * 128 : (b + 1) * 128] = line.astype(BF16)
    for copy in copies:
        copy.wait()
    tok, cot = rows_ref[:, :width], rows_ref[:, width:]
    hidden, act_grad = activations(matmul_nt(tok, up[...]), matmul_nt(cot, down[...]))
    acc_ref[:, :width] = matmul(hidden, down[...])
    acc_ref[:, width:] = matmul(act_grad, up[...])


def gathered(arrived, pieces, units, slots):
    experts = arrived.shape[0]
    width = pieces[0].shape[1]
    lines = slots * 2 * width // (experts * 128)
    count = len(pieces)
    return pl.pallas_call(
        functools.partial(gathered_kernel, units, lines),
        out_shape=(
            jax.ShapeDtypeStruct((slots, 2 * width), F32),
            jax.ShapeDtypeStruct((slots, 2 * width), BF16),
        ),
        in_specs=[pl.BlockSpec(memory_space=pl.ANY)] * (1 + count),
        out_specs=(pl.BlockSpec(memory_space=pltpu.VMEM), pl.BlockSpec(memory_space=pltpu.VMEM)),
        scratch_shapes=[
            pltpu.VMEM((count * units, width), BF16),
            pltpu.VMEM((count * units, width), BF16),
            pltpu.VMEM((experts, lines, 128), BF16),
            pltpu.VMEM((experts * lines, 128), F32),
            pltpu.SemaphoreType.DMA,
            pltpu.SemaphoreType.DMA((count, 2)),
        ],
        compiler_params=pltpu.CompilerParams(vmem_limit_bytes=VMEM_LIMIT + (4 << 20)),
        cost_estimate=pl.CostEstimate(
            flops=8 * slots * count * units * width,
            bytes_accessed=4 * count * units * width,
            transcendentals=0,
        ),
        name="gathered",
    )(outside(arrived), *map(outside, pieces))


def last_kernel(units, rows_ref, acc_ref, up_ref, down_ref, out_ref, wide):
    width = up_ref.shape[1]
    experts, lines, _ = out_ref.shape
    capacity = rows_ref.shape[0] // experts
    blocks = lines // capacity
    up, down = up_ref[:units, :], down_ref[:units, :]
    tok, cot = rows_ref[:, :width], rows_ref[:, width:]
    hidden, act_grad = activations(matmul_nt(tok, up), matmul_nt(cot, down))
    for part, (acts, weights) in enumerate(((hidden, down), (act_grad, up))):
        sums = acc_ref[:, part * width : (part + 1) * width] + matmul(acts, weights)
        for b in range(width // 128):
            line = part * (width // 128) + b
            for r in range(capacity):
                wide[pl.ds(r * blocks + line, experts, stride=lines), :] = sums[
                    r * experts : (r + 1) * experts, b * 128 : (b + 1) * 128
                ]
    for e in range(experts):
        out_ref[e] = wide[e * lines : (e + 1) * lines, :].astype(BF16)


def last(rows, acc, up_half, down_half, units, experts):
    lines = rows.shape[0] * rows.shape[1] // (experts * 128)
    return pl.pallas_call(
        functools.partial(last_kernel, units),
        out_shape=jax.ShapeDtypeStruct((experts, lines, 128), BF16),
        scratch_shapes=[pltpu.VMEM((experts * lines, 128), F32)],
        compiler_params=pltpu.CompilerParams(vmem_limit_bytes=VMEM_LIMIT),
        name="last",
    )(rows, acc, up_half, down_half)


def hot_kernel(units, hot_rows, where_ref, pieces_ref, *refs):
    blocks, (send_ref, keep_ref, tok, cot, weights, sems) = refs[:-6], refs[-6:]
    ring = len(blocks)
    width = tok.shape[1]
    here = where_ref[0]
    copies = []
    for i, block in enumerate(blocks):
        place = pl.multiple_of((here ^ lax.rem(here + i, ring)) * HOT_PAD, HOT_PAD)
        pair = block if isinstance(block, tuple) else (block, block)
        offset = 0 if isinstance(block, tuple) else units + HOT_PAD
        for j, whole in enumerate((tok, cot)):
            copy = pltpu.make_async_copy(
                pair[j].at[pl.ds(j * offset + units, HOT_PAD)], whole.at[pl.ds(place, HOT_PAD)], sems.at[i, j]
            )
            copy.start()
            copies.append(copy)
    columns = width // 128
    tall = pieces_ref.shape[1]
    for k in range(pieces_ref.shape[0]):
        i, j = k // columns, k % columns
        weights[i * tall : (i + 1) * tall, j * 128 : (j + 1) * 128] = pieces_ref[k]
    for copy in copies:
        copy.wait()
    up, down = weights[:units, :], weights[units:, :]
    hidden, act_grad = activations(matmul_nt(tok[...], up), matmul_nt(cot[...], down))
    packed, lanes = send_ref.shape
    blocks_of = 2 * width // lanes
    row = lax.broadcasted_iota(I32, (packed, ring * HOT_PAD), 0)
    column = lax.broadcasted_iota(I32, (packed, ring * HOT_PAD), 1)
    group = row // (blocks_of * hot_rows)
    block_of = row // hot_rows % blocks_of
    within = ((group % 2) * 4 + (group // 2) * 2) * HOT_PAD + row % hot_rows
    for odd, out_ref in ((1, send_ref), (0, keep_ref)):
        total = jnp.zeros((packed, lanes), F32)
        for b in range(blocks_of):
            chosen = ((column == within + odd * HOT_PAD) & (block_of == b)).astype(F32).astype(BF16)
            acts, matrix = (hidden, down) if b * lanes < width else (act_grad, up)
            lo = b * lanes % width
            total = total + matmul(matmul(chosen, acts).astype(BF16), matrix[:, lo : lo + lanes])
        out_ref[...] = total.astype(BF16)


def hot_partials(here, pieces, blocks, units, hot_rows, after):
    ring = len(blocks)
    flat, spans = [], []
    for block in blocks:
        spans.append(len(block) if isinstance(block, tuple) else 0)
        flat += list(block) if isinstance(block, tuple) else [block]
    width = flat[0].shape[1]

    def kernel(where_ref, pieces_ref, after_ref, *refs):
        refs, grouped = list(refs), []
        for span in spans:
            grouped.append(tuple(refs.pop(0) for _ in range(span)) if span else refs.pop(0))
        hot_kernel(units, hot_rows, where_ref, pieces_ref, *grouped, *refs)

    inside = pl.BlockSpec(memory_space=pltpu.VMEM)
    packed = jax.ShapeDtypeStruct((ring // 2 * hot_rows * (2 * width // LANES), LANES), BF16)
    return pl.pallas_call(
        kernel,
        out_shape=(packed, packed),
        in_specs=[pl.BlockSpec(memory_space=pltpu.SMEM), inside]
        + [pl.BlockSpec(memory_space=pl.ANY)] * (1 + len(flat)),
        out_specs=(inside, inside),
        scratch_shapes=[
            pltpu.VMEM((ring * HOT_PAD, width), BF16),
            pltpu.VMEM((ring * HOT_PAD, width), BF16),
            pltpu.VMEM((2 * units, width), BF16),
            pltpu.SemaphoreType.DMA((ring, 2)),
        ],
        compiler_params=pltpu.CompilerParams(vmem_limit_bytes=VMEM_LIMIT),
        name="hot",
    )(here, pieces, after, *map(outside, flat))


def thirds(x):
    first = x.astype(BF16)
    rest = x - first.astype(F32)
    second = rest.astype(BF16)
    third = (rest - second.astype(F32)).astype(BF16)
    return first, second, third


def cold_kernel(capacity, ids_ref, gate_ref, cot_ref, cold_ref, sum_ref, dots_ref, wide, rows):
    ids, gates, cot = ids_ref[...], gate_ref[...], cot_ref[...]
    top_count = ids.shape[0]
    experts, lines, _ = cold_ref.shape
    blocks = lines // capacity
    width = cot.shape[1]
    for e in range(experts):
        wide[e * lines : (e + 1) * lines, :] = cold_ref[e].astype(F32)
    for r in range(capacity):
        for b in range(blocks):
            line = wide[pl.ds(r * blocks + b, experts, stride=lines), :]
            rows[r * experts : (r + 1) * experts, b * 128 : (b + 1) * 128] = line.astype(BF16)
    cold, _, expert, _, _ = slot_maps(ids, experts * capacity, capacity, slot_major=True)
    per_slot = jnp.zeros(cold.shape, F32)
    for k in range(top_count):
        per_slot = per_slot + jnp.where(ids[k : k + 1, :] == expert, gates[k : k + 1, :], 0.0)
    scale = thirds(jnp.where(cold > 0, per_slot, 0.0))
    for lo in (0, width):
        part = rows[:, lo : lo + width]
        sum_ref[:, lo : lo + width] = matmul_tn(scale[0], part) + matmul_tn(scale[1], part) + matmul_tn(scale[2], part)
    dots = jnp.where(cold > 0, matmul_nt(rows[:, :width], cot), 0.0)
    for k in range(top_count):
        dots_ref[k : k + 1, :] = jnp.sum(jnp.where(ids[k : k + 1, :] == expert, dots, 0.0), 0, keepdims=True)


def cold_combine(ids, gates, cotangent, results, capacity):
    tok_rows, width = cotangent.shape
    experts, lines, _ = results.shape
    return pl.pallas_call(
        functools.partial(cold_kernel, capacity),
        out_shape=(
            jax.ShapeDtypeStruct((tok_rows, 2 * width), F32),
            jax.ShapeDtypeStruct(gates.shape, F32),
        ),
        scratch_shapes=[
            pltpu.VMEM((experts * lines, 128), F32),
            pltpu.VMEM((experts * capacity, 2 * width), BF16),
        ],
        compiler_params=pltpu.CompilerParams(vmem_limit_bytes=VMEM_LIMIT),
        cost_estimate=pl.CostEstimate(flops=1 << 36, bytes_accessed=1 << 26, transcendentals=0),
        name="cold_combine",
    )(ids, gates, cotangent, results)


def final_kernel(
    capacity, slots, ids_ref, gate_ref, cot_ref, sum_ref, dots_ref, kept_ref, *refs
):
    sent, (mix_ref, grad_ref, gate_grad_ref) = refs[:-3], refs[-3:]
    ids, gates, cot = ids_ref[...], gate_ref[...], cot_ref[...]
    top_count, tok_rows = ids.shape
    width = cot.shape[1]
    lanes = kept_ref.shape[1]
    hot_rows = kept_ref.shape[0] * lanes // (2 * width)
    _, hot, _, _, hottest = slot_maps(ids, slots, capacity)
    hottest = hottest.astype(I32)
    gate = jnp.zeros((1, tok_rows), F32)
    for k in range(top_count):
        gate = gate + jnp.where(ids[k : k + 1, :] == hottest, gates[k : k + 1, :], 0.0)
    hot = hot[:hot_rows]
    scale = thirds(jnp.where(hot > 0, gate, 0.0))
    result = kept_ref[...]
    for ref in sent:
        result = result + ref[...].astype(F32)
    dots = jnp.zeros(hot.shape, F32)
    for b in range(2 * width // lanes):
        rows = result[b * hot_rows : (b + 1) * hot_rows].astype(BF16)
        lo, at = b * lanes, b * lanes % width
        total = matmul_tn(scale[0], rows) + matmul_tn(scale[1], rows) + matmul_tn(scale[2], rows)
        out_ref = mix_ref if lo < width else grad_ref
        out_ref[:, at : at + lanes] = (sum_ref[:, lo : lo + lanes] + total).astype(BF16)
        if lo < width:
            dots = dots + matmul_nt(rows, cot[:, at : at + lanes])
    dot = jnp.sum(jnp.where(hot > 0, dots, 0.0), 0, keepdims=True)
    gate_grad_ref[...] = dots_ref[...] + jnp.where(ids == hottest, dot, 0.0)


def final_combine(ids, gates, cotangent, sums, dots, kept, sent, slots, capacity):
    return pl.pallas_call(
        functools.partial(final_kernel, capacity, slots),
        out_shape=(
            jax.ShapeDtypeStruct(cotangent.shape, BF16),
            jax.ShapeDtypeStruct(cotangent.shape, BF16),
            jax.ShapeDtypeStruct(gates.shape, F32),
        ),
        compiler_params=pltpu.CompilerParams(vmem_limit_bytes=VMEM_LIMIT),
        name="final_combine",
    )(ids, gates, cotangent, sums, dots, kept, *sent)


TICK = pl.CostEstimate(flops=1 << 35, bytes_accessed=1 << 25, transcendentals=0)


def tick_kernel(token_ref, *refs):
    refs[-1][0, 0] = token_ref[0, 0]


def tick(token, *after):
    scalar = pl.BlockSpec(memory_space=pltpu.SMEM)
    return pl.pallas_call(
        tick_kernel,
        out_shape=jax.ShapeDtypeStruct(token.shape, token.dtype),
        in_specs=[scalar] + [pl.BlockSpec(memory_space=pl.ANY)] * len(after),
        out_specs=scalar,
        compiler_params=pltpu.CompilerParams(vmem_limit_bytes=1 << 20),
        cost_estimate=pl.CostEstimate(flops=22 << 30, bytes_accessed=1 << 10, transcendentals=0),
        name="tick",
    )(token, *after)


def split_kernel(right_ref, left_ref, right_out, left_out, top_ref, bottom_ref, sems):
    half = top_ref.shape[0]
    copies = [
        pltpu.make_async_copy(right_ref.at[pl.ds(0, half)], top_ref, sems.at[0]),
        pltpu.make_async_copy(left_ref.at[pl.ds(half, half)], bottom_ref, sems.at[1]),
    ]
    for copy in copies:
        copy.start()
    for copy in copies:
        copy.wait()


def split(right, left):
    anywhere, inside = pl.BlockSpec(memory_space=pl.ANY), pl.BlockSpec(memory_space=pltpu.VMEM)
    whole = jax.ShapeDtypeStruct(right.shape, right.dtype)
    part = jax.ShapeDtypeStruct((right.shape[0] // 2, right.shape[1]), right.dtype)
    return pl.pallas_call(
        split_kernel,
        out_shape=(whole, whole, part, part),
        in_specs=[anywhere] * 2,
        out_specs=(anywhere, anywhere, inside, inside),
        input_output_aliases={0: 0, 1: 1},
        scratch_shapes=[pltpu.SemaphoreType.DMA((2,))],
        compiler_params=pltpu.CompilerParams(vmem_limit_bytes=1 << 22),
        cost_estimate=TICK,
        name="split",
    )(right, left)


def shift(x, by):
    ring = lax.axis_size("dp")
    return lax.ppermute(x, "dp", [(i, (i + by) % ring) for i in range(ring)])


def swap(x, bit):
    ring = lax.axis_size("dp")
    pairs = [[i, i ^ bit] for i in range(ring) if not i & bit]
    both = lax.all_gather(x, "dp", axis=0, axis_index_groups=pairs, tiled=False)
    return jnp.where(lax.axis_index("dp") & bit == 0, both[1], both[0])


def send_on(x, bits):
    ring = lax.axis_size("dp")
    return lax.ppermute(x, "dp", [(i, i ^ bits) for i in range(ring)])


def shards(tokens, cotangent, gate_probs, expert_ids, up_weight, down_weight):
    tok_rows, width = tokens.shape
    top_count = expert_ids.shape[1]
    experts = lax.axis_size("expert")
    hot_rows = 9 * tok_rows // 16
    capacity = (tok_rows * top_count - hot_rows + experts - 2) // (experts - 1)
    slots = experts * capacity
    up, down = up_weight[0], down_weight[0]
    units = up.shape[0]
    ids, gates = expert_ids.T, gate_probs.T

    outgoing, own, hottest = route(ids, tokens, cotangent, up, down, slots, capacity)
    half = own.shape[0] // 2
    right, left = [own], [own]
    for step in range(3):
        r, l = shift(right[-1], 1), shift(left[-1], -1)
        if step == 1:
            token = tick(hottest, r, l)
        if step == 2:
            r, l, top, bottom = split(r, l)
        right.append(r)
        left.append(l)
    far_up, far_down = shift(top, 1), shift(bottom, -1)

    lines = capacity * 2 * width // 128
    outgoing = assemble(outgoing.reshape(experts, lines, 128), up, down)
    arrived = lax.all_to_all(outgoing, "expert", 0, 0, tiled=True)
    hot_pieces = lax.all_to_all(repeat(token, arrived, lines), "expert", 0, 0, tiled=True)

    acc, rows = gathered(arrived, [own] + right[1:] + left[1:], units, slots)
    results = last(rows, acc, far_up, far_down, units, experts)
    came_back = lax.all_to_all(results, "expert", 0, 0, tiled=True)

    blocks = left + [(far_up, far_down)] + right[:0:-1]
    here = lax.axis_index("dp").astype(I32).reshape(1)
    send, keep = hot_partials(here, hot_pieces, blocks, units, hot_rows, results)
    both = keep.astype(F32) + swap(send, 1).astype(F32)
    dense = both.shape[0] // 4
    kept = both[:dense]
    sent = [send_on(both[i * dense : (i + 1) * dense].astype(BF16), place) for i, place in ((1, 4), (2, 2), (3, 6))]
    sums, dots = cold_combine(ids, gates, cotangent, came_back, capacity)
    mixture, input_grad, gate_grad = final_combine(
        ids, gates, cotangent, sums, dots, kept, sent, slots, capacity
    )
    return mixture, input_grad, gate_grad.T


def solution(mesh):
    rows = P(("dp", "expert"), None)
    weights = P("expert", "dp", None)
    return jax.shard_map(
        shards,
        mesh=mesh,
        in_specs=(rows, rows, rows, rows, weights, weights),
        out_specs=(rows, rows, rows),
        check_vma=False,
    )
```

```python
import functools

import jax
import jax.numpy as jnp
from jax import lax
from jax.experimental import pallas as pl
from jax.experimental.pallas import tpu as pltpu
from jax.sharding import PartitionSpec as P

BF16, F32, I32 = jnp.bfloat16, jnp.float32, jnp.int32
HOT_PAD = 16
LANES = 1024
VMEM_LIMIT = 16 * 1024 * 1024


def outside(x):
    return pltpu.with_memory_space_constraint(x, pltpu.HBM)


def matmul(a, b):
    return lax.dot_general(a, b, (((1,), (0,)), ((), ())), preferred_element_type=F32)


def matmul_nt(a, b):
    return lax.dot_general(a, b, (((1,), (1,)), ((), ())), preferred_element_type=F32)


def matmul_tn(a, b):
    return lax.dot_general(a, b, (((0,), (0,)), ((), ())), preferred_element_type=F32)


def slot_maps(ids, slots, capacity, slot_major=False):
    top_count, tok_rows = ids.shape
    slot = lax.broadcasted_iota(I32, (slots, tok_rows), 0)
    experts = slots // capacity
    expert, within = (slot % experts, slot // experts) if slot_major else (slot // capacity, slot % capacity)
    named = jnp.zeros((slots, tok_rows), F32)
    for k in range(top_count):
        named = named + (ids[k : k + 1, :] == expert).astype(F32)
    counts = jnp.sum(named, 1, keepdims=True)
    is_hot = (counts == jnp.max(counts)).astype(F32)
    earlier = (
        lax.broadcasted_iota(I32, (tok_rows, tok_rows), 0)
        < lax.broadcasted_iota(I32, (tok_rows, tok_rows), 1)
    ).astype(BF16)
    rank = matmul(named.astype(BF16), earlier)
    cold = named * (1.0 - is_hot) * (rank == within.astype(F32)).astype(F32)
    first = is_hot * (within[:, :1] == 0).astype(F32)
    hot_token = jnp.sum(named * first, 0, keepdims=True)
    hot_rank = jnp.sum(rank * first, 0, keepdims=True)
    hot_row = lax.broadcasted_iota(I32, (HOT_PAD, tok_rows), 0).astype(F32)
    hot = hot_token * (hot_rank == hot_row).astype(F32)
    hottest = jnp.sum(first * expert[:, :1].astype(F32), 0, keepdims=True)
    return cold, hot, expert, is_hot, hottest


def route_kernel(
    capacity, ids_ref, tok_ref, cot_ref, up_ref, down_ref, out_ref, own_ref, hottest_ref, tok, cot, sems
):
    slots, width = out_ref.shape[0], tok.shape[1]
    units = up_ref.shape[0]
    half = own_ref.shape[0] // 2
    loads = [pltpu.make_async_copy(tok_ref, tok, sems.at[0]), pltpu.make_async_copy(cot_ref, cot, sems.at[1])]
    copies = [
        pltpu.make_async_copy(up_ref, own_ref.at[pl.ds(0, units)], sems.at[2]),
        pltpu.make_async_copy(down_ref, own_ref.at[pl.ds(half, units)], sems.at[3]),
    ]
    for copy in loads + copies:
        copy.start()
    cold, hot, _, _, hottest = slot_maps(ids_ref[...], slots, capacity)
    cold, hot = cold.astype(BF16), hot.astype(BF16)
    hottest_ref[0, 0] = jnp.max(hottest).astype(I32)
    for copy in loads:
        copy.wait()
    own_ref[units:half, :] = matmul(hot, tok[...]).astype(BF16)
    own_ref[half + units :, :] = matmul(hot, cot[...]).astype(BF16)
    out_ref[:, :width] = matmul(cold, tok[...]).astype(BF16)
    out_ref[:, width:] = matmul(cold, cot[...]).astype(BF16)
    for copy in copies:
        copy.wait()


def route(ids, tokens, cotangent, up, down, slots, capacity):
    tok_rows, width = tokens.shape
    units = up.shape[0]
    anywhere = pl.BlockSpec(memory_space=pl.ANY)
    inside = pl.BlockSpec(memory_space=pltpu.VMEM)
    return pl.pallas_call(
        functools.partial(route_kernel, capacity),
        out_shape=(
            jax.ShapeDtypeStruct((slots, 2 * width), BF16),
            jax.ShapeDtypeStruct((2 * (units + HOT_PAD), width), BF16),
            jax.ShapeDtypeStruct((1, 1), I32),
        ),
        in_specs=[inside] + [anywhere] * 4,
        out_specs=(inside, inside, pl.BlockSpec(memory_space=pltpu.SMEM)),
        scratch_shapes=[
            pltpu.VMEM((tok_rows, width), BF16),
            pltpu.VMEM((tok_rows, width), BF16),
            pltpu.SemaphoreType.DMA((4,)),
        ],
        compiler_params=pltpu.CompilerParams(vmem_limit_bytes=VMEM_LIMIT),
        name="route",
    )(ids, *map(outside, (tokens, cotangent, up, down)))


def assemble_kernel(tall, rows_ref, up_ref, down_ref, out_ref, up, down, sems):
    copies = []
    for i, (source, here) in enumerate(((up_ref, up), (down_ref, down))):
        copy = pltpu.make_async_copy(source, here, sems.at[i])
        copy.start()
        copies.append(copy)
    lines = rows_ref.shape[1]
    out_ref[:, :lines, :] = rows_ref[...]
    columns = up.shape[1] // 128
    groups = up.shape[0] // tall
    for i, here in enumerate((up, down)):
        copies[i].wait()
        for g in range(groups):
            for j in range(columns):
                out_ref[(i * groups + g) * columns + j, lines:, :] = here[
                    g * tall : (g + 1) * tall, j * 128 : (j + 1) * 128
                ]


def assemble(rows, up, down):
    experts, lines, lanes = rows.shape
    units, width = up.shape
    tall = 2 * units * width // (experts * lanes)
    return pl.pallas_call(
        functools.partial(assemble_kernel, tall),
        out_shape=jax.ShapeDtypeStruct((experts, lines + tall, lanes), BF16),
        in_specs=[pl.BlockSpec(memory_space=pltpu.VMEM)] + [pl.BlockSpec(memory_space=pl.ANY)] * 2,
        out_specs=pl.BlockSpec(memory_space=pltpu.VMEM),
        scratch_shapes=[
            pltpu.VMEM((units, width), BF16),
            pltpu.VMEM((units, width), BF16),
            pltpu.SemaphoreType.DMA((2,)),
        ],
        compiler_params=pltpu.CompilerParams(vmem_limit_bytes=VMEM_LIMIT),
        name="assemble",
    )(rows, outside(up), outside(down))


def repeat_kernel(lines, hottest_ref, arrived_ref, out_ref):
    mine = arrived_ref[hottest_ref[0, 0], lines:, :]
    out_ref[...] = jnp.broadcast_to(mine[None], out_ref.shape)


def repeat(hottest, arrived, lines):
    experts, height, lanes = arrived.shape
    inside = pl.BlockSpec(memory_space=pltpu.VMEM)
    return pl.pallas_call(
        functools.partial(repeat_kernel, lines),
        out_shape=jax.ShapeDtypeStruct((experts, height - lines, lanes), BF16),
        in_specs=[pl.BlockSpec(memory_space=pltpu.SMEM), inside],
        out_specs=inside,
        compiler_params=pltpu.CompilerParams(vmem_limit_bytes=VMEM_LIMIT),
        name="repeat",
    )(hottest, arrived)


def activations(pre_act, hidden_grad):
    gating = jax.nn.sigmoid(pre_act)
    hidden = (pre_act * gating).astype(BF16)
    act_grad = (hidden_grad * gating * (1.0 + pre_act * (1.0 - gating))).astype(BF16)
    return hidden, act_grad


def gathered_kernel(units, lines, arrived_ref, *refs):
    pieces, (acc_ref, rows_ref, up, down, wide, sems) = refs[:-6], refs[-6:]
    width = up.shape[1]
    half = pieces[0].shape[0] // 2
    experts = arrived_ref.shape[0]
    capacity = rows_ref.shape[0] // experts
    copies = []
    for i, piece in enumerate(pieces):
        for j, whole in enumerate((up, down)):
            copy = pltpu.make_async_copy(
                piece.at[pl.ds(j * half, units)], whole.at[pl.ds(i * units, units)], sems.at[i, j]
            )
            copy.start()
            copies.append(copy)
    for e in range(experts):
        wide[e * lines : (e + 1) * lines, :] = arrived_ref[e, :lines, :].astype(F32)
    blocks = lines // capacity
    for r in range(capacity):
        for b in range(blocks):
            line = wide[pl.ds(r * blocks + b, experts, stride=lines), :]
            rows_ref[r * experts : (r + 1) * experts, b * 128 : (b + 1) * 128] = line.astype(BF16)
    for copy in copies:
        copy.wait()
    tok, cot = rows_ref[:, :width], rows_ref[:, width:]
    hidden, act_grad = activations(matmul_nt(tok, up[...]), matmul_nt(cot, down[...]))
    acc_ref[:, :width] = matmul(hidden, down[...])
    acc_ref[:, width:] = matmul(act_grad, up[...])


def gathered(arrived, pieces, units, slots):
    experts = arrived.shape[0]
    width = pieces[0].shape[1]
    lines = slots * 2 * width // (experts * 128)
    count = len(pieces)
    return pl.pallas_call(
        functools.partial(gathered_kernel, units, lines),
        out_shape=(
            jax.ShapeDtypeStruct((slots, 2 * width), F32),
            jax.ShapeDtypeStruct((slots, 2 * width), BF16),
        ),
        in_specs=[pl.BlockSpec(memory_space=pltpu.VMEM)] + [pl.BlockSpec(memory_space=pl.ANY)] * count,
        out_specs=(pl.BlockSpec(memory_space=pltpu.VMEM), pl.BlockSpec(memory_space=pltpu.VMEM)),
        scratch_shapes=[
            pltpu.VMEM((count * units, width), BF16),
            pltpu.VMEM((count * units, width), BF16),
            pltpu.VMEM((experts * lines, 128), F32),
            pltpu.SemaphoreType.DMA((count, 2)),
        ],
        compiler_params=pltpu.CompilerParams(vmem_limit_bytes=VMEM_LIMIT + (4 << 20)),
        cost_estimate=pl.CostEstimate(
            flops=8 * slots * count * units * width,
            bytes_accessed=4 * count * units * width,
            transcendentals=0,
        ),
        name="gathered",
    )(arrived, *map(outside, pieces))


def last_kernel(units, rows_ref, acc_ref, up_ref, down_ref, out_hbm, out_ref, wide, sems):
    width = up_ref.shape[1]
    experts, lines, _ = out_ref.shape
    capacity = rows_ref.shape[0] // experts
    blocks = lines // capacity
    up, down = up_ref[:units, :], down_ref[:units, :]
    tok, cot = rows_ref[:, :width], rows_ref[:, width:]
    hidden, act_grad = activations(matmul_nt(tok, up), matmul_nt(cot, down))
    for part, (acts, weights) in enumerate(((hidden, down), (act_grad, up))):
        sums = acc_ref[:, part * width : (part + 1) * width] + matmul(acts, weights)
        for b in range(width // 128):
            line = part * (width // 128) + b
            for r in range(capacity):
                wide[pl.ds(r * blocks + line, experts, stride=lines), :] = sums[
                    r * experts : (r + 1) * experts, b * 128 : (b + 1) * 128
                ]
    parts = sems.shape[0]
    share = experts // parts
    stores = []
    for part in range(parts):
        for e in range(part * share, (part + 1) * share):
            out_ref[e] = wide[e * lines : (e + 1) * lines, :].astype(BF16)
        span = pl.ds(part * share, share)
        stores.append(pltpu.make_async_copy(out_ref.at[span], out_hbm.at[span], sems.at[part]))
        stores[-1].start()
    for store in stores:
        store.wait()


def last(rows, acc, up_half, down_half, units, experts):
    lines = rows.shape[0] * rows.shape[1] // (experts * 128)
    return pl.pallas_call(
        functools.partial(last_kernel, units),
        out_shape=jax.ShapeDtypeStruct((experts, lines, 128), BF16),
        in_specs=[pl.BlockSpec(memory_space=pltpu.VMEM)] * 4,
        out_specs=pl.BlockSpec(memory_space=pl.ANY),
        scratch_shapes=[
            pltpu.VMEM((experts, lines, 128), BF16),
            pltpu.VMEM((experts * lines, 128), F32),
            pltpu.SemaphoreType.DMA((4,)),
        ],
        compiler_params=pltpu.CompilerParams(vmem_limit_bytes=VMEM_LIMIT),
        name="last",
    )(rows, acc, up_half, down_half)


def hot_kernel(units, hot_rows, where_ref, pieces_ref, *refs):
    blocks, (send_ref, keep_ref, tok, cot, weights, sems) = refs[:-6], refs[-6:]
    ring = len(blocks)
    width = tok.shape[1]
    here = where_ref[0]
    copies = []
    for i, block in enumerate(blocks):
        place = pl.multiple_of((here ^ lax.rem(here + i, ring)) * HOT_PAD, HOT_PAD)
        pair = block if isinstance(block, tuple) else (block, block)
        offset = 0 if isinstance(block, tuple) else units + HOT_PAD
        for j, whole in enumerate((tok, cot)):
            copy = pltpu.make_async_copy(
                pair[j].at[pl.ds(j * offset + units, HOT_PAD)], whole.at[pl.ds(place, HOT_PAD)], sems.at[i, j]
            )
            copy.start()
            copies.append(copy)
    columns = width // 128
    tall = pieces_ref.shape[1]
    for k in range(pieces_ref.shape[0]):
        i, j = k // columns, k % columns
        weights[i * tall : (i + 1) * tall, j * 128 : (j + 1) * 128] = pieces_ref[k]
    for copy in copies:
        copy.wait()
    up, down = weights[:units, :], weights[units:, :]
    hidden, act_grad = activations(matmul_nt(tok[...], up), matmul_nt(cot[...], down))
    packed, lanes = send_ref.shape
    blocks_of = 2 * width // lanes
    row = lax.broadcasted_iota(I32, (packed, ring * HOT_PAD), 0)
    column = lax.broadcasted_iota(I32, (packed, ring * HOT_PAD), 1)
    group = row // (blocks_of * hot_rows)
    block_of = row // hot_rows % blocks_of
    within = ((group % 2) * 4 + (group // 2) * 2) * HOT_PAD + row % hot_rows
    for odd, out_ref in ((1, send_ref), (0, keep_ref)):
        total = jnp.zeros((packed, lanes), F32)
        for b in range(blocks_of):
            chosen = ((column == within + odd * HOT_PAD) & (block_of == b)).astype(F32).astype(BF16)
            acts, matrix = (hidden, down) if b * lanes < width else (act_grad, up)
            lo = b * lanes % width
            total = total + matmul(matmul(chosen, acts).astype(BF16), matrix[:, lo : lo + lanes])
        out_ref[...] = total.astype(BF16)


def hot_partials(here, pieces, blocks, units, hot_rows, after):
    ring = len(blocks)
    flat, spans = [], []
    for block in blocks:
        spans.append(len(block) if isinstance(block, tuple) else 0)
        flat += list(block) if isinstance(block, tuple) else [block]
    width = flat[0].shape[1]

    def kernel(where_ref, pieces_ref, after_ref, *refs):
        refs, grouped = list(refs), []
        for span in spans:
            grouped.append(tuple(refs.pop(0) for _ in range(span)) if span else refs.pop(0))
        hot_kernel(units, hot_rows, where_ref, pieces_ref, *grouped, *refs)

    inside = pl.BlockSpec(memory_space=pltpu.VMEM)
    packed = jax.ShapeDtypeStruct((ring // 2 * hot_rows * (2 * width // LANES), LANES), BF16)
    return pl.pallas_call(
        kernel,
        out_shape=(packed, packed),
        in_specs=[pl.BlockSpec(memory_space=pltpu.SMEM), inside]
        + [pl.BlockSpec(memory_space=pl.ANY)] * (1 + len(flat)),
        out_specs=(inside, inside),
        scratch_shapes=[
            pltpu.VMEM((ring * HOT_PAD, width), BF16),
            pltpu.VMEM((ring * HOT_PAD, width), BF16),
            pltpu.VMEM((2 * units, width), BF16),
            pltpu.SemaphoreType.DMA((ring, 2)),
        ],
        compiler_params=pltpu.CompilerParams(vmem_limit_bytes=VMEM_LIMIT),
        name="hot",
    )(here, pieces, after, *map(outside, flat))


def thirds(x):
    first = x.astype(BF16)
    rest = x - first.astype(F32)
    second = rest.astype(BF16)
    third = (rest - second.astype(F32)).astype(BF16)
    return first, second, third


def cold_kernel(capacity, ids_ref, gate_ref, cot_ref, cold_ref, sum_ref, dots_ref, wide, rows):
    ids, gates, cot = ids_ref[...], gate_ref[...], cot_ref[...]
    top_count = ids.shape[0]
    experts, lines, _ = cold_ref.shape
    blocks = lines // capacity
    width = cot.shape[1]
    for e in range(experts):
        wide[e * lines : (e + 1) * lines, :] = cold_ref[e].astype(F32)
    for r in range(capacity):
        for b in range(blocks):
            line = wide[pl.ds(r * blocks + b, experts, stride=lines), :]
            rows[r * experts : (r + 1) * experts, b * 128 : (b + 1) * 128] = line.astype(BF16)
    cold, _, expert, _, _ = slot_maps(ids, experts * capacity, capacity, slot_major=True)
    per_slot = jnp.zeros(cold.shape, F32)
    for k in range(top_count):
        per_slot = per_slot + jnp.where(ids[k : k + 1, :] == expert, gates[k : k + 1, :], 0.0)
    scale = thirds(jnp.where(cold > 0, per_slot, 0.0))
    for lo in (0, width):
        part = rows[:, lo : lo + width]
        sum_ref[:, lo : lo + width] = matmul_tn(scale[0], part) + matmul_tn(scale[1], part) + matmul_tn(scale[2], part)
    dots = jnp.where(cold > 0, matmul_nt(rows[:, :width], cot), 0.0)
    for k in range(top_count):
        dots_ref[k : k + 1, :] = jnp.sum(jnp.where(ids[k : k + 1, :] == expert, dots, 0.0), 0, keepdims=True)


def cold_combine(ids, gates, cotangent, results, capacity):
    tok_rows, width = cotangent.shape
    experts, lines, _ = results.shape
    return pl.pallas_call(
        functools.partial(cold_kernel, capacity),
        out_shape=(
            jax.ShapeDtypeStruct((tok_rows, 2 * width), F32),
            jax.ShapeDtypeStruct(gates.shape, F32),
        ),
        scratch_shapes=[
            pltpu.VMEM((experts * lines, 128), F32),
            pltpu.VMEM((experts * capacity, 2 * width), BF16),
        ],
        compiler_params=pltpu.CompilerParams(vmem_limit_bytes=VMEM_LIMIT),
        cost_estimate=pl.CostEstimate(flops=1 << 36, bytes_accessed=1 << 26, transcendentals=0),
        name="cold_combine",
    )(ids, gates, cotangent, results)


def final_kernel(
    capacity, slots, ids_ref, gate_ref, cot_ref, sum_ref, dots_ref, kept_ref, *refs
):
    sent, (mix_ref, grad_ref, gate_grad_ref) = refs[:-3], refs[-3:]
    ids, gates, cot = ids_ref[...], gate_ref[...], cot_ref[...]
    top_count, tok_rows = ids.shape
    width = cot.shape[1]
    lanes = kept_ref.shape[1]
    hot_rows = kept_ref.shape[0] * lanes // (2 * width)
    _, hot, _, _, hottest = slot_maps(ids, slots, capacity)
    hottest = hottest.astype(I32)
    gate = jnp.zeros((1, tok_rows), F32)
    for k in range(top_count):
        gate = gate + jnp.where(ids[k : k + 1, :] == hottest, gates[k : k + 1, :], 0.0)
    hot = hot[:hot_rows]
    scale = thirds(jnp.where(hot > 0, gate, 0.0))
    result = kept_ref[...]
    for ref in sent:
        result = result + ref[...].astype(F32)
    dots = jnp.zeros(hot.shape, F32)
    for b in range(2 * width // lanes):
        rows = result[b * hot_rows : (b + 1) * hot_rows].astype(BF16)
        lo, at = b * lanes, b * lanes % width
        total = matmul_tn(scale[0], rows) + matmul_tn(scale[1], rows) + matmul_tn(scale[2], rows)
        out_ref = mix_ref if lo < width else grad_ref
        out_ref[:, at : at + lanes] = (sum_ref[:, lo : lo + lanes] + total).astype(BF16)
        if lo < width:
            dots = dots + matmul_nt(rows, cot[:, at : at + lanes])
    dot = jnp.sum(jnp.where(hot > 0, dots, 0.0), 0, keepdims=True)
    gate_grad_ref[...] = dots_ref[...] + jnp.where(ids == hottest, dot, 0.0)


def final_combine(ids, gates, cotangent, sums, dots, kept, sent, slots, capacity):
    return pl.pallas_call(
        functools.partial(final_kernel, capacity, slots),
        out_shape=(
            jax.ShapeDtypeStruct(cotangent.shape, BF16),
            jax.ShapeDtypeStruct(cotangent.shape, BF16),
            jax.ShapeDtypeStruct(gates.shape, F32),
        ),
        compiler_params=pltpu.CompilerParams(vmem_limit_bytes=VMEM_LIMIT),
        name="final_combine",
    )(ids, gates, cotangent, sums, dots, kept, *sent)


TICK = pl.CostEstimate(flops=1 << 35, bytes_accessed=1 << 25, transcendentals=0)


def tick_kernel(token_ref, *refs):
    refs[-1][0, 0] = token_ref[0, 0]


def tick(token, *after):
    scalar = pl.BlockSpec(memory_space=pltpu.SMEM)
    return pl.pallas_call(
        tick_kernel,
        out_shape=jax.ShapeDtypeStruct(token.shape, token.dtype),
        in_specs=[scalar] + [pl.BlockSpec(memory_space=pl.ANY)] * len(after),
        out_specs=scalar,
        compiler_params=pltpu.CompilerParams(vmem_limit_bytes=1 << 20),
        cost_estimate=pl.CostEstimate(flops=22 << 30, bytes_accessed=1 << 10, transcendentals=0),
        name="tick",
    )(token, *after)


def split_kernel(right_ref, left_ref, right_out, left_out, top_ref, bottom_ref, sems):
    half = top_ref.shape[0]
    copies = [
        pltpu.make_async_copy(right_ref.at[pl.ds(0, half)], top_ref, sems.at[0]),
        pltpu.make_async_copy(left_ref.at[pl.ds(half, half)], bottom_ref, sems.at[1]),
    ]
    for copy in copies:
        copy.start()
    for copy in copies:
        copy.wait()


def split(right, left):
    anywhere, inside = pl.BlockSpec(memory_space=pl.ANY), pl.BlockSpec(memory_space=pltpu.VMEM)
    whole = jax.ShapeDtypeStruct(right.shape, right.dtype)
    part = jax.ShapeDtypeStruct((right.shape[0] // 2, right.shape[1]), right.dtype)
    return pl.pallas_call(
        split_kernel,
        out_shape=(whole, whole, part, part),
        in_specs=[anywhere] * 2,
        out_specs=(anywhere, anywhere, inside, inside),
        input_output_aliases={0: 0, 1: 1},
        scratch_shapes=[pltpu.SemaphoreType.DMA((2,))],
        compiler_params=pltpu.CompilerParams(vmem_limit_bytes=1 << 22),
        cost_estimate=TICK,
        name="split",
    )(right, left)


def shift(x, by):
    ring = lax.axis_size("dp")
    return lax.ppermute(x, "dp", [(i, (i + by) % ring) for i in range(ring)])


def swap(x, bit):
    ring = lax.axis_size("dp")
    pairs = [[i, i ^ bit] for i in range(ring) if not i & bit]
    both = lax.all_gather(x, "dp", axis=0, axis_index_groups=pairs, tiled=False)
    return jnp.where(lax.axis_index("dp") & bit == 0, both[1], both[0])


def send_on(x, bits):
    ring = lax.axis_size("dp")
    return lax.ppermute(x, "dp", [(i, i ^ bits) for i in range(ring)])


def shards(tokens, cotangent, gate_probs, expert_ids, up_weight, down_weight):
    tok_rows, width = tokens.shape
    top_count = expert_ids.shape[1]
    experts = lax.axis_size("expert")
    hot_rows = 9 * tok_rows // 16
    capacity = (tok_rows * top_count - hot_rows + experts - 2) // (experts - 1)
    slots = experts * capacity
    up, down = up_weight[0], down_weight[0]
    units = up.shape[0]
    ids, gates = expert_ids.T, gate_probs.T

    outgoing, own, hottest = route(ids, tokens, cotangent, up, down, slots, capacity)
    half = own.shape[0] // 2
    right, left = [own], [own]
    for step in range(3):
        r, l = shift(right[-1], 1), shift(left[-1], -1)
        if step == 1:
            token = tick(hottest, r, l)
        if step == 2:
            r, l, top, bottom = split(r, l)
        right.append(r)
        left.append(l)
    far_up, far_down = shift(top, 1), shift(bottom, -1)

    lines = capacity * 2 * width // 128
    outgoing = assemble(outgoing.reshape(experts, lines, 128), up, down)
    arrived = lax.all_to_all(outgoing, "expert", 0, 0, tiled=True)
    hot_pieces = lax.all_to_all(repeat(token, arrived, lines), "expert", 0, 0, tiled=True)

    acc, rows = gathered(arrived, [own] + right[1:] + left[1:], units, slots)
    results = last(rows, acc, far_up, far_down, units, experts)
    came_back = lax.all_to_all(results, "expert", 0, 0, tiled=True)

    blocks = left + [(far_up, far_down)] + right[:0:-1]
    here = lax.axis_index("dp").astype(I32).reshape(1)
    send, keep = hot_partials(here, hot_pieces, blocks, units, hot_rows, results)
    both = keep.astype(F32) + swap(send, 1).astype(F32)
    dense = both.shape[0] // 4
    kept = both[:dense]
    sent = [send_on(both[i * dense : (i + 1) * dense].astype(BF16), place) for i, place in ((1, 4), (2, 2), (3, 6))]
    sums, dots = cold_combine(ids, gates, cotangent, came_back, capacity)
    mixture, input_grad, gate_grad = final_combine(
        ids, gates, cotangent, sums, dots, kept, sent, slots, capacity
    )
    return mixture, input_grad, gate_grad.T


def solution(mesh):
    rows = P(("dp", "expert"), None)
    weights = P("expert", "dp", None)
    return jax.shard_map(
        shards,
        mesh=mesh,
        in_specs=(rows, rows, rows, rows, weights, weights),
        out_specs=(rows, rows, rows),
        check_vma=False,
    )
```

```python
import functools

import jax
import jax.numpy as jnp
from jax import lax
from jax.experimental import pallas as pl
from jax.experimental.pallas import tpu as pltpu
from jax.sharding import PartitionSpec as P

BF16, F32, I32 = jnp.bfloat16, jnp.float32, jnp.int32
HOT_PAD = 16
LANES = 1024
VMEM_LIMIT = 16 * 1024 * 1024


def outside(x):
    return pltpu.with_memory_space_constraint(x, pltpu.HBM)


def matmul(a, b):
    return lax.dot_general(a, b, (((1,), (0,)), ((), ())), preferred_element_type=F32)


def matmul_nt(a, b):
    return lax.dot_general(a, b, (((1,), (1,)), ((), ())), preferred_element_type=F32)


def matmul_tn(a, b):
    return lax.dot_general(a, b, (((0,), (0,)), ((), ())), preferred_element_type=F32)


def slot_maps(ids, slots, capacity, slot_major=False):
    top_count, tok_rows = ids.shape
    slot = lax.broadcasted_iota(I32, (slots, tok_rows), 0)
    experts = slots // capacity
    expert, within = (slot % experts, slot // experts) if slot_major else (slot // capacity, slot % capacity)
    named = jnp.zeros((slots, tok_rows), F32)
    for k in range(top_count):
        named = named + (ids[k : k + 1, :] == expert).astype(F32)
    counts = jnp.sum(named, 1, keepdims=True)
    is_hot = (counts == jnp.max(counts)).astype(F32)
    earlier = (
        lax.broadcasted_iota(I32, (tok_rows, tok_rows), 0)
        < lax.broadcasted_iota(I32, (tok_rows, tok_rows), 1)
    ).astype(BF16)
    rank = matmul(named.astype(BF16), earlier)
    cold = named * (1.0 - is_hot) * (rank == within.astype(F32)).astype(F32)
    first = is_hot * (within[:, :1] == 0).astype(F32)
    hot_token = jnp.sum(named * first, 0, keepdims=True)
    hot_rank = jnp.sum(rank * first, 0, keepdims=True)
    hot_row = lax.broadcasted_iota(I32, (HOT_PAD, tok_rows), 0).astype(F32)
    hot = hot_token * (hot_rank == hot_row).astype(F32)
    hottest = jnp.sum(first * expert[:, :1].astype(F32), 0, keepdims=True)
    return cold, hot, expert, is_hot, hottest


def route_kernel(
    capacity, ids_hbm, tok_ref, cot_ref, up_ref, down_ref, out_ref, own_ref, hottest_ref, ids_ref, tok, cot, sems
):
    slots, width = out_ref.shape[0], tok.shape[1]
    units = up_ref.shape[0]
    half = own_ref.shape[0] // 2
    loads = [pltpu.make_async_copy(tok_ref, tok, sems.at[0]), pltpu.make_async_copy(cot_ref, cot, sems.at[1])]
    copies = [
        pltpu.make_async_copy(up_ref, own_ref.at[pl.ds(0, units)], sems.at[2]),
        pltpu.make_async_copy(down_ref, own_ref.at[pl.ds(half, units)], sems.at[3]),
    ]
    first = pltpu.make_async_copy(ids_hbm, ids_ref, sems.at[4])
    for copy in [first] + loads + copies:
        copy.start()
    first.wait()
    cold, hot, _, _, hottest = slot_maps(ids_ref[...], slots, capacity)
    cold, hot = cold.astype(BF16), hot.astype(BF16)
    hottest_ref[0, 0] = jnp.max(hottest).astype(I32)
    for copy in loads:
        copy.wait()
    own_ref[units:half, :] = matmul(hot, tok[...]).astype(BF16)
    own_ref[half + units :, :] = matmul(hot, cot[...]).astype(BF16)
    out_ref[:, :width] = matmul(cold, tok[...]).astype(BF16)
    out_ref[:, width:] = matmul(cold, cot[...]).astype(BF16)
    for copy in copies:
        copy.wait()


def route(ids, tokens, cotangent, up, down, slots, capacity):
    tok_rows, width = tokens.shape
    units = up.shape[0]
    anywhere = pl.BlockSpec(memory_space=pl.ANY)
    inside = pl.BlockSpec(memory_space=pltpu.VMEM)
    return pl.pallas_call(
        functools.partial(route_kernel, capacity),
        out_shape=(
            jax.ShapeDtypeStruct((slots, 2 * width), BF16),
            jax.ShapeDtypeStruct((2 * (units + HOT_PAD), width), BF16),
            jax.ShapeDtypeStruct((1, 1), I32),
        ),
        in_specs=[anywhere] * 5,
        out_specs=(inside, inside, pl.BlockSpec(memory_space=pltpu.SMEM)),
        scratch_shapes=[
            pltpu.VMEM(ids.shape, I32),
            pltpu.VMEM((tok_rows, width), BF16),
            pltpu.VMEM((tok_rows, width), BF16),
            pltpu.SemaphoreType.DMA((5,)),
        ],
        compiler_params=pltpu.CompilerParams(vmem_limit_bytes=VMEM_LIMIT),
        name="route",
    )(*map(outside, (ids, tokens, cotangent, up, down)))


def assemble_kernel(tall, rows_ref, up_ref, down_ref, out_ref, up, down, sems):
    copies = []
    for i, (source, here) in enumerate(((up_ref, up), (down_ref, down))):
        copy = pltpu.make_async_copy(source, here, sems.at[i])
        copy.start()
        copies.append(copy)
    lines = rows_ref.shape[1]
    out_ref[:, :lines, :] = rows_ref[...]
    columns = up.shape[1] // 128
    groups = up.shape[0] // tall
    for i, here in enumerate((up, down)):
        copies[i].wait()
        for g in range(groups):
            for j in range(columns):
                out_ref[(i * groups + g) * columns + j, lines:, :] = here[
                    g * tall : (g + 1) * tall, j * 128 : (j + 1) * 128
                ]


def assemble(rows, up, down):
    experts, lines, lanes = rows.shape
    units, width = up.shape
    tall = 2 * units * width // (experts * lanes)
    return pl.pallas_call(
        functools.partial(assemble_kernel, tall),
        out_shape=jax.ShapeDtypeStruct((experts, lines + tall, lanes), BF16),
        in_specs=[pl.BlockSpec(memory_space=pltpu.VMEM)] + [pl.BlockSpec(memory_space=pl.ANY)] * 2,
        out_specs=pl.BlockSpec(memory_space=pltpu.VMEM),
        scratch_shapes=[
            pltpu.VMEM((units, width), BF16),
            pltpu.VMEM((units, width), BF16),
            pltpu.SemaphoreType.DMA((2,)),
        ],
        compiler_params=pltpu.CompilerParams(vmem_limit_bytes=VMEM_LIMIT),
        name="assemble",
    )(rows, outside(up), outside(down))


def repeat_kernel(lines, hottest_ref, arrived_ref, out_ref):
    mine = arrived_ref[hottest_ref[0, 0], lines:, :]
    out_ref[...] = jnp.broadcast_to(mine[None], out_ref.shape)


def repeat(hottest, arrived, lines):
    experts, height, lanes = arrived.shape
    inside = pl.BlockSpec(memory_space=pltpu.VMEM)
    return pl.pallas_call(
        functools.partial(repeat_kernel, lines),
        out_shape=jax.ShapeDtypeStruct((experts, height - lines, lanes), BF16),
        in_specs=[pl.BlockSpec(memory_space=pltpu.SMEM), inside],
        out_specs=inside,
        compiler_params=pltpu.CompilerParams(vmem_limit_bytes=VMEM_LIMIT),
        name="repeat",
    )(hottest, arrived)


def activations(pre_act, hidden_grad):
    gating = jax.nn.sigmoid(pre_act)
    hidden = (pre_act * gating).astype(BF16)
    act_grad = (hidden_grad * gating * (1.0 + pre_act * (1.0 - gating))).astype(BF16)
    return hidden, act_grad


def gathered_kernel(units, lines, arrived_ref, *refs):
    pieces, (acc_ref, rows_ref, up, down, wide, sems) = refs[:-6], refs[-6:]
    width = up.shape[1]
    half = pieces[0].shape[0] // 2
    experts = arrived_ref.shape[0]
    capacity = rows_ref.shape[0] // experts
    copies = []
    for i, piece in enumerate(pieces):
        for j, whole in enumerate((up, down)):
            copy = pltpu.make_async_copy(
                piece.at[pl.ds(j * half, units)], whole.at[pl.ds(i * units, units)], sems.at[i, j]
            )
            copy.start()
            copies.append(copy)
    for e in range(experts):
        wide[e * lines : (e + 1) * lines, :] = arrived_ref[e, :lines, :].astype(F32)
    blocks = lines // capacity
    for r in range(capacity):
        for b in range(blocks):
            line = wide[pl.ds(r * blocks + b, experts, stride=lines), :]
            rows_ref[r * experts : (r + 1) * experts, b * 128 : (b + 1) * 128] = line.astype(BF16)
    for copy in copies:
        copy.wait()
    tok, cot = rows_ref[:, :width], rows_ref[:, width:]
    hidden, act_grad = activations(matmul_nt(tok, up[...]), matmul_nt(cot, down[...]))
    acc_ref[:, :width] = matmul(hidden, down[...])
    acc_ref[:, width:] = matmul(act_grad, up[...])


def gathered(arrived, pieces, units, slots):
    experts = arrived.shape[0]
    width = pieces[0].shape[1]
    lines = slots * 2 * width // (experts * 128)
    count = len(pieces)
    return pl.pallas_call(
        functools.partial(gathered_kernel, units, lines),
        out_shape=(
            jax.ShapeDtypeStruct((slots, 2 * width), F32),
            jax.ShapeDtypeStruct((slots, 2 * width), BF16),
        ),
        in_specs=[pl.BlockSpec(memory_space=pltpu.VMEM)] + [pl.BlockSpec(memory_space=pl.ANY)] * count,
        out_specs=(pl.BlockSpec(memory_space=pltpu.VMEM), pl.BlockSpec(memory_space=pltpu.VMEM)),
        scratch_shapes=[
            pltpu.VMEM((count * units, width), BF16),
            pltpu.VMEM((count * units, width), BF16),
            pltpu.VMEM((experts * lines, 128), F32),
            pltpu.SemaphoreType.DMA((count, 2)),
        ],
        compiler_params=pltpu.CompilerParams(vmem_limit_bytes=VMEM_LIMIT + (4 << 20)),
        cost_estimate=pl.CostEstimate(
            flops=8 * slots * count * units * width,
            bytes_accessed=4 * count * units * width,
            transcendentals=0,
        ),
        name="gathered",
    )(arrived, *map(outside, pieces))


def last_kernel(units, rows_ref, acc_ref, up_ref, down_ref, out_ref, wide):
    width = up_ref.shape[1]
    experts, lines, _ = out_ref.shape
    capacity = rows_ref.shape[0] // experts
    blocks = lines // capacity
    up, down = up_ref[:units, :], down_ref[:units, :]
    tok, cot = rows_ref[:, :width], rows_ref[:, width:]
    hidden, act_grad = activations(matmul_nt(tok, up), matmul_nt(cot, down))
    for part, (acts, weights) in enumerate(((hidden, down), (act_grad, up))):
        sums = acc_ref[:, part * width : (part + 1) * width] + matmul(acts, weights)
        for b in range(width // 128):
            line = part * (width // 128) + b
            for r in range(capacity):
                wide[pl.ds(r * blocks + line, experts, stride=lines), :] = sums[
                    r * experts : (r + 1) * experts, b * 128 : (b + 1) * 128
                ]
    for e in range(experts):
        out_ref[e] = wide[e * lines : (e + 1) * lines, :].astype(BF16)


def last(rows, acc, up_half, down_half, units, experts):
    lines = rows.shape[0] * rows.shape[1] // (experts * 128)
    return pl.pallas_call(
        functools.partial(last_kernel, units),
        out_shape=jax.ShapeDtypeStruct((experts, lines, 128), BF16),
        scratch_shapes=[pltpu.VMEM((experts * lines, 128), F32)],
        compiler_params=pltpu.CompilerParams(vmem_limit_bytes=VMEM_LIMIT),
        name="last",
    )(rows, acc, up_half, down_half)


def hot_kernel(units, hot_rows, where_ref, pieces_ref, *refs):
    blocks, (send_ref, keep_ref, tok, cot, weights, sems) = refs[:-6], refs[-6:]
    ring = len(blocks)
    width = tok.shape[1]
    here = where_ref[0]
    copies = []
    for i, block in enumerate(blocks):
        place = pl.multiple_of((here ^ lax.rem(here + i, ring)) * HOT_PAD, HOT_PAD)
        pair = block if isinstance(block, tuple) else (block, block)
        offset = 0 if isinstance(block, tuple) else units + HOT_PAD
        for j, whole in enumerate((tok, cot)):
            copy = pltpu.make_async_copy(
                pair[j].at[pl.ds(j * offset + units, HOT_PAD)], whole.at[pl.ds(place, HOT_PAD)], sems.at[i, j]
            )
            copy.start()
            copies.append(copy)
    columns = width // 128
    tall = pieces_ref.shape[1]
    for k in range(pieces_ref.shape[0]):
        i, j = k // columns, k % columns
        weights[i * tall : (i + 1) * tall, j * 128 : (j + 1) * 128] = pieces_ref[k]
    for copy in copies:
        copy.wait()
    up, down = weights[:units, :], weights[units:, :]
    hidden, act_grad = activations(matmul_nt(tok[...], up), matmul_nt(cot[...], down))
    packed, lanes = send_ref.shape
    blocks_of = 2 * width // lanes
    row = lax.broadcasted_iota(I32, (packed, ring * HOT_PAD), 0)
    column = lax.broadcasted_iota(I32, (packed, ring * HOT_PAD), 1)
    group = row // (blocks_of * hot_rows)
    block_of = row // hot_rows % blocks_of
    within = ((group % 2) * 4 + (group // 2) * 2) * HOT_PAD + row % hot_rows
    for odd, out_ref in ((1, send_ref), (0, keep_ref)):
        total = jnp.zeros((packed, lanes), F32)
        for b in range(blocks_of):
            chosen = ((column == within + odd * HOT_PAD) & (block_of == b)).astype(F32).astype(BF16)
            acts, matrix = (hidden, down) if b * lanes < width else (act_grad, up)
            lo = b * lanes % width
            total = total + matmul(matmul(chosen, acts).astype(BF16), matrix[:, lo : lo + lanes])
        out_ref[...] = total.astype(BF16)


def hot_partials(here, pieces, blocks, units, hot_rows, after):
    ring = len(blocks)
    flat, spans = [], []
    for block in blocks:
        spans.append(len(block) if isinstance(block, tuple) else 0)
        flat += list(block) if isinstance(block, tuple) else [block]
    width = flat[0].shape[1]

    def kernel(where_ref, pieces_ref, after_ref, *refs):
        refs, grouped = list(refs), []
        for span in spans:
            grouped.append(tuple(refs.pop(0) for _ in range(span)) if span else refs.pop(0))
        hot_kernel(units, hot_rows, where_ref, pieces_ref, *grouped, *refs)

    inside = pl.BlockSpec(memory_space=pltpu.VMEM)
    packed = jax.ShapeDtypeStruct((ring // 2 * hot_rows * (2 * width // LANES), LANES), BF16)
    return pl.pallas_call(
        kernel,
        out_shape=(packed, packed),
        in_specs=[pl.BlockSpec(memory_space=pltpu.SMEM), inside]
        + [pl.BlockSpec(memory_space=pl.ANY)] * (1 + len(flat)),
        out_specs=(inside, inside),
        scratch_shapes=[
            pltpu.VMEM((ring * HOT_PAD, width), BF16),
            pltpu.VMEM((ring * HOT_PAD, width), BF16),
            pltpu.VMEM((2 * units, width), BF16),
            pltpu.SemaphoreType.DMA((ring, 2)),
        ],
        compiler_params=pltpu.CompilerParams(vmem_limit_bytes=VMEM_LIMIT),
        name="hot",
    )(here, pieces, after, *map(outside, flat))


def thirds(x):
    first = x.astype(BF16)
    rest = x - first.astype(F32)
    second = rest.astype(BF16)
    third = (rest - second.astype(F32)).astype(BF16)
    return first, second, third


def cold_kernel(capacity, ids_ref, gate_ref, cot_ref, cold_ref, sum_ref, dots_ref, wide, rows):
    ids, gates, cot = ids_ref[...], gate_ref[...], cot_ref[...]
    top_count = ids.shape[0]
    experts, lines, _ = cold_ref.shape
    blocks = lines // capacity
    width = cot.shape[1]
    for e in range(experts):
        wide[e * lines : (e + 1) * lines, :] = cold_ref[e].astype(F32)
    for r in range(capacity):
        for b in range(blocks):
            line = wide[pl.ds(r * blocks + b, experts, stride=lines), :]
            rows[r * experts : (r + 1) * experts, b * 128 : (b + 1) * 128] = line.astype(BF16)
    cold, _, expert, _, _ = slot_maps(ids, experts * capacity, capacity, slot_major=True)
    per_slot = jnp.zeros(cold.shape, F32)
    for k in range(top_count):
        per_slot = per_slot + jnp.where(ids[k : k + 1, :] == expert, gates[k : k + 1, :], 0.0)
    scale = thirds(jnp.where(cold > 0, per_slot, 0.0))
    for lo in (0, width):
        part = rows[:, lo : lo + width]
        sum_ref[:, lo : lo + width] = matmul_tn(scale[0], part) + matmul_tn(scale[1], part) + matmul_tn(scale[2], part)
    dots = jnp.where(cold > 0, matmul_nt(rows[:, :width], cot), 0.0)
    for k in range(top_count):
        dots_ref[k : k + 1, :] = jnp.sum(jnp.where(ids[k : k + 1, :] == expert, dots, 0.0), 0, keepdims=True)


def cold_combine(ids, gates, cotangent, results, capacity):
    tok_rows, width = cotangent.shape
    experts, lines, _ = results.shape
    return pl.pallas_call(
        functools.partial(cold_kernel, capacity),
        out_shape=(
            jax.ShapeDtypeStruct((tok_rows, 2 * width), F32),
            jax.ShapeDtypeStruct(gates.shape, F32),
        ),
        scratch_shapes=[
            pltpu.VMEM((experts * lines, 128), F32),
            pltpu.VMEM((experts * capacity, 2 * width), BF16),
        ],
        compiler_params=pltpu.CompilerParams(vmem_limit_bytes=VMEM_LIMIT),
        cost_estimate=pl.CostEstimate(flops=1 << 36, bytes_accessed=1 << 26, transcendentals=0),
        name="cold_combine",
    )(ids, gates, cotangent, results)


def final_kernel(
    capacity, slots, ids_ref, gate_ref, cot_ref, sum_ref, dots_ref, kept_ref, *refs
):
    sent, (mix_ref, grad_ref, gate_grad_ref) = refs[:-3], refs[-3:]
    ids, gates, cot = ids_ref[...], gate_ref[...], cot_ref[...]
    top_count, tok_rows = ids.shape
    width = cot.shape[1]
    lanes = kept_ref.shape[1]
    hot_rows = kept_ref.shape[0] * lanes // (2 * width)
    _, hot, _, _, hottest = slot_maps(ids, slots, capacity)
    hottest = hottest.astype(I32)
    gate = jnp.zeros((1, tok_rows), F32)
    for k in range(top_count):
        gate = gate + jnp.where(ids[k : k + 1, :] == hottest, gates[k : k + 1, :], 0.0)
    hot = hot[:hot_rows]
    scale = thirds(jnp.where(hot > 0, gate, 0.0))
    result = kept_ref[...]
    for ref in sent:
        result = result + ref[...].astype(F32)
    dots = jnp.zeros(hot.shape, F32)
    for b in range(2 * width // lanes):
        rows = result[b * hot_rows : (b + 1) * hot_rows].astype(BF16)
        lo, at = b * lanes, b * lanes % width
        total = matmul_tn(scale[0], rows) + matmul_tn(scale[1], rows) + matmul_tn(scale[2], rows)
        out_ref = mix_ref if lo < width else grad_ref
        out_ref[:, at : at + lanes] = (sum_ref[:, lo : lo + lanes] + total).astype(BF16)
        if lo < width:
            dots = dots + matmul_nt(rows, cot[:, at : at + lanes])
    dot = jnp.sum(jnp.where(hot > 0, dots, 0.0), 0, keepdims=True)
    gate_grad_ref[...] = dots_ref[...] + jnp.where(ids == hottest, dot, 0.0)


def final_combine(ids, gates, cotangent, sums, dots, kept, sent, slots, capacity):
    return pl.pallas_call(
        functools.partial(final_kernel, capacity, slots),
        out_shape=(
            jax.ShapeDtypeStruct(cotangent.shape, BF16),
            jax.ShapeDtypeStruct(cotangent.shape, BF16),
            jax.ShapeDtypeStruct(gates.shape, F32),
        ),
        compiler_params=pltpu.CompilerParams(vmem_limit_bytes=VMEM_LIMIT),
        name="final_combine",
    )(ids, gates, cotangent, sums, dots, kept, *sent)


TICK = pl.CostEstimate(flops=1 << 35, bytes_accessed=1 << 25, transcendentals=0)


def tick_kernel(token_ref, *refs):
    refs[-1][0, 0] = token_ref[0, 0]


def tick(token, *after):
    scalar = pl.BlockSpec(memory_space=pltpu.SMEM)
    return pl.pallas_call(
        tick_kernel,
        out_shape=jax.ShapeDtypeStruct(token.shape, token.dtype),
        in_specs=[scalar] + [pl.BlockSpec(memory_space=pl.ANY)] * len(after),
        out_specs=scalar,
        compiler_params=pltpu.CompilerParams(vmem_limit_bytes=1 << 20),
        cost_estimate=pl.CostEstimate(flops=22 << 30, bytes_accessed=1 << 10, transcendentals=0),
        name="tick",
    )(token, *after)


def split_kernel(right_ref, left_ref, right_out, left_out, top_ref, bottom_ref, sems):
    half = top_ref.shape[0]
    copies = [
        pltpu.make_async_copy(right_ref.at[pl.ds(0, half)], top_ref, sems.at[0]),
        pltpu.make_async_copy(left_ref.at[pl.ds(half, half)], bottom_ref, sems.at[1]),
    ]
    for copy in copies:
        copy.start()
    for copy in copies:
        copy.wait()


def split(right, left):
    anywhere, inside = pl.BlockSpec(memory_space=pl.ANY), pl.BlockSpec(memory_space=pltpu.VMEM)
    whole = jax.ShapeDtypeStruct(right.shape, right.dtype)
    part = jax.ShapeDtypeStruct((right.shape[0] // 2, right.shape[1]), right.dtype)
    return pl.pallas_call(
        split_kernel,
        out_shape=(whole, whole, part, part),
        in_specs=[anywhere] * 2,
        out_specs=(anywhere, anywhere, inside, inside),
        input_output_aliases={0: 0, 1: 1},
        scratch_shapes=[pltpu.SemaphoreType.DMA((2,))],
        compiler_params=pltpu.CompilerParams(vmem_limit_bytes=1 << 22),
        cost_estimate=TICK,
        name="split",
    )(right, left)


def shift(x, by):
    ring = lax.axis_size("dp")
    return lax.ppermute(x, "dp", [(i, (i + by) % ring) for i in range(ring)])


def swap(x, bit):
    ring = lax.axis_size("dp")
    pairs = [[i, i ^ bit] for i in range(ring) if not i & bit]
    both = lax.all_gather(x, "dp", axis=0, axis_index_groups=pairs, tiled=False)
    return jnp.where(lax.axis_index("dp") & bit == 0, both[1], both[0])


def send_on(x, bits):
    ring = lax.axis_size("dp")
    return lax.ppermute(x, "dp", [(i, i ^ bits) for i in range(ring)])


def shards(tokens, cotangent, gate_probs, expert_ids, up_weight, down_weight):
    tok_rows, width = tokens.shape
    top_count = expert_ids.shape[1]
    experts = lax.axis_size("expert")
    hot_rows = 9 * tok_rows // 16
    capacity = (tok_rows * top_count - hot_rows + experts - 2) // (experts - 1)
    slots = experts * capacity
    up, down = up_weight[0], down_weight[0]
    units = up.shape[0]
    ids, gates = expert_ids.T, gate_probs.T

    outgoing, own, hottest = route(ids, tokens, cotangent, up, down, slots, capacity)
    half = own.shape[0] // 2
    right, left = [own], [own]
    for step in range(3):
        r, l = shift(right[-1], 1), shift(left[-1], -1)
        if step == 1:
            token = tick(hottest, r, l)
        if step == 2:
            r, l, top, bottom = split(r, l)
        right.append(r)
        left.append(l)
    far_up, far_down = shift(top, 1), shift(bottom, -1)

    lines = capacity * 2 * width // 128
    outgoing = assemble(outgoing.reshape(experts, lines, 128), up, down)
    arrived = lax.all_to_all(outgoing, "expert", 0, 0, tiled=True)
    hot_pieces = lax.all_to_all(repeat(token, arrived, lines), "expert", 0, 0, tiled=True)

    acc, rows = gathered(arrived, [own] + right[1:] + left[1:], units, slots)
    results = last(rows, acc, far_up, far_down, units, experts)
    came_back = lax.all_to_all(results, "expert", 0, 0, tiled=True)

    blocks = left + [(far_up, far_down)] + right[:0:-1]
    here = lax.axis_index("dp").astype(I32).reshape(1)
    send, keep = hot_partials(here, hot_pieces, blocks, units, hot_rows, results)
    both = keep.astype(F32) + swap(send, 1).astype(F32)
    dense = both.shape[0] // 4
    kept = both[:dense]
    sent = [send_on(both[i * dense : (i + 1) * dense].astype(BF16), place) for i, place in ((1, 4), (2, 2), (3, 6))]
    sums, dots = cold_combine(ids, gates, cotangent, came_back, capacity)
    mixture, input_grad, gate_grad = final_combine(
        ids, gates, cotangent, sums, dots, kept, sent, slots, capacity
    )
    return mixture, input_grad, gate_grad.T


def solution(mesh):
    rows = P(("dp", "expert"), None)
    weights = P("expert", "dp", None)
    return jax.shard_map(
        shards,
        mesh=mesh,
        in_specs=(rows, rows, rows, rows, weights, weights),
        out_specs=(rows, rows, rows),
        check_vma=False,
    )
```
